32 devices in a mesh: dp: 8 (over z, x), blk: 4 (over y, core).
Axes of the slice: x: 2, y: 2, z: 4, core: 2. Of those that a mesh axis runs over, the one named last changes fastest.
Arguments:
- tokens: bfloat16 [8, 1024, 768], P('dp', 'blk'), may hold values from -6 to 6
- segments: int32 [8, 1024], P('dp', 'blk'), may hold values from 0 to 2, as said below
- positions: int32 [8, 1024], P('dp', 'blk'), may hold values from 0 to 1008, as said below
- cotangent: bfloat16 [8, 1024, 768], P('dp', 'blk'), may hold values from -6 to 6
- attn_gain: bfloat16 [768], P(('dp', 'blk')), may hold values from 0.5 to 1.5
- w_query: bfloat16 [768, 768], P(('dp', 'blk')), may hold values from -0.3125 to 0.3125
- w_key: bfloat16 [768, 768], P(('dp', 'blk')), may hold values from -0.3125 to 0.3125
- w_value: bfloat16 [768, 768], P(('dp', 'blk')), may hold values from -0.21875 to 0.21875
- w_out: bfloat16 [768, 768], P(('dp', 'blk')), may hold values from -1.75 to 1.75
- mlp_gain: bfloat16 [768], P(('dp', 'blk')), may hold values from 0.5 to 1.5
- w_gate: bfloat16 [768, 2048], P(('dp', 'blk')), may hold values from -0.21875 to 0.21875
- w_up: bfloat16 [768, 2048], P(('dp', 'blk')), may hold values from -0.21875 to 0.21875
- w_down: bfloat16 [2048, 768], P(('dp', 'blk')), may hold values from -0.1875 to 0.1875
Outputs:
- output: bfloat16 [8, 1024, 768], P('dp', 'blk')
- grad_tokens: bfloat16 [8, 1024, 768], P('dp', 'blk')
- grad_attn_gain: float32 [768], P(('dp', 'blk'))
- grad_w_query: float32 [768, 768], P(('dp', 'blk'))
- grad_w_key: float32 [768, 768], P(('dp', 'blk'))
- grad_w_value: float32 [768, 768], P(('dp', 'blk'))
- grad_w_out: float32 [768, 768], P(('dp', 'blk'))
- grad_mlp_gain: float32 [768], P(('dp', 'blk'))
- grad_w_gate: float32 [768, 2048], P(('dp', 'blk'))
- grad_w_up: float32 [768, 2048], P(('dp', 'blk'))
- grad_w_down: float32 [2048, 768], P(('dp', 'blk'))
The draws below stay inside these ranges and needn't reach their ends.
Inputs may be any that keep to these rules, and one draw needn't show every extreme that they name: `segments`: each pack holds three documents in order: the first, of 1 + 24 h slots, ends within the first 256 slots; the second, of 1 + 24 h slots, ends within the last 256 slots; the third fills the rest. `positions`: the index of each slot within its document, as given by segments.
All inputs are finite; a program needn't handle non-finite values.
Results may differ from the reference program's by a relative error of at most 0.03.
Values may be sent and summed in bfloat16 or wider, within the bound.
No kernel may reach another device: no remote copies, remote signals or barrier semaphores. Data moves between devices by JAX's collectives and lax.ppermute only.
A program may use at most 192 MiB of HBM per device.

```python
import math
import jax
import jax.numpy as jnp
from jax import lax

D = 768
HEADS = 12
HEAD_DIM = 64
FF = 2048
TOK_DEV = 256
CROP = 24
SEQ_LEN = 1024
SEQS = 8
N_BLK = 4


def pack_layout(key):
    head_key, long_key = jax.random.split(key)
    pack_index = jnp.arange(SEQS, dtype=jnp.int32)
    head_rows = jax.random.randint(head_key, (SEQS,), 0, (TOK_DEV - 2) // CROP + 1)
    head_rows = jnp.where(pack_index == 0, 0, head_rows)
    head_length = 1 + CROP * head_rows
    remaining = SEQ_LEN - head_length
    longest = 1 + CROP * ((remaining - 2) // CROP)
    needed_length = (N_BLK - 1) * TOK_DEV + 1 - head_length
    spare_rows = (longest - needed_length) // CROP
    cut_rows = jax.random.randint(long_key, (SEQS,), 0, spare_rows + 1)
    cut_rows = jnp.where(pack_index == 0, 0, cut_rows)
    long_length = longest - CROP * cut_rows
    slot_index = jnp.arange(SEQ_LEN, dtype=jnp.int32)[None, :]
    first_end = head_length[:, None]
    second_end = (head_length + long_length)[:, None]
    seg_numbers = (slot_index >= first_end).astype(jnp.int32) + (slot_index >= second_end).astype(jnp.int32)
    doc_start = jnp.where(slot_index >= second_end, second_end, jnp.where(slot_index >= first_end, first_end, 0))
    return (seg_numbers, (slot_index - doc_start).astype(jnp.int32))


def draw_segments(key, part):
    layout = pack_layout(key)
    return layout[0]


def draw_positions(key, part):
    layout = pack_layout(key)
    return layout[1]


def block_levels(own_key, dims, pieces, smallest, high):
    factor_of, own = 1.0, jax.random.fold_in(own_key, 6)
    for position, parts in pieces:
        draws = jnp.exp(jax.random.uniform(jax.random.fold_in(own, position), (parts,), jnp.float32, smallest / len(pieces), high / len(pieces)))
        factor_of = factor_of * jnp.repeat(draws, dims[position] // parts).reshape([-1 if axis == position else 1 for axis in range(len(dims))])
    return factor_of


def normal_values(key, shape, width, bound, pieces=(), held_as=jnp.bfloat16):
    entries = width * jax.random.normal(key, shape, jnp.float32)
    if pieces:
        entries = entries * block_levels(key, shape, pieces, -0.22, 0.18)
    return jnp.clip(entries, -bound, bound).astype(held_as)


def setup_inputs(seed: int = 0) -> dict:
    streams_of = jax.random.split(jax.random.key(seed), 14)
    tokens = normal_values(streams_of[0], (SEQS, SEQ_LEN, D), 1.0, 6.0, ((0, 8), (1, 4)))
    segments = draw_segments(jax.random.fold_in(streams_of[13], 71), 0)
    positions = draw_positions(jax.random.fold_in(streams_of[13], 71), 0)
    cotangent = normal_values(streams_of[3], (SEQS, SEQ_LEN, D), 1.0, 6.0, ((0, 8), (1, 4)))
    attn_gain = jnp.clip(1.0 + 0.1 * jax.random.normal(streams_of[4], (D,), jnp.float32), 0.5, 1.5).astype(jnp.bfloat16)
    w_query = normal_values(streams_of[5], (D, D), (D // 2) ** -0.5, 0.3125, ((0, 32),))
    w_key = normal_values(streams_of[6], (D, D), (D // 2) ** -0.5, 0.3125, ((0, 32),))
    w_value = normal_values(streams_of[7], (D, D), D ** -0.5, 0.21875, ((0, 32),))
    w_out = normal_values(streams_of[8], (D, D), (D // 64) ** -0.5, 1.75, ((0, 32),))
    mlp_gain = jnp.clip(1.0 + 0.1 * jax.random.normal(streams_of[9], (D,), jnp.float32), 0.5, 1.5).astype(jnp.bfloat16)
    w_gate = normal_values(streams_of[10], (D, FF), D ** -0.5, 0.21875, ((0, 32),))
    w_up = normal_values(streams_of[11], (D, FF), D ** -0.5, 0.21875, ((0, 32),))
    w_down = normal_values(streams_of[12], (FF, D), (FF // 2) ** -0.5, 0.1875, ((0, 32),))
    return {"tokens": tokens, "segments": segments, "positions": positions, "cotangent": cotangent, "attn_gain": attn_gain, "w_query": w_query, "w_key": w_key, "w_value": w_value, "w_out": w_out, "mlp_gain": mlp_gain, "w_gate": w_gate, "w_up": w_up, "w_down": w_down}


EPS = 1e-05
SCALE = 0.125
NEG = -1e+30
HIGH = lax.Precision.HIGHEST

@jax.custom_vjp
def low(v):
    return lax.optimization_barrier(v.astype(jnp.bfloat16)).astype(jnp.float32)

@jax.custom_vjp
def low_back(v):
    return v

def low_keep(v):
    return (low(v), None)

def low_pass(kept, grad):
    return (grad,)

def back_keep(v):
    return (v, None)

def back_low(kept, grad):
    return (low(grad),)
low.defvjp(low_keep, low_pass)
low_back.defvjp(back_keep, back_low)

def product(left_matrix, right_matrix):
    return jnp.dot(left_matrix, right_matrix, precision=HIGH, preferred_element_type=jnp.float32)

def rms_norm(values, gain):
    return values * lax.rsqrt(lax.optimization_barrier(jnp.mean(values * values, axis=-1, keepdims=True)) + EPS) * gain

def rope_tables(slot_positions, half_dim):
    inverse = jnp.exp(-math.log(10000.0) * jnp.arange(half_dim, dtype=jnp.float32) / half_dim)
    angles = slot_positions.astype(jnp.float32)[:, None] * inverse[None, :]
    return (jnp.cos(angles)[:, None, :], jnp.sin(angles)[:, None, :])

def rotate(tensor, cosine_table, sine_table):
    half_dim = tensor.shape[-1] // 2
    leading = tensor[..., :half_dim]
    trailing = tensor[..., half_dim:]
    return jnp.concatenate([leading * cosine_table - trailing * sine_table, trailing * cosine_table + leading * sine_table], axis=-1)

def block_layer(x_float, gain_one, full_query, full_key, full_value, full_out, gain_two, full_gate, full_up, full_down, pack_segments, cosine_table, sine_table):
    pack_length = x_float.shape[0]
    normed = low(rms_norm(x_float, gain_one))
    query_rot = low(rotate(low_back(product(normed, full_query)).reshape(pack_length, HEADS, HEAD_DIM), cosine_table, sine_table))
    key_rot = low(rotate(low_back(product(normed, full_key)).reshape(pack_length, HEADS, HEAD_DIM), cosine_table, sine_table))
    value_heads = low(low_back(product(normed, full_value))).reshape(pack_length, HEADS, HEAD_DIM)
    block_rows = math.gcd(pack_length, 512)
    slot_index = jnp.arange(pack_length, dtype=jnp.int32)

    def attend(block_items):
        query_block, query_index, query_segments = block_items
        scores = low_back(SCALE * jnp.einsum('qhd,khd->hqk', query_block, key_rot, precision=HIGH))
        allowed = (query_segments[:, None] == pack_segments[None, :]) & (slot_index[None, :] <= query_index[:, None])
        scores = jnp.where(allowed[None], scores, NEG)
        probability = jax.nn.softmax(scores, axis=-1)
        return jnp.einsum('hqk,khd->qhd', low(probability), value_heads, precision=HIGH)
    mixed = lax.map(jax.checkpoint(attend), (query_rot.reshape(pack_length // block_rows, block_rows, HEADS, HEAD_DIM), slot_index.reshape(-1, block_rows), pack_segments.reshape(-1, block_rows)))
    attn = low(low_back(mixed.reshape(pack_length, HEADS * HEAD_DIM)))
    resid = x_float + low_back(product(attn, full_out))
    normed_two = low(rms_norm(resid, gain_two))
    gate = low_back(product(normed_two, full_gate))
    up_values = low_back(product(normed_two, full_up))
    hidden = low(jax.nn.silu(gate) * up_values)
    return resid + low_back(product(hidden, full_down))

def reference(tokens, segments, positions, cotangent, attn_gain, w_query, w_key, w_value, w_out, mlp_gain, w_gate, w_up, w_down):
    params = tuple((weight.astype(jnp.float32) for weight in (attn_gain, w_query, w_key, w_value, w_out, mlp_gain, w_gate, w_up, w_down)))

    def one_pack(totals, pack_items):
        pack_tokens, pack_segments, pack_positions, pack_cotangent = pack_items
        cosine_table, sine_table = rope_tables(pack_positions, HEAD_DIM // 2)

        def forward(x_float, *weights):
            return block_layer(x_float, *weights, pack_segments, cosine_table, sine_table)
        result, pullback = jax.vjp(forward, pack_tokens.astype(jnp.float32), *params)
        gradients = pullback(pack_cotangent.astype(jnp.float32))
        totals = tuple((total + gradient for total, gradient in zip(totals, gradients[1:])))
        return (totals, (result.astype(jnp.bfloat16), gradients[0].astype(jnp.bfloat16)))
    zero_grads = tuple((jnp.zeros(weight.shape, jnp.float32) for weight in params))
    totals, (results, input_grads) = lax.scan(one_pack, zero_grads, (tokens, segments, positions, cotangent))
    return (results, input_grads, totals[0], totals[1], totals[2], totals[3], totals[4], totals[5], totals[6], totals[7], totals[8])
```

```python
import math

import jax
import jax.numpy as jnp
from jax import lax
from jax.experimental import pallas as pl
from jax.experimental.pallas import tpu as pltpu
from jax.sharding import PartitionSpec as P

HEADS = 12
HEAD_DIM = 64


EPS = 1e-05
SCALE = 0.125
NEG = -1e30


def rope_tables(slot_positions, half_dim):
    inverse = jnp.exp(-math.log(10000.0) * jnp.arange(half_dim, dtype=jnp.float32) / half_dim)
    angles = slot_positions.astype(jnp.float32)[:, None] * inverse[None, :]
    return (jnp.cos(angles)[:, None, :], jnp.sin(angles)[:, None, :])


def rotate(tensor, cosine_table, sine_table):
    half_dim = tensor.shape[-1] // 2
    leading = tensor[..., :half_dim]
    trailing = tensor[..., half_dim:]
    return jnp.concatenate(
        [
            leading * cosine_table - trailing * sine_table,
            trailing * cosine_table + leading * sine_table,
        ],
        axis=-1,
    )


def matmul(left_matrix, right_matrix):
    return jnp.dot(left_matrix, right_matrix, preferred_element_type=jnp.float32)


def left_product(left_matrix, right_matrix):
    return lax.dot_general(
        left_matrix, right_matrix, (((0,), (0,)), ((), ())), preferred_element_type=jnp.float32
    )


def right_product(left_matrix, right_matrix):
    return lax.dot_general(
        left_matrix, right_matrix, (((1,), (1,)), ((), ())), preferred_element_type=jnp.float32
    )


def norm_back(grad_normed, values, inverse, gain):
    unit_normed = values * inverse
    scaled = grad_normed * gain
    grad_gain = jnp.sum(grad_normed * unit_normed, axis=0)
    grad_values = inverse * (
        scaled - unit_normed * jnp.mean(scaled * unit_normed, axis=-1, keepdims=True)
    )
    return (grad_values, grad_gain)


def score_mask(query_segments, query_index, key_segments, key_index):
    return (query_segments[:, None] == key_segments[None, :]) & (
        key_index[None, :] <= query_index[:, None]
    )


def block_grads(query_block, grad_block, lse_rows, delta_rows, allowed, key_block, value_block):
    scores = (
        jnp.einsum("qhd,khd->hqk", query_block, key_block, preferred_element_type=jnp.float32)
        * SCALE
    )
    probability = jnp.exp(jnp.where(allowed[None], scores - lse_rows.T[:, :, None], NEG))
    grad_value = jnp.einsum(
        "hqk,qhd->khd",
        probability.astype(jnp.bfloat16),
        grad_block,
        preferred_element_type=jnp.float32,
    )
    grad_probs = jnp.einsum(
        "qhd,khd->hqk", grad_block, value_block, preferred_element_type=jnp.float32
    )
    grad_scores = (probability * (grad_probs - delta_rows.T[:, :, None])).astype(jnp.bfloat16)
    grad_query = (
        jnp.einsum("hqk,khd->qhd", grad_scores, key_block, preferred_element_type=jnp.float32)
        * SCALE
    )
    grad_key = (
        jnp.einsum("hqk,qhd->khd", grad_scores, query_block, preferred_element_type=jnp.float32)
        * SCALE
    )
    return (grad_query, grad_key, grad_value)


def shards(
    tokens,
    segments,
    positions,
    cotangent,
    attn_gain,
    w_query,
    w_key,
    w_value,
    w_out,
    mlp_gain,
    w_gate,
    w_up,
    w_down,
):
    local_rows = tokens.shape[1]
    model_width = tokens.shape[2]
    blocks = lax.axis_size("blk")
    own_start = lax.axis_index("blk") * local_rows
    query_index = own_start + jnp.arange(local_rows, dtype=jnp.int32)
    own_segments = segments[0]
    cosine_table, sine_table = rope_tables(positions[0], HEAD_DIM // 2)
    x_float = tokens[0].astype(jnp.float32)
    gathered = (
        lax.all_gather(attn_gain, ("dp", "blk"), axis=0, tiled=True),
        lax.all_gather(w_query, ("dp", "blk"), axis=0, tiled=True),
        lax.all_gather(w_key, ("dp", "blk"), axis=0, tiled=True),
        lax.all_gather(w_value, ("dp", "blk"), axis=0, tiled=True),
        lax.all_gather(w_out, ("dp", "blk"), axis=0, tiled=True),
        lax.all_gather(mlp_gain, ("dp", "blk"), axis=0, tiled=True),
        lax.all_gather(w_gate, ("dp", "blk"), axis=0, tiled=True),
        lax.all_gather(w_up, ("dp", "blk"), axis=0, tiled=True),
        lax.all_gather(w_down, ("dp", "blk"), axis=0, tiled=True),
    )
    gain_one = gathered[0].astype(jnp.float32)
    gain_two = gathered[5].astype(jnp.float32)
    inverse_one = lax.rsqrt(jnp.mean(x_float * x_float, axis=-1, keepdims=True) + EPS)
    normed = (x_float * inverse_one * gain_one).astype(jnp.bfloat16)
    query_rot = rotate(
        matmul(normed, gathered[1]).reshape(local_rows, HEADS, HEAD_DIM), cosine_table, sine_table
    ).astype(jnp.bfloat16)
    key_rot = rotate(
        matmul(normed, gathered[2]).reshape(local_rows, HEADS, HEAD_DIM), cosine_table, sine_table
    ).astype(jnp.bfloat16)
    value_heads = (
        matmul(normed, gathered[3]).astype(jnp.bfloat16).reshape(local_rows, HEADS, HEAD_DIM)
    )
    key_flat = key_rot.reshape(local_rows, model_width)
    value_flat = value_heads.reshape(local_rows, model_width)
    start_state = (
        jnp.full((HEADS, local_rows), NEG, jnp.float32),
        jnp.zeros((HEADS, local_rows), jnp.float32),
        jnp.zeros((local_rows, HEADS, HEAD_DIM), jnp.float32),
    )
    key_piece = lax.all_gather(key_flat, "blk", axis=0, tiled=True)
    value_piece = lax.all_gather(value_flat, "blk", axis=0, tiled=True)
    seg_piece = lax.all_gather(own_segments, "blk", axis=0, tiled=True)
    piece_rows = key_piece.shape[0]
    needed = (jnp.int32(0) <= own_start + local_rows - 1) & (
        seg_piece[piece_rows - 1] >= own_segments[0]
    )

    def attend_sweep(current):

        def attend_visit(number, partial_value):
            running_max, running_sum, weighted = partial_value
            offset = number * local_rows
            key_block = lax.dynamic_slice_in_dim(key_piece, offset, local_rows, 0).reshape(
                local_rows, HEADS, HEAD_DIM
            )
            value_block = lax.dynamic_slice_in_dim(value_piece, offset, local_rows, 0).reshape(
                local_rows, HEADS, HEAD_DIM
            )
            seg_block = lax.dynamic_slice_in_dim(seg_piece, offset, local_rows, 0)
            key_index = offset + jnp.arange(local_rows, dtype=jnp.int32)
            allowed = score_mask(own_segments, query_index, seg_block, key_index)
            scores = (
                jnp.einsum("qhd,khd->hqk", query_rot, key_block, preferred_element_type=jnp.float32)
                * SCALE
            )
            scores = jnp.where(allowed[None], scores, NEG)
            new_max = jnp.maximum(running_max, jnp.max(scores, axis=-1))
            probability = jnp.where(allowed[None], jnp.exp(scores - new_max[:, :, None]), 0.0)
            factor = jnp.exp(running_max - new_max)
            running_sum = running_sum * factor + jnp.sum(probability, axis=-1)
            weighted = weighted * factor.T[:, :, None] + jnp.einsum(
                "hqk,khd->qhd",
                probability.astype(jnp.bfloat16),
                value_block,
                preferred_element_type=jnp.float32,
            )
            return (new_max, running_sum, weighted)

        return lax.fori_loop(0, piece_rows // local_rows, attend_visit, current)

    final_max, final_sum, final_weighted = lax.cond(
        needed, attend_sweep, lambda unchanged: unchanged, start_state
    )
    attn_heads = (final_weighted / final_sum.T[:, :, None]).astype(jnp.bfloat16)
    lse_rows = (final_max + jnp.log(final_sum)).T
    attn_flat = attn_heads.reshape(local_rows, model_width)
    resid = x_float + matmul(attn_flat, gathered[4])
    inverse_two = lax.rsqrt(jnp.mean(resid * resid, axis=-1, keepdims=True) + EPS)
    normed_two = (resid * inverse_two * gain_two).astype(jnp.bfloat16)
    gate = matmul(normed_two, gathered[6])
    up_values = matmul(normed_two, gathered[7])
    hidden = (jax.nn.silu(gate) * up_values).astype(jnp.bfloat16)
    output = (resid + matmul(hidden, gathered[8])).astype(jnp.bfloat16)
    later = (
        lax.all_gather(attn_gain, ("dp", "blk"), axis=0, tiled=True),
        lax.all_gather(w_query, ("dp", "blk"), axis=0, tiled=True),
        lax.all_gather(w_key, ("dp", "blk"), axis=0, tiled=True),
        lax.all_gather(w_value, ("dp", "blk"), axis=0, tiled=True),
        lax.all_gather(w_out, ("dp", "blk"), axis=0, tiled=True),
        lax.all_gather(mlp_gain, ("dp", "blk"), axis=0, tiled=True),
        lax.all_gather(w_gate, ("dp", "blk"), axis=0, tiled=True),
        lax.all_gather(w_up, ("dp", "blk"), axis=0, tiled=True),
        lax.all_gather(w_down, ("dp", "blk"), axis=0, tiled=True),
    )
    grad_res = cotangent[0].astype(jnp.float32)
    grad_mlp = grad_res.astype(jnp.bfloat16)
    grad_down = left_product(hidden, grad_mlp)
    grad_hidden = right_product(grad_mlp, later[8])
    sigmoid_gate = jax.nn.sigmoid(gate)
    grad_gate_low = (
        grad_hidden * up_values * sigmoid_gate * (1.0 + gate * (1.0 - sigmoid_gate))
    ).astype(jnp.bfloat16)
    grad_up_low = (grad_hidden * gate * sigmoid_gate).astype(jnp.bfloat16)
    grad_gate_w = left_product(normed_two, grad_gate_low)
    grad_up_w = left_product(normed_two, grad_up_low)
    grad_normed_two = right_product(grad_gate_low, later[6]) + right_product(grad_up_low, later[7])
    grad_resid_norm, grad_gain_two = norm_back(grad_normed_two, resid, inverse_two, gain_two)
    grad_mid = grad_res + grad_resid_norm
    grad_branch = grad_mid.astype(jnp.bfloat16)
    grad_out_w = left_product(attn_flat, grad_branch)
    grad_attn = (
        right_product(grad_branch, later[4])
        .astype(jnp.bfloat16)
        .reshape(local_rows, HEADS, HEAD_DIM)
    )
    delta_rows = jnp.sum(grad_attn.astype(jnp.float32) * attn_heads.astype(jnp.float32), axis=-1)
    pack_length = local_rows * blocks
    empty_back = (
        jnp.zeros((local_rows, HEADS, HEAD_DIM), jnp.float32),
        jnp.zeros((pack_length, 2 * model_width), jnp.float32),
    )
    back_key_piece = lax.all_gather(key_flat, "blk", axis=0, tiled=True)
    back_value_piece = lax.all_gather(value_flat, "blk", axis=0, tiled=True)
    back_seg_piece = lax.all_gather(own_segments, "blk", axis=0, tiled=True)
    back_piece_rows = back_key_piece.shape[0]
    needed = (jnp.int32(0) <= own_start + local_rows - 1) & (
        back_seg_piece[back_piece_rows - 1] >= own_segments[0]
    )

    def back_sweep(current):

        def back_visit(number, partial_value):
            grad_query_acc, grad_pairs = partial_value
            offset = number * local_rows
            key_block = lax.dynamic_slice_in_dim(back_key_piece, offset, local_rows, 0).reshape(
                local_rows, HEADS, HEAD_DIM
            )
            value_block = lax.dynamic_slice_in_dim(back_value_piece, offset, local_rows, 0).reshape(
                local_rows, HEADS, HEAD_DIM
            )
            seg_block = lax.dynamic_slice_in_dim(back_seg_piece, offset, local_rows, 0)
            key_index = offset + jnp.arange(local_rows, dtype=jnp.int32)
            allowed = score_mask(own_segments, query_index, seg_block, key_index)
            part_query, part_key, part_value = block_grads(
                query_rot, grad_attn, lse_rows, delta_rows, allowed, key_block, value_block
            )
            new_rows = jnp.concatenate(
                [
                    part_key.reshape(local_rows, model_width),
                    part_value.reshape(local_rows, model_width),
                ],
                axis=1,
            )
            existing = lax.dynamic_slice_in_dim(grad_pairs, offset, local_rows, 0)
            grad_pairs = lax.dynamic_update_slice_in_dim(grad_pairs, existing + new_rows, offset, 0)
            return (grad_query_acc + part_query, grad_pairs)

        return lax.fori_loop(0, back_piece_rows // local_rows, back_visit, current)

    grad_query_rot, grad_pairs_all = lax.cond(
        needed, back_sweep, lambda unchanged: unchanged, empty_back
    )
    own_pairs = lax.psum_scatter(
        grad_pairs_all.astype(jnp.bfloat16), "blk", scatter_dimension=0, tiled=True
    ).astype(jnp.float32)
    grad_key_rot = own_pairs[:, :model_width].reshape(local_rows, HEADS, HEAD_DIM)
    grad_value_heads = own_pairs[:, model_width:].reshape(local_rows, HEADS, HEAD_DIM)
    grad_query_low = (
        rotate(grad_query_rot, cosine_table, -sine_table)
        .reshape(local_rows, model_width)
        .astype(jnp.bfloat16)
    )
    grad_key_low = (
        rotate(grad_key_rot, cosine_table, -sine_table)
        .reshape(local_rows, model_width)
        .astype(jnp.bfloat16)
    )
    grad_value_low = grad_value_heads.reshape(local_rows, model_width).astype(jnp.bfloat16)
    grad_query_w = left_product(normed, grad_query_low)
    grad_key_w = left_product(normed, grad_key_low)
    grad_value_w = left_product(normed, grad_value_low)
    grad_normed = (
        right_product(grad_query_low, later[1])
        + right_product(grad_key_low, later[2])
        + right_product(grad_value_low, later[3])
    )
    grad_x_norm, grad_gain_one = norm_back(grad_normed, x_float, inverse_one, gain_one)
    grad_input = (grad_mid + grad_x_norm).astype(jnp.bfloat16)
    summed = (
        lax.psum_scatter(grad_gain_one, ("dp", "blk"), scatter_dimension=0, tiled=True),
        lax.psum_scatter(grad_query_w, ("dp", "blk"), scatter_dimension=0, tiled=True),
        lax.psum_scatter(grad_key_w, ("dp", "blk"), scatter_dimension=0, tiled=True),
        lax.psum_scatter(grad_value_w, ("dp", "blk"), scatter_dimension=0, tiled=True),
        lax.psum_scatter(grad_out_w, ("dp", "blk"), scatter_dimension=0, tiled=True),
        lax.psum_scatter(grad_gain_two, ("dp", "blk"), scatter_dimension=0, tiled=True),
        lax.psum_scatter(grad_gate_w, ("dp", "blk"), scatter_dimension=0, tiled=True),
        lax.psum_scatter(grad_up_w, ("dp", "blk"), scatter_dimension=0, tiled=True),
        lax.psum_scatter(grad_down, ("dp", "blk"), scatter_dimension=0, tiled=True),
    )
    return (
        output.reshape(1, local_rows, model_width),
        grad_input.reshape(1, local_rows, model_width),
        summed[0],
        summed[1],
        summed[2],
        summed[3],
        summed[4],
        summed[5],
        summed[6],
        summed[7],
        summed[8],
    )


BF = jnp.bfloat16
F32 = jnp.float32
VMEM = pltpu.VMEM
LANES = 256


def ids():
    dp, blk = lax.axis_index("dp"), lax.axis_index("blk")
    return dp // 2, dp % 2, blk // 2, blk % 2, blk


def flip(bit, other):
    total = 0
    weight = 1
    while weight <= 2:
        own = (bit // weight) % 2
        total = total + weight * ((1 - own) if (other // weight) % 2 else own)
        weight *= 2
    return total


def aligned(value, multiple):
    return pl.multiple_of(value, multiple)


def dot(a, b, ca=1, cb=0):
    return lax.dot_general(a, b, (((ca,), (cb,)), ((), ())), preferred_element_type=F32)


def call(kernel, outs, ins, anys=0, scratch=(), flops=0, nbytes=0):
    blocked = len(ins) - anys
    return pl.pallas_call(
        kernel,
        out_shape=[jax.ShapeDtypeStruct(shape, dtype) for shape, dtype in outs],
        in_specs=[pl.BlockSpec(memory_space=VMEM)] * blocked
        + [pl.BlockSpec(memory_space=pl.ANY)] * anys,
        out_specs=[pl.BlockSpec(memory_space=VMEM)] * len(outs),
        scratch_shapes=list(scratch),
        compiler_params=pltpu.CompilerParams(vmem_limit_bytes=56 * 1024 * 1024),
        cost_estimate=pl.CostEstimate(flops=flops, bytes_accessed=nbytes, transcendentals=0),
    )(*ins)


def chip_rows(xy, zr, z, x, y):
    return 4 * flip(z, zr) + 2 * flip(x, xy // 2) + flip(y, xy % 2)


def assembly(pieces, dst, sems, rows, z, x, y, view=lambda ref, zr: ref.at[zr]):
    copies = []
    for xy in range(4):
        for zr in range(4):
            chip = chip_rows(xy, zr, z, x, y)
            copies.append(
                pltpu.make_async_copy(
                    view(pieces[xy], zr),
                    dst.at[pl.ds(aligned(chip * rows, rows), rows)],
                    sems.at[4 * xy + zr],
                )
            )
    return copies


def half_swap(tile, lane):
    return jnp.where(lane % 64 < 32, pltpu.roll(tile, 96, 1), pltpu.roll(tile, 32, 1))


def attend_kernel(x0, x1, x2, x3, cos, sin, start, wa, wb,
                  q_o, k_o, v_o, n_o, attn_o, lse_o, gains_o, w_o, sems):
    z, x, y, c, b = ids()
    copies = []
    for xr, piece in enumerate((wa, wb)):
        for zr in range(4):
            dp = 2 * flip(z, zr) + flip(x, xr)
            copies.append(
                pltpu.make_async_copy(
                    piece.at[zr], w_o.at[pl.ds(aligned(dp * 96, 96), 96)], sems.at[4 * xr + zr]
                )
            )
    for copy in copies:
        copy.start()
    for copy in copies:
        copy.wait()
    last = w_o[:, 512:640].astype(F32).T
    gains = last[64:72, :]
    gains_o[...] = gains
    gain = gains[0:1, :]
    weights = w_o[...]
    lane = lax.broadcasted_iota(jnp.int32, (256, 128), 1)
    for k, piece in enumerate((x0, x1, x2, x3)):
        rows = pl.ds(aligned(flip(b, k) * 256, 256), 256)
        values = piece[...].astype(F32)
        inverse = lax.rsqrt(jnp.mean(values * values, axis=-1, keepdims=True) + EPS)
        normed = (values * inverse * gain).astype(BF)
        n_o[rows, :] = normed
        qkv = dot(normed, weights)
        cosine, sine = cos[rows, :], sin[rows, :]
        tiles = []
        for t in range(3):
            tile = qkv[:, 128 * t : 128 * t + 128]
            tiles.append(tile * cosine + half_swap(tile, lane) * sine)
        r1, r2 = pltpu.roll(tiles[1], 64, 1), pltpu.roll(tiles[2], 64, 1)
        low = lane < 64
        zero = jnp.zeros_like(r1)
        q_o[rows, 0:128] = tiles[0].astype(BF)
        q_o[rows, 128:256] = jnp.where(low, tiles[1], zero).astype(BF)
        k_o[rows, 0:128] = jnp.where(low, r1, r2).astype(BF)
        k_o[rows, 128:256] = jnp.where(low, r2, zero).astype(BF)
        v_o[rows, 0:128] = qkv[:, 384:512].astype(BF)
        v_o[rows, 128:256] = jnp.where(low, qkv[:, 512:640], zero).astype(BF)
    head = lax.broadcasted_iota(jnp.int32, (256, LANES), 1) // 64
    for i in range(4):
        width = 256 * (i + 1)
        query = q_o[256 * i : 256 * i + 256, :]
        begin = start[256 * i : 256 * i + 256, :]
        column = lax.broadcasted_iota(jnp.int32, (256, width), 1)
        row = lax.broadcasted_iota(jnp.int32, (256, width), 0) + 256 * i
        allowed = (column <= row) & (column >= begin)
        total = jnp.zeros((256, LANES), F32)
        stats = jnp.zeros((256, 128), F32)
        for h in range(3):
            mine = jnp.where(head == h, query, jnp.zeros_like(query))
            scores = dot(mine, k_o[0:width, :], 1, 1) * SCALE
            scores = jnp.where(allowed, scores, NEG)
            top = jnp.max(scores, axis=-1, keepdims=True)
            weight = jnp.exp(scores - top)
            norm = jnp.sum(weight, axis=-1, keepdims=True)
            mixed = dot(weight.astype(BF), v_o[0:width, :]) / norm
            total = jnp.where(head == h, mixed, total)
            stats = jnp.where(lane == h, top + jnp.log(norm), stats)
        attn_o[flip(b, i)] = total.astype(BF)
        lse_o[256 * i : 256 * i + 256, :] = stats


def attend(xs, cos, sin, start, wa, wb):
    outs = [((1024, LANES), BF)] * 3 + [
        ((1024, 768), BF), ((4, 256, LANES), BF), ((1024, 128), F32), ((8, 768), F32), ((768, 640), BF),
    ]
    return call(
        attend_kernel, outs, [*xs, cos, sin, start, wa, wb], anys=2,
        scratch=[pltpu.SemaphoreType.DMA((8,))], flops=4_000_000_000, nbytes=8_000_000,
    )


def wo_copies(own, other, wo, sems, z, x, y, c):
    copies = []
    for which, pieces in enumerate((own, other)):
        half = flip(c, which)
        for xy in range(4):
            for zr in range(4):
                chip = chip_rows(xy, zr, z, x, y)
                copies.append(
                    pltpu.make_async_copy(
                        pieces.at[xy, zr],
                        wo.at[half, pl.ds(aligned(chip * 48, 48), 48)],
                        sems.at[which, 4 * xy + zr],
                    )
                )
    return copies


def out_kernel(a0, a1, a2, a3, x0, gains, own, other, resid_o, n_o, stack_o, wo_o, sems):
    z, x, y, c, b = ids()
    copies = wo_copies(own, other, wo_o, sems, z, x, y, c)
    for copy in copies:
        copy.start()
    for copy in copies:
        copy.wait()
    total = [jnp.zeros((256, 384), F32)] * 2
    for k, piece in enumerate((a0, a1, a2, a3)):
        rows = pl.ds(aligned(flip(b, k) * 192, 192), 192)
        values = piece[...]
        stack_o[k] = values
        for half in range(2):
            total[half] += dot(values[:, 0:192], wo_o[half, rows, :])
    resid = x0[...].astype(F32) + jnp.concatenate(total, axis=1)
    resid_o[...] = resid
    inverse = lax.rsqrt(jnp.mean(resid * resid, axis=-1, keepdims=True) + EPS)
    n_o[...] = (resid * inverse * gains[1:2, :]).astype(BF)


def project(a, x0, gains, own, other):
    outs = [((256, 768), F32), ((256, 768), BF), ((4, 256, LANES), BF), ((2, 768, 384), BF)]
    return call(
        out_kernel, outs, [*a, x0, gains, own, other], anys=2,
        scratch=[pltpu.SemaphoreType.DMA((2, 16))], flops=400_000_000, nbytes=4_000_000,
    )


def hidden_kernel(n0, n1, ct0, ct1, *refs):
    (g, u, d, (hid_o, dg_o, du_o, keep_o, send_o, wg_o, wu_o, wd_o), sems) = (
        refs[0:4], refs[4:8], refs[8:12], refs[12:20], refs[20])
    z, x, y, c, b = ids()
    copies = assembly(g, wg_o, sems.at[0], 48, z, x, y, lambda ref, zr: ref.at[zr, :, pl.ds(0, 1024)])
    copies += assembly(u, wu_o, sems.at[1], 48, z, x, y)
    copies += assembly(d, wd_o, sems.at[2], 64, z, x, y)
    for copy in copies:
        copy.start()
    for copy in copies:
        copy.wait()
    normed = jnp.concatenate([n0[...], n1[...]], axis=0)
    cot = jnp.concatenate([ct0[...], ct1[...]], axis=0)
    for j in range(4):
        cols = slice(256 * j, 256 * j + 256)
        gate = dot(normed, wg_o[:, cols])
        up = dot(normed, wu_o[:, cols])
        back = dot(cot, wd_o[cols, :], 1, 1)
        sig = 1.0 / (1.0 + jnp.exp(-gate))
        silu = gate * sig
        hidden = (silu * up).astype(BF)
        hid_o[:, cols] = hidden
        dg_o[:, cols] = (back * up * sig * (1.0 + gate * (1.0 - sig))).astype(BF)
        du_o[:, cols] = (back * silu).astype(BF)
        grad = dot(hidden, cot, 0, 0)
        for yp in range(2):
            low, high = grad[64 * yp : 64 * yp + 64], grad[128 + 64 * yp : 192 + 64 * yp]
            keep_o[flip(y, yp) % 2, flip(z, j)] = jnp.where(x == 0, low, high).astype(BF)
            send_o[flip(y, yp) % 2, flip(z, j)] = jnp.where(x == 0, high, low).astype(BF)


def hidden_and_back(n, ct, g, u, d):
    outs = [((512, 1024), BF)] * 3 + [((2, 4, 64, 768), BF)] * 2 + [((768, 1024), BF)] * 2 + [((1024, 768), BF)]
    return call(
        hidden_kernel, outs, [*n, *ct, *g, *u, *d], anys=12,
        scratch=[pltpu.SemaphoreType.DMA((3, 16))], flops=3_300_000_000, nbytes=12_000_000,
    )


def store_by_y(grad, cols, keep_o, send_o, z, x, y):
    for zp in range(4):
        for xp in range(2):
            at = 48 * (4 * zp + 2 * xp)
            low, high = grad[at : at + 48], grad[at + 48 : at + 96]
            keep_o[flip(x, xp) % 2, flip(z, zp), :, cols] = jnp.where(y == 0, low, high).astype(BF)
            send_o[flip(x, xp) % 2, flip(z, zp), :, cols] = jnp.where(y == 0, high, low).astype(BF)


def gate_kernel(n0, n1, dg, du, wg, wu, keep_o, send_o, own_o, other_o):
    z, x, y, c, b = ids()
    normed = jnp.concatenate([n0[...].T, n1[...].T], axis=1)
    for j in range(4):
        cols = slice(256 * j, 256 * j + 256)
        store_by_y(dot(normed, dg[:, cols]), cols, keep_o, send_o, z, x, y)
    for t, out in enumerate((own_o, other_o)):
        rows = slice(256 * t, 256 * t + 256)
        out[...] = dot(dg[rows, :], wg[...], 1, 1) + dot(du[rows, :], wu[...], 1, 1)


def gate_back(n, dg, du, wg, wu):
    outs = [((2, 4, 48, 1024), BF)] * 2 + [((256, 768), F32)] * 2
    return call(gate_kernel, outs, [*n, dg, du, wg, wu], flops=2_500_000_000, nbytes=9_000_000)


def mid_kernel(gn_own, gn_in, resid, ct0, gains, wo, mid_o, branch_o, grad_o, gain_o):
    z, x, y, c, b = ids()
    grad = gn_own[...] + gn_in[...]
    values = resid[...]
    inverse = lax.rsqrt(jnp.mean(values * values, axis=-1, keepdims=True) + EPS)
    unit = values * inverse
    scaled = grad * gains[1:2, :]
    gain_o[...] = jnp.broadcast_to(jnp.sum(grad * unit, axis=0, keepdims=True), gain_o.shape)
    mid = ct0[...].astype(F32) + inverse * (
        scaled - unit * jnp.mean(scaled * unit, axis=-1, keepdims=True)
    )
    mid_o[...] = mid
    branch = mid.astype(BF)
    branch_o[...] = branch
    pad = jnp.zeros((256, LANES - 192), BF)
    for k in range(4):
        rows = pl.ds(aligned(flip(b, k) * 192, 192), 192)
        part = dot(branch[:, 0:384], wo[0, rows, :], 1, 1) + dot(branch[:, 384:768], wo[1, rows, :], 1, 1)
        grad_o[k] = jnp.concatenate([part.astype(BF), pad], axis=1)


def mid_back(gn_own, gn_in, resid, ct0, gains, wo):
    outs = [((256, 768), F32), ((256, 768), BF), ((4, 256, LANES), BF), ((8, 768), F32)]
    return call(mid_kernel, outs, [gn_own, gn_in, resid, ct0, gains, wo], flops=400_000_000, nbytes=5_000_000)


def up_out_kernel(n0, n1, du, s0, s1, br0, br1, keep_o, send_o, grad):
    z, x, y, c, b = ids()
    normed = jnp.concatenate([n0[...].T, n1[...].T], axis=1)
    for j in range(4):
        cols = slice(256 * j, 256 * j + 256)
        store_by_y(dot(normed, du[:, cols]), cols, keep_o, send_o, z, x, y)
    own = [br[:, 0:384] for br in (br0, br1)]
    far = [br[:, 384:768] for br in (br0, br1)]
    branch = [jnp.where(c == 0, a, f) for a, f in zip(own, far)]
    for k in range(4):
        part = dot(s0[k], branch[0], 0, 0) + dot(s1[k ^ 1], branch[1], 0, 0)
        grad[pl.ds(aligned(flip(b, k) * 192, 192), 192), :] = part[0:192]
    store_by_y(grad[...], slice(1024, 1408), keep_o, send_o, z, x, y)


def up_out_back(n, du, s, br):
    outs = [((2, 4, 48, 1408), BF)] * 2
    return call(
        up_out_kernel, outs, [*n, du, *s, *br], scratch=[pltpu.VMEM((768, 384), F32)],
        flops=1_200_000_000, nbytes=8_000_000,
    )


def down_kernel(hid, wd, resid, own_o, other_o):
    own_o[...] = resid[...] + dot(hid[0:256, :], wd[...])
    other_o[...] = dot(hid[256:512, :], wd[...])


def down(hid, wd, resid):
    outs = [((256, 768), F32)] * 2
    return call(down_kernel, outs, [hid, wd, resid], flops=800_000_000, nbytes=5_000_000)


def attend_back_kernel(q, k, v, n, attn, g0, g1, g2, g3, lse, cos, sin, start, w, x0, x1, x2, x3, gain2,
                       keep_o, send_o, gk_o, gs_o, do, dq, dk, dv, grads, wide):
    z, x, y, c, b = ids()
    for kk, piece in enumerate((g0, g1, g2, g3)):
        do[pl.ds(aligned(flip(b, kk) * 256, 256), 256), :] = piece[...]
    dk[...] = jnp.zeros_like(dk)
    dv[...] = jnp.zeros_like(dv)
    head = lax.broadcasted_iota(jnp.int32, (256, LANES), 1) // 64
    for i in range(4):
        width = 256 * (i + 1)
        rows = slice(256 * i, 256 * i + 256)
        query, out_grad = q[rows, :], do[rows, :]
        begin = start[rows, :]
        column = lax.broadcasted_iota(jnp.int32, (256, width), 1)
        row = lax.broadcasted_iota(jnp.int32, (256, width), 0) + 256 * i
        allowed = (column <= row) & (column >= begin)
        product = out_grad.astype(F32) * attn[flip(b, i)].astype(F32)
        total = jnp.zeros((256, LANES), F32)
        for h in range(3):
            here = head == h
            mine = jnp.where(here, query, jnp.zeros_like(query))
            ours = jnp.where(here, out_grad, jnp.zeros_like(out_grad))
            delta = jnp.sum(jnp.where(here, product, 0.0), axis=-1, keepdims=True)
            scores = dot(mine, k[0:width, :], 1, 1) * SCALE
            prob = jnp.exp(jnp.where(allowed, scores - lse[rows, h : h + 1], NEG))
            dv[0:width, :] += dot(prob.astype(BF), ours, 0, 0)
            dprob = dot(ours, v[0:width, :], 1, 1)
            dscore = (prob * (dprob - delta)).astype(BF)
            dk[0:width, :] += dot(dscore, mine, 0, 0)
            total = jnp.where(here, dot(dscore, k[0:width, :]), total)
        dq[rows, :] = total
    lane = lax.broadcasted_iota(jnp.int32, (256, 128), 1)
    low = lane < 64
    zero = jnp.zeros((256, 128), F32)
    for i in range(4):
        rows = slice(256 * i, 256 * i + 256)
        cosine, sine = cos[rows, :] * SCALE, sin[rows, :] * SCALE
        turned = []
        for ref in (dq, dk):
            for t in range(2):
                tile = ref[rows, 128 * t : 128 * t + 128]
                turned.append(tile * cosine - half_swap(tile, lane) * sine)
        k0, k1 = pltpu.roll(turned[2], 64, 1), pltpu.roll(turned[3], 64, 1)
        grads[rows, 0:128] = turned[0].astype(BF)
        grads[rows, 128:256] = jnp.where(low, turned[1], k0).astype(BF)
        grads[rows, 256:384] = jnp.where(low, k0, k1).astype(BF)
        grads[rows, 384:512] = dv[rows, 0:128].astype(BF)
        grads[rows, 512:640] = jnp.where(low, dv[rows, 128:256], zero).astype(BF)
    gain_sum = jnp.zeros((1, 768), F32)
    for kk, piece in enumerate((x0, x1, x2, x3)):
        rows = pl.ds(aligned(flip(b, kk) * 256, 256), 256)
        grad = dot(grads[rows, :], w[...], 1, 1)
        values = piece[...].astype(F32)
        inverse = lax.rsqrt(jnp.mean(values * values, axis=-1, keepdims=True) + EPS)
        gain_sum += jnp.sum(grad * (values * inverse), axis=0, keepdims=True)
        (gs_o if kk % 2 else gk_o)[kk // 2] = grad.astype(BF)
    row_at = lax.broadcasted_iota(jnp.int32, (128, 768), 0)
    gain_rows = jnp.where(row_at == 64, gain_sum, jnp.where(row_at == 65, gain2[0:1, :], 0.0))
    gain_columns = gain_rows.T
    normed = n[...].T
    for j in range(5):
        cols = slice(128 * j, 128 * j + 128)
        part = dot(normed, grads[:, cols])
        if j == 4:
            part = part + gain_columns
        wide[:, cols] = part
    for xr, out in enumerate((keep_o, send_o)):
        for zr in range(4):
            dp = 2 * flip(z, zr) + flip(x, xr)
            out[zr] = wide[pl.ds(aligned(dp * 96, 96), 96), :].astype(BF)


def attend_back(q, k, v, n, attn, g, lse, cos, sin, start, w, xs, gain2):
    outs = [((4, 96, 640), BF)] * 2 + [((2, 256, 768), BF)] * 2
    return call(
        attend_back_kernel, outs, [q, k, v, n, attn, *g, lse, cos, sin, start, w, *xs, gain2],
        scratch=[
            pltpu.VMEM((1024, LANES), BF), pltpu.VMEM((1024, LANES), F32), pltpu.VMEM((1024, LANES), F32),
            pltpu.VMEM((1024, LANES), F32), pltpu.VMEM((1024, 640), BF), pltpu.VMEM((768, 640), F32),
        ],
        flops=10_000_000_000, nbytes=12_000_000,
    )


def last_kernel(kept, arrived, mid, x0, gains, out):
    grad = kept[...].astype(F32) + arrived[...].astype(F32)
    values = x0[...].astype(F32)
    inverse = lax.rsqrt(jnp.mean(values * values, axis=-1, keepdims=True) + EPS)
    unit = values * inverse
    scaled = grad * gains[0:1, :]
    out[...] = (
        mid[...] + inverse * (scaled - unit * jnp.mean(scaled * unit, axis=-1, keepdims=True))
    ).astype(BF)


def swap_z(v, k):
    return lax.ppermute(v, "dp", [(i, i ^ (2 * k)) for i in range(8)])


def swap_x(v):
    return lax.ppermute(v, "dp", [(i, i ^ 1) for i in range(8)])


def swap_b(v, k):
    return lax.ppermute(v, "blk", [(i, i ^ k) for i in range(4)])


def swap_core(v):
    return swap_b(v, 1)


def swap_y(v):
    return swap_b(v, 2)


def stack_z(v):
    return jnp.stack([v] + [swap_z(v, k) for k in (1, 2, 3)])


def by_index(four, bits):
    one, two = bits % 2 == 1, bits // 2 == 1
    a, b, c, d = four
    a, b, c, d = jnp.where(one, b, a), jnp.where(one, a, b), jnp.where(one, d, c), jnp.where(one, c, d)
    return [jnp.where(two, c, a), jnp.where(two, d, b), jnp.where(two, a, c), jnp.where(two, b, d)]


def sum_z(v):
    terms = [v[0]] + [swap_z(v[k], k) for k in (1, 2, 3)]
    return sum(term.astype(F32) for term in terms)


def added(kept, arrived):
    return (kept.astype(F32) + arrived.astype(F32)).astype(BF)


def fast_shards(tokens, segments, positions, cotangent, attn_gain, w_query, w_key, w_value, w_out,
                mlp_gain, w_gate, w_up, w_down):
    z, x, y, c, b = ids()
    first = c == 0
    x0 = tokens[0]
    ct0 = cotangent[0]

    gains24 = jnp.stack([attn_gain, mlp_gain], axis=1)
    parts = jnp.concatenate(
        [w.reshape(24, 4, 192) for w in (w_query, w_key, w_value)]
        + [jnp.broadcast_to(jnp.pad(gains24, ((0, 0), (0, 62)))[:, None, :], (24, 4, 64))], axis=2)
    relative = jnp.stack(by_index([parts[:, j] for j in range(4)], b))
    qkv_z = [relative] + [swap_z(relative, k) for k in (1, 2, 3)]

    x2 = swap_y(x0)
    x1 = swap_core(x0)
    x3 = swap_core(x2)
    ct1 = swap_core(ct0)
    where_at = lax.all_gather(positions[0], "blk", axis=0, tiled=True)

    gate_parts = w_gate.reshape(24, 16, 2, 64)
    up_parts = w_up.reshape(24, 16, 2, 64)
    out_parts = w_out.reshape(24, 2, 384)

    def half(which):
        pick = lambda a, low, high: jnp.where(first == (which == 0), low, high)
        return jnp.concatenate(
            [
                pick(0, gate_parts[:, :, 0], gate_parts[:, :, 1]).reshape(24, 1024),
                pick(0, out_parts[:, 0], out_parts[:, 1]),
                pick(0, up_parts[:, :, 0], up_parts[:, :, 1]).reshape(24, 1024),
            ], axis=1)

    mine, theirs = half(0), half(1)
    arrived = swap_core(theirs)
    chip = jnp.concatenate([jnp.where(first, mine, arrived), jnp.where(first, arrived, mine)], axis=0)

    to_blk = [jnp.stack([part[k] for part in qkv_z]) for k in range(4)]
    from_blk = [to_blk[0]] + [swap_b(to_blk[k], k) for k in (1, 2, 3)]
    qkv_a = jnp.stack(by_index(from_blk, b), axis=1).reshape(4, 96, 640)
    qkv_b = swap_x(qkv_a)

    g_z = stack_z(chip[:, :1408])
    u_z = stack_z(chip[:, 1408:])
    d_z = stack_z(w_down)
    g_x, g_y = swap_x(g_z), swap_y(g_z)
    u_y, u_x = swap_y(u_z), swap_x(u_z)
    d_y, d_x = swap_y(d_z), swap_x(d_z)
    g = (g_z, g_y, g_x, swap_y(g_x))
    u = (u_z, u_y, u_x, swap_x(u_y))
    d = (d_z, d_y, d_x, swap_x(d_y))
    out_own = jnp.stack([piece[:, :, 1024:] for piece in g])
    out_other = swap_core(out_own)

    lane = jnp.arange(128)
    inverse = jnp.exp(-math.log(10000.0) * (lane % 32).astype(F32) / 32)
    angles = where_at.astype(F32)[:, None] * inverse[None, :]
    cos = jnp.cos(angles)
    sin = jnp.sin(angles) * jnp.where(lane % 64 < 32, -1.0, 1.0)[None, :]
    start = (jnp.arange(1024, dtype=jnp.int32) - where_at)[:, None]

    xs = (x0, x1, x2, x3)
    q, k, v, normed, attn, lse, gains, wqkv = attend(xs, cos, sin, start, qkv_a, qkv_b)
    a = [attn[0]] + [swap_b(attn[j], j) for j in (2, 3, 1)]
    a = [a[0], a[3], a[1], a[2]]
    resid, n0, s0, wo = project(a, x0, gains, out_own, out_other)
    n1 = swap_core(n0)
    s1 = swap_core(s0)

    hid, dg, du, down_keep, down_send, wg, wu, wd = hidden_and_back((n0, n1), (ct0, ct1), g, u, d)
    down_in = swap_x(down_send)
    gate_keep, gate_send, gn_own, gn_other = gate_back((n0, n1), dg, du, wg, wu)
    gn_in = swap_core(gn_other)
    gate_in = swap_y(gate_send)
    mid, br0, grad_heads, gain2 = mid_back(gn_own, gn_in, resid, ct0, gains, wo)
    ga = [grad_heads[0]] + [swap_b(grad_heads[j], j) for j in (2, 3, 1)]
    ga = [ga[0], ga[3], ga[1], ga[2]]
    br1 = swap_core(br0)
    up_keep, up_send = up_out_back((n0, n1), du, (s0, s1), (br0, br1))
    up_in = swap_y(up_send)

    qkv_keep, qkv_send, gn_keep, gn_send = attend_back(
        q, k, v, normed, attn, ga, lse, cos, sin, start, wqkv, xs, gain2)
    qkv_in = swap_x(qkv_send)

    down_2 = added(down_keep, down_in)
    down_2in = swap_y(down_2[1])
    grad_down = sum_z(added(down_2[0], down_2in))
    gate_2 = added(gate_keep, gate_in)
    gate_2in = swap_x(gate_2[1])
    gate_rows = sum_z(added(gate_2[0], gate_2in))
    up_2 = added(up_keep, up_in)
    up_2in = swap_x(up_2[1])
    up_rows = sum_z(added(up_2[0], up_2in))

    own_half, other_half = down(hid, wd, resid)
    output = (own_half + swap_core(other_half)).astype(BF)

    gn_2 = added(gn_keep, swap_core(gn_send))
    gn_2in = swap_y(gn_2[1])
    (grad_input,) = call(last_kernel, [((256, 768), BF)], [gn_2[0], gn_2in, mid, x0, gains],
                         flops=10_000_000, nbytes=3_000_000)

    rows96 = sum_z(added(qkv_keep, qkv_in)).astype(BF).reshape(4, 24, 640)
    order = by_index([rows96[j] for j in range(4)], b)
    pieces = by_index([order[0]] + [swap_b(order[j], j) for j in (1, 2, 3)], b)
    whole = [piece.astype(F32) for piece in pieces]
    grad_query, grad_key, grad_value = (
        jnp.concatenate([piece[:, 192 * j : 192 * j + 192] for piece in whole], axis=1) for j in range(3))
    gain_sums = sum(piece[:, 576:578] for piece in whole)

    rows48 = jnp.concatenate([gate_rows, up_rows], axis=1)
    to_other = jnp.where(first, rows48[24:], rows48[:24])
    to_own = jnp.where(first, rows48[:24], rows48[24:])
    came = swap_core(to_other)
    even, odd = jnp.where(first, to_own, came), jnp.where(first, came, to_own)

    def woven(at):
        return jnp.stack([even[:, at : at + 1024].reshape(24, 16, 64), odd[:, at : at + 1024].reshape(24, 16, 64)],
                         axis=2).reshape(24, 2048)

    grad_out = jnp.concatenate([even[:, 2048:], odd[:, 2048:]], axis=1)
    return (output[None], grad_input[None], gain_sums[:, 0], grad_query, grad_key, grad_value, grad_out,
            gain_sums[:, 1], woven(0), woven(1024), grad_down)


def solution(mesh):
    fits = dict(mesh.shape) == {"dp": 8, "blk": 4}
    return jax.shard_map(
        fast_shards if fits else shards,
        mesh=mesh,
        in_specs=(
            P("dp", "blk", None),
            P("dp", "blk"),
            P("dp", "blk"),
            P("dp", "blk", None),
            P(("dp", "blk")),
            P(("dp", "blk"), None),
            P(("dp", "blk"), None),
            P(("dp", "blk"), None),
            P(("dp", "blk"), None),
            P(("dp", "blk")),
            P(("dp", "blk"), None),
            P(("dp", "blk"), None),
            P(("dp", "blk"), None),
        ),
        out_specs=(
            P("dp", "blk", None),
            P("dp", "blk", None),
            P(("dp", "blk")),
            P(("dp", "blk"), None),
            P(("dp", "blk"), None),
            P(("dp", "blk"), None),
            P(("dp", "blk"), None),
            P(("dp", "blk")),
            P(("dp", "blk"), None),
            P(("dp", "blk"), None),
            P(("dp", "blk"), None),
        ),
        check_vma=False,
    )
```

```python
import math

import jax
import jax.numpy as jnp
from jax import lax
from jax.experimental import pallas as pl
from jax.experimental.pallas import tpu as pltpu
from jax.sharding import PartitionSpec as P

HEADS = 12
HEAD_DIM = 64


EPS = 1e-05
SCALE = 0.125
NEG = -1e30


def rope_tables(slot_positions, half_dim):
    inverse = jnp.exp(-math.log(10000.0) * jnp.arange(half_dim, dtype=jnp.float32) / half_dim)
    angles = slot_positions.astype(jnp.float32)[:, None] * inverse[None, :]
    return (jnp.cos(angles)[:, None, :], jnp.sin(angles)[:, None, :])


def rotate(tensor, cosine_table, sine_table):
    half_dim = tensor.shape[-1] // 2
    leading = tensor[..., :half_dim]
    trailing = tensor[..., half_dim:]
    return jnp.concatenate(
        [
            leading * cosine_table - trailing * sine_table,
            trailing * cosine_table + leading * sine_table,
        ],
        axis=-1,
    )


def matmul(left_matrix, right_matrix):
    return jnp.dot(left_matrix, right_matrix, preferred_element_type=jnp.float32)


def left_product(left_matrix, right_matrix):
    return lax.dot_general(
        left_matrix, right_matrix, (((0,), (0,)), ((), ())), preferred_element_type=jnp.float32
    )


def right_product(left_matrix, right_matrix):
    return lax.dot_general(
        left_matrix, right_matrix, (((1,), (1,)), ((), ())), preferred_element_type=jnp.float32
    )


def norm_back(grad_normed, values, inverse, gain):
    unit_normed = values * inverse
    scaled = grad_normed * gain
    grad_gain = jnp.sum(grad_normed * unit_normed, axis=0)
    grad_values = inverse * (
        scaled - unit_normed * jnp.mean(scaled * unit_normed, axis=-1, keepdims=True)
    )
    return (grad_values, grad_gain)


def score_mask(query_segments, query_index, key_segments, key_index):
    return (query_segments[:, None] == key_segments[None, :]) & (
        key_index[None, :] <= query_index[:, None]
    )


def block_grads(query_block, grad_block, lse_rows, delta_rows, allowed, key_block, value_block):
    scores = (
        jnp.einsum("qhd,khd->hqk", query_block, key_block, preferred_element_type=jnp.float32)
        * SCALE
    )
    probability = jnp.exp(jnp.where(allowed[None], scores - lse_rows.T[:, :, None], NEG))
    grad_value = jnp.einsum(
        "hqk,qhd->khd",
        probability.astype(jnp.bfloat16),
        grad_block,
        preferred_element_type=jnp.float32,
    )
    grad_probs = jnp.einsum(
        "qhd,khd->hqk", grad_block, value_block, preferred_element_type=jnp.float32
    )
    grad_scores = (probability * (grad_probs - delta_rows.T[:, :, None])).astype(jnp.bfloat16)
    grad_query = (
        jnp.einsum("hqk,khd->qhd", grad_scores, key_block, preferred_element_type=jnp.float32)
        * SCALE
    )
    grad_key = (
        jnp.einsum("hqk,qhd->khd", grad_scores, query_block, preferred_element_type=jnp.float32)
        * SCALE
    )
    return (grad_query, grad_key, grad_value)


def shards(
    tokens,
    segments,
    positions,
    cotangent,
    attn_gain,
    w_query,
    w_key,
    w_value,
    w_out,
    mlp_gain,
    w_gate,
    w_up,
    w_down,
):
    local_rows = tokens.shape[1]
    model_width = tokens.shape[2]
    blocks = lax.axis_size("blk")
    own_start = lax.axis_index("blk") * local_rows
    query_index = own_start + jnp.arange(local_rows, dtype=jnp.int32)
    own_segments = segments[0]
    cosine_table, sine_table = rope_tables(positions[0], HEAD_DIM // 2)
    x_float = tokens[0].astype(jnp.float32)
    gathered = (
        lax.all_gather(attn_gain, ("dp", "blk"), axis=0, tiled=True),
        lax.all_gather(w_query, ("dp", "blk"), axis=0, tiled=True),
        lax.all_gather(w_key, ("dp", "blk"), axis=0, tiled=True),
        lax.all_gather(w_value, ("dp", "blk"), axis=0, tiled=True),
        lax.all_gather(w_out, ("dp", "blk"), axis=0, tiled=True),
        lax.all_gather(mlp_gain, ("dp", "blk"), axis=0, tiled=True),
        lax.all_gather(w_gate, ("dp", "blk"), axis=0, tiled=True),
        lax.all_gather(w_up, ("dp", "blk"), axis=0, tiled=True),
        lax.all_gather(w_down, ("dp", "blk"), axis=0, tiled=True),
    )
    gain_one = gathered[0].astype(jnp.float32)
    gain_two = gathered[5].astype(jnp.float32)
    inverse_one = lax.rsqrt(jnp.mean(x_float * x_float, axis=-1, keepdims=True) + EPS)
    normed = (x_float * inverse_one * gain_one).astype(jnp.bfloat16)
    query_rot = rotate(
        matmul(normed, gathered[1]).reshape(local_rows, HEADS, HEAD_DIM), cosine_table, sine_table
    ).astype(jnp.bfloat16)
    key_rot = rotate(
        matmul(normed, gathered[2]).reshape(local_rows, HEADS, HEAD_DIM), cosine_table, sine_table
    ).astype(jnp.bfloat16)
    value_heads = (
        matmul(normed, gathered[3]).astype(jnp.bfloat16).reshape(local_rows, HEADS, HEAD_DIM)
    )
    key_flat = key_rot.reshape(local_rows, model_width)
    value_flat = value_heads.reshape(local_rows, model_width)
    start_state = (
        jnp.full((HEADS, local_rows), NEG, jnp.float32),
        jnp.zeros((HEADS, local_rows), jnp.float32),
        jnp.zeros((local_rows, HEADS, HEAD_DIM), jnp.float32),
    )
    key_piece = lax.all_gather(key_flat, "blk", axis=0, tiled=True)
    value_piece = lax.all_gather(value_flat, "blk", axis=0, tiled=True)
    seg_piece = lax.all_gather(own_segments, "blk", axis=0, tiled=True)
    piece_rows = key_piece.shape[0]
    needed = (jnp.int32(0) <= own_start + local_rows - 1) & (
        seg_piece[piece_rows - 1] >= own_segments[0]
    )

    def attend_sweep(current):

        def attend_visit(number, partial_value):
            running_max, running_sum, weighted = partial_value
            offset = number * local_rows
            key_block = lax.dynamic_slice_in_dim(key_piece, offset, local_rows, 0).reshape(
                local_rows, HEADS, HEAD_DIM
            )
            value_block = lax.dynamic_slice_in_dim(value_piece, offset, local_rows, 0).reshape(
                local_rows, HEADS, HEAD_DIM
            )
            seg_block = lax.dynamic_slice_in_dim(seg_piece, offset, local_rows, 0)
            key_index = offset + jnp.arange(local_rows, dtype=jnp.int32)
            allowed = score_mask(own_segments, query_index, seg_block, key_index)
            scores = (
                jnp.einsum("qhd,khd->hqk", query_rot, key_block, preferred_element_type=jnp.float32)
                * SCALE
            )
            scores = jnp.where(allowed[None], scores, NEG)
            new_max = jnp.maximum(running_max, jnp.max(scores, axis=-1))
            probability = jnp.where(allowed[None], jnp.exp(scores - new_max[:, :, None]), 0.0)
            factor = jnp.exp(running_max - new_max)
            running_sum = running_sum * factor + jnp.sum(probability, axis=-1)
            weighted = weighted * factor.T[:, :, None] + jnp.einsum(
                "hqk,khd->qhd",
                probability.astype(jnp.bfloat16),
                value_block,
                preferred_element_type=jnp.float32,
            )
            return (new_max, running_sum, weighted)

        return lax.fori_loop(0, piece_rows // local_rows, attend_visit, current)

    final_max, final_sum, final_weighted = lax.cond(
        needed, attend_sweep, lambda unchanged: unchanged, start_state
    )
    attn_heads = (final_weighted / final_sum.T[:, :, None]).astype(jnp.bfloat16)
    lse_rows = (final_max + jnp.log(final_sum)).T
    attn_flat = attn_heads.reshape(local_rows, model_width)
    resid = x_float + matmul(attn_flat, gathered[4])
    inverse_two = lax.rsqrt(jnp.mean(resid * resid, axis=-1, keepdims=True) + EPS)
    normed_two = (resid * inverse_two * gain_two).astype(jnp.bfloat16)
    gate = matmul(normed_two, gathered[6])
    up_values = matmul(normed_two, gathered[7])
    hidden = (jax.nn.silu(gate) * up_values).astype(jnp.bfloat16)
    output = (resid + matmul(hidden, gathered[8])).astype(jnp.bfloat16)
    later = (
        lax.all_gather(attn_gain, ("dp", "blk"), axis=0, tiled=True),
        lax.all_gather(w_query, ("dp", "blk"), axis=0, tiled=True),
        lax.all_gather(w_key, ("dp", "blk"), axis=0, tiled=True),
        lax.all_gather(w_value, ("dp", "blk"), axis=0, tiled=True),
        lax.all_gather(w_out, ("dp", "blk"), axis=0, tiled=True),
        lax.all_gather(mlp_gain, ("dp", "blk"), axis=0, tiled=True),
        lax.all_gather(w_gate, ("dp", "blk"), axis=0, tiled=True),
        lax.all_gather(w_up, ("dp", "blk"), axis=0, tiled=True),
        lax.all_gather(w_down, ("dp", "blk"), axis=0, tiled=True),
    )
    grad_res = cotangent[0].astype(jnp.float32)
    grad_mlp = grad_res.astype(jnp.bfloat16)
    grad_down = left_product(hidden, grad_mlp)
    grad_hidden = right_product(grad_mlp, later[8])
    sigmoid_gate = jax.nn.sigmoid(gate)
    grad_gate_low = (
        grad_hidden * up_values * sigmoid_gate * (1.0 + gate * (1.0 - sigmoid_gate))
    ).astype(jnp.bfloat16)
    grad_up_low = (grad_hidden * gate * sigmoid_gate).astype(jnp.bfloat16)
    grad_gate_w = left_product(normed_two, grad_gate_low)
    grad_up_w = left_product(normed_two, grad_up_low)
    grad_normed_two = right_product(grad_gate_low, later[6]) + right_product(grad_up_low, later[7])
    grad_resid_norm, grad_gain_two = norm_back(grad_normed_two, resid, inverse_two, gain_two)
    grad_mid = grad_res + grad_resid_norm
    grad_branch = grad_mid.astype(jnp.bfloat16)
    grad_out_w = left_product(attn_flat, grad_branch)
    grad_attn = (
        right_product(grad_branch, later[4])
        .astype(jnp.bfloat16)
        .reshape(local_rows, HEADS, HEAD_DIM)
    )
    delta_rows = jnp.sum(grad_attn.astype(jnp.float32) * attn_heads.astype(jnp.float32), axis=-1)
    pack_length = local_rows * blocks
    empty_back = (
        jnp.zeros((local_rows, HEADS, HEAD_DIM), jnp.float32),
        jnp.zeros((pack_length, 2 * model_width), jnp.float32),
    )
    back_key_piece = lax.all_gather(key_flat, "blk", axis=0, tiled=True)
    back_value_piece = lax.all_gather(value_flat, "blk", axis=0, tiled=True)
    back_seg_piece = lax.all_gather(own_segments, "blk", axis=0, tiled=True)
    back_piece_rows = back_key_piece.shape[0]
    needed = (jnp.int32(0) <= own_start + local_rows - 1) & (
        back_seg_piece[back_piece_rows - 1] >= own_segments[0]
    )

    def back_sweep(current):

        def back_visit(number, partial_value):
            grad_query_acc, grad_pairs = partial_value
            offset = number * local_rows
            key_block = lax.dynamic_slice_in_dim(back_key_piece, offset, local_rows, 0).reshape(
                local_rows, HEADS, HEAD_DIM
            )
            value_block = lax.dynamic_slice_in_dim(back_value_piece, offset, local_rows, 0).reshape(
                local_rows, HEADS, HEAD_DIM
            )
            seg_block = lax.dynamic_slice_in_dim(back_seg_piece, offset, local_rows, 0)
            key_index = offset + jnp.arange(local_rows, dtype=jnp.int32)
            allowed = score_mask(own_segments, query_index, seg_block, key_index)
            part_query, part_key, part_value = block_grads(
                query_rot, grad_attn, lse_rows, delta_rows, allowed, key_block, value_block
            )
            new_rows = jnp.concatenate(
                [
                    part_key.reshape(local_rows, model_width),
                    part_value.reshape(local_rows, model_width),
                ],
                axis=1,
            )
            existing = lax.dynamic_slice_in_dim(grad_pairs, offset, local_rows, 0)
            grad_pairs = lax.dynamic_update_slice_in_dim(grad_pairs, existing + new_rows, offset, 0)
            return (grad_query_acc + part_query, grad_pairs)

        return lax.fori_loop(0, back_piece_rows // local_rows, back_visit, current)

    grad_query_rot, grad_pairs_all = lax.cond(
        needed, back_sweep, lambda unchanged: unchanged, empty_back
    )
    own_pairs = lax.psum_scatter(
        grad_pairs_all.astype(jnp.bfloat16), "blk", scatter_dimension=0, tiled=True
    ).astype(jnp.float32)
    grad_key_rot = own_pairs[:, :model_width].reshape(local_rows, HEADS, HEAD_DIM)
    grad_value_heads = own_pairs[:, model_width:].reshape(local_rows, HEADS, HEAD_DIM)
    grad_query_low = (
        rotate(grad_query_rot, cosine_table, -sine_table)
        .reshape(local_rows, model_width)
        .astype(jnp.bfloat16)
    )
    grad_key_low = (
        rotate(grad_key_rot, cosine_table, -sine_table)
        .reshape(local_rows, model_width)
        .astype(jnp.bfloat16)
    )
    grad_value_low = grad_value_heads.reshape(local_rows, model_width).astype(jnp.bfloat16)
    grad_query_w = left_product(normed, grad_query_low)
    grad_key_w = left_product(normed, grad_key_low)
    grad_value_w = left_product(normed, grad_value_low)
    grad_normed = (
        right_product(grad_query_low, later[1])
        + right_product(grad_key_low, later[2])
        + right_product(grad_value_low, later[3])
    )
    grad_x_norm, grad_gain_one = norm_back(grad_normed, x_float, inverse_one, gain_one)
    grad_input = (grad_mid + grad_x_norm).astype(jnp.bfloat16)
    summed = (
        lax.psum_scatter(grad_gain_one, ("dp", "blk"), scatter_dimension=0, tiled=True),
        lax.psum_scatter(grad_query_w, ("dp", "blk"), scatter_dimension=0, tiled=True),
        lax.psum_scatter(grad_key_w, ("dp", "blk"), scatter_dimension=0, tiled=True),
        lax.psum_scatter(grad_value_w, ("dp", "blk"), scatter_dimension=0, tiled=True),
        lax.psum_scatter(grad_out_w, ("dp", "blk"), scatter_dimension=0, tiled=True),
        lax.psum_scatter(grad_gain_two, ("dp", "blk"), scatter_dimension=0, tiled=True),
        lax.psum_scatter(grad_gate_w, ("dp", "blk"), scatter_dimension=0, tiled=True),
        lax.psum_scatter(grad_up_w, ("dp", "blk"), scatter_dimension=0, tiled=True),
        lax.psum_scatter(grad_down, ("dp", "blk"), scatter_dimension=0, tiled=True),
    )
    return (
        output.reshape(1, local_rows, model_width),
        grad_input.reshape(1, local_rows, model_width),
        summed[0],
        summed[1],
        summed[2],
        summed[3],
        summed[4],
        summed[5],
        summed[6],
        summed[7],
        summed[8],
    )


BF = jnp.bfloat16
F32 = jnp.float32
VMEM = pltpu.VMEM
LANES = 256


def ids():
    dp, blk = lax.axis_index("dp"), lax.axis_index("blk")
    return dp // 2, dp % 2, blk // 2, blk % 2, blk


def flip(bit, other):
    total = 0
    weight = 1
    while weight <= 2:
        own = (bit // weight) % 2
        total = total + weight * ((1 - own) if (other // weight) % 2 else own)
        weight *= 2
    return total


def exclusive(a, b):
    low, high = (a + b) % 2, (a // 2 + b // 2) % 2
    return low + 2 * high


def aligned(value, multiple):
    return pl.multiple_of(value, multiple)


def dot(a, b, ca=1, cb=0):
    return lax.dot_general(a, b, (((ca,), (cb,)), ((), ())), preferred_element_type=F32)


HBM = "hbm"


def call(kernel, outs, ins, anys=(), scratch=(), flops=0, nbytes=0, grant=24):
    def place(far):
        return pl.BlockSpec(memory_space=pltpu.MemorySpace.HBM if far else VMEM)

    return pl.pallas_call(
        kernel,
        out_shape=[jax.ShapeDtypeStruct(out[0], out[1]) for out in outs],
        in_specs=[place(i in anys) for i in range(len(ins))],
        out_specs=[place(len(out) > 2) for out in outs],
        scratch_shapes=list(scratch),
        compiler_params=pltpu.CompilerParams(vmem_limit_bytes=grant * 1024 * 1024),
        cost_estimate=pl.CostEstimate(flops=flops, bytes_accessed=nbytes, transcendentals=0),
    )(*ins)


def pair(low, first, second):
    (a, i), (b, j) = first, second
    left = a[:, 128 * (i // 2) : 128 * (i // 2) + 128]
    right = b[:, 128 * (j // 2) : 128 * (j // 2) + 128]
    left = pltpu.roll(left, 64, 1) if i % 2 else left
    right = right if j % 2 else pltpu.roll(right, 64, 1)
    return jnp.where(low, left, right)


def pairs(low, blocks):
    return jnp.concatenate([pair(low, blocks[i], blocks[i + 1]) for i in range(0, len(blocks), 2)], axis=1)


def prepare_kernel(gains, place, wq_h, wk_h, wv_h, wg_h, wu_h, x_h, r0_o, r1_o, r2_o, r3_o, x_o,
                   wq, wk, wv, wg, wu, order, sems):
    z, x, y, c, b = ids()
    far, near = (wq_h, wk_h, wv_h, wg_h, wu_h), (wq, wk, wv, wg, wu)
    copies = [pltpu.make_async_copy(a, d, sems.at[i]) for i, (a, d) in enumerate(zip(far, near))]
    copies.append(pltpu.make_async_copy(x_h, x_o.at[pl.ds(0, 256)], sems.at[5]))
    for copy in copies:
        copy.start()
    for copy in copies[:5]:
        copy.wait()
    low = lax.broadcasted_iota(jnp.int32, (wq.shape[0], 128), 1) < 64
    q, k, v, g, gate, up = (ref[...].astype(F32) for ref in (wq, wk, wv, gains, wg, wu))
    at = jnp.broadcast_to(place[...], (16, 256)).astype(F32)
    tens = jnp.floor(at * (1.0 / 32))
    x_o[256:272, :] = jnp.concatenate([tens, at - 32.0 * tens, jnp.zeros_like(at)], axis=1).astype(BF)
    for j in range(4):
        blocks = [(w, 3 * j + t) for w in (q, k, v) for t in range(3)] + [(g, 1)]
        order[flip(b, j)] = pairs(low, blocks).astype(BF)
        wide = pairs(low, [(w, 4 * i + j) for w in (gate, up) for i in range(8)])
        rest = jnp.concatenate([wide[8 * t : 8 * t + 8, 768:1024] for t in range(3)], axis=1)
        x_o[272 + 32 * j : 304 + 32 * j, :] = jnp.concatenate([wide[:, 0:768], rest], axis=0).astype(BF)
    for k, out in enumerate((r0_o, r1_o, r2_o, r3_o)):
        out[...] = order[k]
    copies[5].wait()


def prepare(tokens, place, wq, wk, wv, gains, wg, wu):
    outs = [((24, 640), BF)] * 4 + [((400, 768), BF)]
    scratch = [*[VMEM((24, 768), BF)] * 3, *[VMEM((24, 2048), BF)] * 2, VMEM((4, 24, 640), BF),
               pltpu.SemaphoreType.DMA((7,))]
    return call(prepare_kernel, outs, [gains, place, wq, wk, wv, wg, wu, tokens], anys=range(2, 8), scratch=scratch,
                flops=1_000_000, nbytes=1_000_000, grant=60)


def columns_kernel(r0, r1, r2, r3, out, rows):
    z, x, y, c, b = ids()
    for k, piece in enumerate((r0, r1, r2, r3)):
        rows[pl.ds(aligned(flip(b, k) * 24, 24), 24), :] = piece[...].astype(F32)
    out[...] = rows[...].astype(BF)


def columns(pieces):
    (out,) = call(columns_kernel, [((96, 640), BF)], pieces, scratch=[VMEM((96, 640), F32)], flops=1_000_000, nbytes=300_000)
    return out


def units_kernel(x0, x1, x2, x3, out, rows):
    z, x, y, c, b = ids()
    for k, piece in enumerate((x0, x1, x2, x3)):
        part = piece[pl.ds(aligned(272 + 32 * b, 16), 32), :].astype(F32)
        rest = jnp.concatenate([part[24:32, 256 * t : 256 * t + 256] for t in range(3)], axis=0)
        rows[pl.ds(aligned(flip(b, k) * 24, 24), 24), :] = jnp.concatenate([part[0:24], rest], axis=1)
    out[...] = rows[...].astype(BF)


def units(xs):
    (out,) = call(units_kernel, [((96, 1024), BF)], xs, scratch=[VMEM((96, 1024), F32)], flops=1_000_000, nbytes=3_000_000)
    return out


def finish_kernel(h0, h1, h2, h3, u0, u1, u2, u3, q_o, k_o, v_o, gate_o, up_o, gains_o, heads, units):
    z, x, y, c, b = ids()
    for k in range(4):
        heads[k] = (h0, h1, h2, h3)[k][...]
        units[k] = (u0, u1, u2, u3)[k][...]
    low = lax.broadcasted_iota(jnp.int32, (heads.shape[1], 128), 1) < 64
    parts = [heads[flip(b, j)].astype(F32) for j in range(4)]
    for t, out in enumerate((q_o, k_o, v_o)):
        out[...] = pairs(low, [(parts[m // 3], 3 * t + m % 3) for m in range(12)])
    gains_o[...] = parts[0][:, 512:640] + parts[1][:, 512:640] + parts[2][:, 512:640] + parts[3][:, 512:640]
    parts = [units[flip(b, j)].astype(F32) for j in range(4)]
    for t, out in enumerate((gate_o, up_o)):
        out[...] = pairs(low, [(parts[m % 4], 8 * t + m // 4) for m in range(32)])


def finish(heads, units):
    outs = [((24, 768), F32)] * 3 + [((24, 2048), F32)] * 2 + [((24, 128), F32)]
    return call(finish_kernel, outs, [*heads, *units], scratch=[VMEM((4, 24, 640), BF), VMEM((4, 24, 1024), BF)],
                flops=1_000_000, nbytes=2_000_000)


def tables_kernel(x0, x1, x2, x3, cos_o, sin_o, start_o, rows_o, marks, cos, sin, start, rows, sems, out_sems):
    z, x, y, c, b = ids()
    copies = [
        pltpu.make_async_copy(piece.at[pl.ds(256, 16)], marks.at[k], sems.at[k])
        for k, piece in enumerate((x0, x1, x2, x3))
    ]
    for copy in copies:
        copy.start()
    for copy in copies:
        copy.wait()
    lane = lax.broadcasted_iota(jnp.int32, (256, 128), 1)
    row = lax.broadcasted_iota(jnp.int32, (256, 128), 0)
    inverse = jnp.exp((lane % 32).astype(F32) * (-math.log(10000.0) / 32))
    sign = jnp.where(lane % 64 < 32, -1.0, 1.0)
    for k in range(4):
        own = marks[k].astype(F32)
        place = (32.0 * own[:, 0:256] + own[:, 256:512])[0:1]
        slot = lax.broadcasted_iota(jnp.int32, (8, 256), 1) + 256 * flip(b, k)
        rows[k] = slot.astype(F32) - jnp.broadcast_to(place, (8, 256))
        place = jnp.broadcast_to(place, (128, 256)).T
        angles = place * inverse
        cos[k] = jnp.cos(angles)
        sin[k] = jnp.sin(angles) * sign
        start[k] = 256 * flip(b, k) + row - place.astype(jnp.int32)
    leaving = [
        pltpu.make_async_copy(ref, out, out_sems.at[i])
        for i, (ref, out) in enumerate(((cos, cos_o), (sin, sin_o), (start, start_o), (rows, rows_o)))
    ]
    for copy in leaving:
        copy.start()
    for copy in leaving:
        copy.wait()


def tables(xs):
    outs = [((4, 256, 128), F32, HBM)] * 2 + [((4, 256, 128), jnp.int32, HBM), ((4, 8, 256), F32, HBM)]
    scratch = [
        VMEM((4, 16, 768), BF), *[VMEM((4, 256, 128), F32)] * 2, VMEM((4, 256, 128), jnp.int32),
        VMEM((4, 8, 256), F32), pltpu.SemaphoreType.DMA((4,)), pltpu.SemaphoreType.DMA((4,)),
    ]
    return call(tables_kernel, outs, xs, anys=range(4), scratch=scratch, flops=10_000_000, nbytes=3_000_000)


def half_swap(tile, lane):
    return jnp.where(lane % 64 < 32, pltpu.roll(tile, 96, 1), pltpu.roll(tile, 32, 1))


def attend_kernel(x0, x1, x2, x3, wa, wb, cos_h, sin_h, start_h,
                  q_o, k_o, v_o, n_o, w_o, attn_o, lse_o, gains_o, a0_o, a1_o, a2_o, a3_o,
                  xs, w, q, k, v, n, attn, lse, cos, sin, start, sems, out_sems):
    z, x, y, c, b = ids()
    copies = []
    for xr, piece in enumerate((wa, wb)):
        for zr in range(4):
            dp = 2 * flip(z, zr) + flip(x, xr)
            copies.append(pltpu.make_async_copy(
                piece.at[zr], w.at[pl.ds(aligned(dp * 96, 96), 96)], sems.at[4 * xr + zr]))
    for kk, piece in enumerate((x0, x1, x2, x3)):
        copies.append(pltpu.make_async_copy(piece.at[pl.ds(0, 272)], xs.at[kk], sems.at[8 + kk]))
    for at, (ref, near) in enumerate(((cos_h, cos), (sin_h, sin), (start_h, start))):
        copies.append(pltpu.make_async_copy(ref, near, sems.at[12 + at]))
    for copy in copies:
        copy.start()
    for copy in copies[:8] + copies[12:14]:
        copy.wait()
    leaving = [pltpu.make_async_copy(w, w_o, out_sems.at[0])]
    leaving[0].start()
    last = w[:, 512:640].astype(F32).T
    gains = last[64:72, :]
    gains_o[...] = gains
    gain = gains[0:1, :]
    lane = lax.broadcasted_iota(jnp.int32, (256, 128), 1)
    low = lane < 64
    for kk in range(4):
        rows = pl.ds(aligned(flip(b, kk) * 256, 256), 256)
        copies[8 + kk].wait()
        values = xs[kk, 0:256, :].astype(F32)
        inverse = lax.rsqrt(jnp.mean(values * values, axis=-1, keepdims=True) + EPS)
        normed = (values * inverse * gain).astype(BF)
        n[rows, :] = normed
        qkv = dot(normed, w[...])
        cosine, sine = cos[kk], sin[kk]
        tiles = []
        for t in range(3):
            tile = qkv[:, 128 * t : 128 * t + 128]
            tiles.append(tile * cosine + half_swap(tile, lane) * sine)
        r1, r2 = pltpu.roll(tiles[1], 64, 1), pltpu.roll(tiles[2], 64, 1)
        zero = jnp.zeros_like(r1)
        q[rows, 0:128] = tiles[0].astype(BF)
        q[rows, 128:256] = jnp.where(low, tiles[1], zero).astype(BF)
        k[rows, 0:128] = jnp.where(low, r1, r2).astype(BF)
        k[rows, 128:256] = jnp.where(low, r2, zero).astype(BF)
        v[rows, 0:128] = qkv[:, 384:512].astype(BF)
        v[rows, 128:256] = jnp.where(low, qkv[:, 512:640], zero).astype(BF)
    for at, (ref, out) in enumerate(((n, n_o), (q, q_o), (k, k_o), (v, v_o))):
        leaving.append(pltpu.make_async_copy(ref, out, out_sems.at[3 + at]))
        leaving[-1].start()
    copies[14].wait()
    head = lax.broadcasted_iota(jnp.int32, (256, LANES), 1) // 64
    for i in range(4):
        width = 256 * (i + 1)
        query = q[256 * i : 256 * i + 256, :]
        begin = start[flip(b, i)][:, 0:1]
        column = lax.broadcasted_iota(jnp.int32, (256, width), 1)
        row = lax.broadcasted_iota(jnp.int32, (256, width), 0) + 256 * i
        allowed = (column <= row) & (column >= begin)
        total = jnp.zeros((256, LANES), F32)
        stats = jnp.zeros((256, 128), F32)
        for h in range(3):
            mine = jnp.where(head == h, query, jnp.zeros_like(query))
            scores = dot(mine, k[0:width, :], 1, 1) * SCALE
            scores = jnp.where(allowed, scores, NEG)
            top = jnp.max(scores, axis=-1, keepdims=True)
            weight = jnp.exp(scores - top)
            norm = jnp.sum(weight, axis=-1, keepdims=True)
            mixed = dot(weight.astype(BF), v[0:width, :]) / norm
            total = jnp.where(head == h, mixed, total)
            stats = jnp.where(lane == h, top + jnp.log(norm), stats)
        attn[256 * i : 256 * i + 256, :] = total.astype(BF)
        lse[:, 256 * i : 256 * i + 256] = stats.T[0:8]
    for at, (ref, out) in enumerate(((attn, attn_o), (lse, lse_o))):
        leaving.append(pltpu.make_async_copy(ref, out, out_sems.at[1 + at]))
        leaving[-1].start()
    for kk, out in enumerate((a0_o, a1_o, a2_o, a3_o)):
        out[...] = attn[pl.ds(aligned(flip(b, kk) * 256, 256), 256), :]
    for copy in leaving:
        copy.wait()


def attend(xs, wa, wb, cos, sin, start):
    outs = [
        *[((1024, LANES), BF, HBM)] * 3, ((1024, 768), BF, HBM), ((768, 640), BF, HBM), ((1024, LANES), BF, HBM),
        ((8, 1024), F32, HBM), ((8, 768), F32), *[((256, LANES), BF)] * 4,
    ]
    return call(
        attend_kernel, outs, [*xs, wa, wb, cos, sin, start], anys=range(9), grant=60,
        scratch=[
            VMEM((4, 272, 768), BF), VMEM((768, 640), BF), *[VMEM((1024, LANES), BF)] * 3, VMEM((1024, 768), BF),
            VMEM((1024, LANES), BF), VMEM((8, 1024), F32), *[VMEM((4, 256, 128), F32)] * 2, VMEM((4, 256, 128), jnp.int32),
            pltpu.SemaphoreType.DMA((15,)), pltpu.SemaphoreType.DMA((7,)),
        ],
        flops=4_000_000_000, nbytes=8_000_000,
    )


def out_kernel(a0, a1, a2, a3, x0, gains, own, other, resid_o, n_o, wo_o, stack_o, wide):
    z, x, y, c, b = ids()
    for xy in range(4):
        for zr in range(4):
            chip = 8 * flip(z, zr) + 4 * flip(x, xy // 2) + 2 * flip(y, xy % 2)
            for core, pieces in enumerate((own, other)):
                at = aligned((chip + flip(c, core)) * 24, 24)
                wide[pl.ds(at, 24), :] = pieces[xy, zr].astype(F32)
    wo_o[...] = wide[...].astype(BF)
    total = x0[0:256, :].astype(F32)
    for k, piece in enumerate((a0, a1, a2, a3)):
        rows = pl.ds(aligned(flip(b, k) * 192, 192), 192)
        stack_o[k] = piece[...]
        total += dot(piece[:, 0:192], wo_o[rows, :])
    resid_o[...] = total
    inverse = lax.rsqrt(jnp.mean(total * total, axis=-1, keepdims=True) + EPS)
    n_o[...] = (total * inverse * gains[1:2, :]).astype(BF)


def project(a, x0, gains, own, other):
    outs = [((256, 768), F32), ((256, 768), BF), ((768, 768), BF), ((4, 256, LANES), BF)]
    return call(out_kernel, outs, [*a, x0, gains, own, other], scratch=[VMEM((768, 768), F32)],
                flops=400_000_000, nbytes=4_000_000)


def hidden_kernel(n0, n1, n2, n3, ct0, ct1, ct2, ct3, gu_near, gu_far, d_near, d_far,
                  n_o, ct_o, hid_o, dg_o, du_o, wgu_o, wd_o, sems):
    z, x, y, c, b = ids()
    copies = []
    for xr, (gu, d) in enumerate(((gu_near, d_near), (gu_far, d_far))):
        for zr in range(4):
            dp = 2 * flip(z, zr) + flip(x, xr)
            at = 4 * xr + zr
            copies.append(pltpu.make_async_copy(
                gu.at[zr], wgu_o.at[pl.ds(aligned(dp * 96, 96), 96)], sems.at[0, at]))
            copies.append(pltpu.make_async_copy(
                d.at[zr, pl.ds(0, 64)], wd_o.at[pl.ds(aligned(dp * 64, 64), 64)], sems.at[1, at]))
    for k, piece in enumerate((ct0, ct1, ct2, ct3)):
        copies.append(pltpu.make_async_copy(piece, ct_o.at[pl.ds(256 * k, 256)], sems.at[2, k]))
    for copy in copies:
        copy.start()
    for k in range(4):
        n_o[256 * k : 256 * k + 256, :] = (n0, n1, n2, n3)[k][...]
    for copy in copies:
        copy.wait()
    for k in range(4):
        rows = slice(256 * k, 256 * k + 256)
        normed, cot = n_o[rows, :], ct_o[rows, :]
        for j in range(2):
            cols = slice(256 * j, 256 * j + 256)
            gate = dot(normed, wgu_o[:, 256 * j : 256 * j + 256])
            up = dot(normed, wgu_o[:, 512 + 256 * j : 768 + 256 * j])
            back = dot(cot, wd_o[cols, :], 1, 1)
            sig = 1.0 / (1.0 + jnp.exp(-gate))
            silu = gate * sig
            hid_o[rows, cols] = (silu * up).astype(BF)
            dg_o[rows, cols] = (back * up * sig * (1.0 + gate * (1.0 - sig))).astype(BF)
            du_o[rows, cols] = (back * silu).astype(BF)


def hidden_and_back(n, ct, pieces):
    outs = [((1024, 768), BF)] * 2 + [((1024, 512), BF)] * 3 + [((768, 1024), BF), ((512, 768), BF)]
    return call(
        hidden_kernel, outs, [*n, *ct, *pieces], anys=range(4, 12),
        scratch=[pltpu.SemaphoreType.DMA((3, 8))], flops=2_500_000_000, nbytes=8_000_000,
    )


def normed_back_kernel(dg, du, wgu, own_o, far_o, send_o):
    for k in range(4):
        rows = slice(256 * k, 256 * k + 256)
        grad = dot(dg[rows, :], wgu[:, 0:512], 1, 1) + dot(du[rows, :], wgu[:, 512:1024], 1, 1)
        if k == 0:
            own_o[...] = grad
        elif k == 2:
            far_o[...] = grad
        else:
            send_o[k // 2] = grad.astype(BF)


def normed_back(dg, du, wgu):
    outs = [((256, 768), F32)] * 2 + [((2, 256, 768), BF)]
    return call(normed_back_kernel, outs, [dg, du, wgu], flops=1_600_000_000, nbytes=6_000_000)


def store_by_x(grad, rows, cols, keep_o, send_o, z, x):
    for zp in range(4):
        at = 2 * rows * zp
        low, high = grad[at : at + rows], grad[at + rows : at + 2 * rows]
        keep_o[flip(z, zp), :, cols] = jnp.where(x == 0, low, high).astype(BF)
        send_o[flip(z, zp), :, cols] = jnp.where(x == 0, high, low).astype(BF)


def ff_grads_kernel(n, ct, hid, dg, du, gu_keep_o, gu_send_o, d_keep_o, d_send_o):
    z, x, y, c, b = ids()
    normed = n[...].T
    for j in range(4):
        cols = slice(256 * j, 256 * j + 256)
        part = (dg, du)[j // 2][:, 256 * (j % 2) : 256 * (j % 2) + 256]
        store_by_x(dot(normed, part), 96, cols, gu_keep_o, gu_send_o, z, x)
    hidden = hid[...].T
    for j in range(3):
        cols = slice(256 * j, 256 * j + 256)
        store_by_x(dot(hidden, ct[:, cols]), 64, cols, d_keep_o, d_send_o, z, x)


def ff_grads(n, ct, hid, dg, du):
    outs = [((4, 96, 1024), BF)] * 2 + [((4, 64, 768), BF)] * 2
    return call(ff_grads_kernel, outs, [n, ct, hid, dg, du], flops=2_400_000_000, nbytes=10_000_000)


def mid_kernel(gn_own, gn_in, resid, ct0, gains, wo, out_own, out_far, out_in, here_o, there_o, mid_o, branch_o, g0_o, g1_o, g2_o, g3_o, gain_o):
    z, x, y, c, b = ids()
    here_o[...] = out_own[...] + out_in[0].astype(F32)
    there_o[...] = (out_far[...] + out_in[1].astype(F32)).astype(BF)
    grad = gn_own[...] + gn_in[...].astype(F32)
    values = resid[...]
    inverse = lax.rsqrt(jnp.mean(values * values, axis=-1, keepdims=True) + EPS)
    unit = values * inverse
    scaled = grad * gains[1:2, :]
    gain_o[...] = jnp.broadcast_to(jnp.sum(grad * unit, axis=0, keepdims=True), gain_o.shape)
    mid = ct0[...].astype(F32) + inverse * (
        scaled - unit * jnp.mean(scaled * unit, axis=-1, keepdims=True)
    )
    mid_o[...] = mid
    branch = mid.astype(BF)
    branch_o[...] = branch
    pad = jnp.zeros((256, LANES - 192), BF)
    for k in range(4):
        rows = pl.ds(aligned(flip(b, k) * 192, 192), 192)
        part = dot(branch, wo[rows, :], 1, 1)
        (g0_o, g1_o, g2_o, g3_o)[k][...] = jnp.concatenate([part.astype(BF), pad], axis=1)


def mid_back(gn_own, gn_in, resid, ct0, gains, wo, out):
    outs = [((256, 768), F32), ((256, 768), BF), ((256, 768), F32), ((256, 768), BF), *[((256, LANES), BF)] * 4, ((8, 768), F32)]
    return call(mid_kernel, outs, [gn_own, gn_in, resid, ct0, gains, wo, *out], flops=400_000_000, nbytes=5_000_000)


def out_grads_kernel(stack, branch, keep_o, send_o, wide):
    z, x, y, c, b = ids()
    for k in range(4):
        part = dot(stack[k].T, branch[...])[0:192]
        wide[pl.ds(aligned(exclusive(flip(b, k), z) * 192, 192), 192), :] = part
    for cr, out in enumerate((keep_o, send_o)):
        for yr in range(2):
            for xr in range(2):
                for zr in range(4):
                    at = 4 * (flip(x, xr) % 2) + 2 * (flip(y, yr) % 2) + flip(c, cr) % 2 + 8 * zr
                    out[xr, yr, zr] = wide[pl.ds(aligned(at * 24, 24), 24), :].astype(BF)


def out_grads(stack, branch):
    outs = [((2, 2, 4, 24, 768), BF)] * 2
    return call(out_grads_kernel, outs, [stack, branch], scratch=[VMEM((768, 768), F32)],
                flops=400_000_000, nbytes=3_000_000)


def down_kernel(hid, wd, resid, own_o, far_o, send_o):
    for k in range(4):
        part = dot(hid[256 * k : 256 * k + 256, :], wd[...])
        if k == 0:
            own_o[...] = resid[...] + part
        elif k == 2:
            far_o[...] = part
        else:
            send_o[k // 2] = part.astype(BF)


def down(hid, wd, resid):
    outs = [((256, 768), F32)] * 2 + [((2, 256, 768), BF)]
    return call(down_kernel, outs, [hid, wd, resid], flops=800_000_000, nbytes=5_000_000)


def attend_back_kernel(q_h, k_h, v_h, n_h, w_h, attn_h, lse_h, cos_h, sin_h, start_h, x0, x1, x2, x3, g0, g1, g2, g3, gain2_h,
                       keep_h, send_h, gk0_h, gk1_h, gs_h,
                       q, k, v, n, w, attn, lse, cos, sin, start, xs, do, dq, dk, dv, grads, wide, gain2,
                       keep_o, send_o, gk0_o, gk1_o, gs_o, sems, out_sems):
    z, x, y, c, b = ids()
    far = (q_h, k_h, v_h, attn_h, lse_h, start_h, cos_h, sin_h, n_h, w_h)
    near = (q, k, v, attn, lse, start, cos, sin, n, w)
    copies = [pltpu.make_async_copy(a, d, sems.at[i]) for i, (a, d) in enumerate(zip(far, near))]
    copies += [
        pltpu.make_async_copy(a.at[pl.ds(0, 272)], xs.at[i], sems.at[10 + i]) for i, a in enumerate((x0, x1, x2, x3))
    ]
    copies.append(pltpu.make_async_copy(gain2_h, gain2, sems.at[14]))
    first = copies[:6] + [
        pltpu.make_async_copy(a, do.at[pl.ds(aligned(flip(b, i) * 256, 256), 256)], sems.at[15 + i])
        for i, a in enumerate((g0, g1, g2, g3))
    ]
    for copy in first + copies[6:]:
        copy.start()
    dk[...] = jnp.zeros_like(dk)
    dv[...] = jnp.zeros_like(dv)
    for copy in first:
        copy.wait()
    head = lax.broadcasted_iota(jnp.int32, (256, LANES), 1) // 64
    lane = lax.broadcasted_iota(jnp.int32, (256, 128), 1)
    for i in range(4):
        width = 256 * (i + 1)
        rows = slice(256 * i, 256 * i + 256)
        query, out_grad = q[rows, :], do[rows, :]
        product = out_grad.astype(F32) * attn[rows, :].astype(F32)
        delta = jnp.zeros((256, 128), F32)
        for h in range(3):
            delta = jnp.where(
                lane == h, jnp.sum(jnp.where(head == h, product, 0.0), axis=-1, keepdims=True), delta)
        delta = delta.T
        begin = start[flip(b, i)][0:1, :]
        key = lax.broadcasted_iota(jnp.int32, (width, 256), 0)
        slot = lax.broadcasted_iota(jnp.int32, (width, 256), 1) + 256 * i
        allowed = (key <= slot) & (key.astype(F32) >= begin)
        probs, dscores = [], []
        mine = [jnp.where(head == h, query, jnp.zeros_like(query)) for h in range(3)]
        ours = [jnp.where(head == h, out_grad, jnp.zeros_like(out_grad)) for h in range(3)]
        for h in range(3):
            scores = dot(k[0:width, :], mine[h], 1, 1) * SCALE
            prob = jnp.exp(jnp.where(allowed, scores - lse[h : h + 1, rows], NEG))
            dprob = dot(v[0:width, :], ours[h], 1, 1)
            probs.append(prob.astype(BF))
            dscores.append((prob * (dprob - delta[h : h + 1, :])).astype(BF))
        dv[0:width, :] += dot(jnp.concatenate(probs, axis=1), jnp.concatenate(ours, axis=0))
        dk[0:width, :] += dot(jnp.concatenate(dscores, axis=1), jnp.concatenate(mine, axis=0))
        total = jnp.zeros((256, LANES), F32)
        for h in range(3):
            total = jnp.where(head == h, dot(dscores[h], k[0:width, :], 0, 0), total)
        dq[rows, :] = total
    for copy in copies[6:]:
        copy.wait()
    low = lane < 64
    zero = jnp.zeros((256, 128), F32)
    for i in range(4):
        rows = slice(256 * i, 256 * i + 256)
        cosine, sine = cos[flip(b, i)] * SCALE, sin[flip(b, i)] * SCALE
        turned = []
        for ref in (dq, dk):
            for t in range(2):
                tile = ref[rows, 128 * t : 128 * t + 128]
                turned.append(tile * cosine - half_swap(tile, lane) * sine)
        k0, k1 = pltpu.roll(turned[2], 64, 1), pltpu.roll(turned[3], 64, 1)
        grads[rows, 0:128] = turned[0].astype(BF)
        grads[rows, 128:256] = jnp.where(low, turned[1], k0).astype(BF)
        grads[rows, 256:384] = jnp.where(low, k0, k1).astype(BF)
        grads[rows, 384:512] = dv[rows, 0:128].astype(BF)
        grads[rows, 512:640] = jnp.where(low, dv[rows, 128:256], zero).astype(BF)
    leaving = []

    def leave(ref, out):
        leaving.append(pltpu.make_async_copy(ref, out, out_sems.at[len(leaving)]))
        leaving[-1].start()

    gain_sum = jnp.zeros((1, 768), F32)
    for kk in range(4):
        rows = pl.ds(aligned(flip(b, kk) * 256, 256), 256)
        grad = dot(grads[rows, :], w[...], 1, 1)
        values = xs[kk, 0:256, :].astype(F32)
        inverse = lax.rsqrt(jnp.mean(values * values, axis=-1, keepdims=True) + EPS)
        gain_sum += jnp.sum(grad * (values * inverse), axis=0, keepdims=True)
        if kk % 2:
            gs_o[kk // 2] = grad.astype(BF)
        else:
            (gk0_o, gk1_o)[kk // 2][...] = grad.astype(BF)
    for ref, out in ((gs_o, gs_h), (gk0_o, gk0_h), (gk1_o, gk1_h)):
        leave(ref, out)
    row_at = lax.broadcasted_iota(jnp.int32, (128, 768), 0)
    gain_rows = jnp.where(row_at == 64, gain_sum, jnp.where(row_at == 65, gain2[0:1, :], 0.0))
    gain_columns = gain_rows.T
    normed = n[...].T
    for j in range(5):
        cols = slice(128 * j, 128 * j + 128)
        part = dot(normed, grads[:, cols])
        if j == 4:
            part = part + gain_columns
        wide[:, cols] = part
    for xr, (ref, out) in ((1, (send_o, send_h)), (0, (keep_o, keep_h))):
        for zr in range(4):
            dp = 2 * flip(z, zr) + flip(x, xr)
            ref[zr] = wide[pl.ds(aligned(dp * 96, 96), 96), :].astype(BF)
        leave(ref, out)
    for copy in leaving:
        copy.wait()


def attend_back(saved, tabs, xs, g, gain2):
    outs = [((4, 96, 640), BF, HBM)] * 2 + [((256, 768), BF, HBM)] * 2 + [((2, 256, 768), BF, HBM)]
    return call(
        attend_back_kernel, outs, [*saved, *tabs, *xs, *g, gain2], anys=range(19), grant=60,
        scratch=[
            *[VMEM((1024, LANES), BF)] * 3, VMEM((1024, 768), BF), VMEM((768, 640), BF), VMEM((1024, LANES), BF),
            VMEM((8, 1024), F32), *[VMEM((4, 256, 128), F32)] * 2, VMEM((4, 8, 256), F32),
            VMEM((4, 272, 768), BF), VMEM((1024, LANES), BF), *[VMEM((1024, LANES), F32)] * 3,
            VMEM((1024, 640), BF), VMEM((768, 640), F32), VMEM((8, 768), F32),
            *[VMEM(out[0], out[1]) for out in outs], pltpu.SemaphoreType.DMA((19,)), pltpu.SemaphoreType.DMA((5,)),
        ],
        flops=10_000_000_000, nbytes=12_000_000,
    )


def last_kernel(kept, arrived, mid, x0, gains, out):
    grad = kept[...].astype(F32) + arrived[...].astype(F32)
    values = x0[0:256, :].astype(F32)
    inverse = lax.rsqrt(jnp.mean(values * values, axis=-1, keepdims=True) + EPS)
    unit = values * inverse
    scaled = grad * gains[0:1, :]
    out[...] = (
        mid[...] + inverse * (scaled - unit * jnp.mean(scaled * unit, axis=-1, keepdims=True))
    ).astype(BF)


def swap_z(v, k):
    return lax.ppermute(v, "dp", [(i, i ^ (2 * k)) for i in range(8)])


def swap_x(v):
    return lax.ppermute(v, "dp", [(i, i ^ 1) for i in range(8)])


def swap_b(v, k):
    return lax.ppermute(v, "blk", [(i, i ^ k) for i in range(4)])


def swap_core(v):
    return swap_b(v, 1)


def swap_y(v):
    return swap_b(v, 2)


def after(value, *tokens):
    return lax.optimization_barrier((value, tokens))[0]


def stack_z(v):
    return jnp.stack([v] + [swap_z(v, k) for k in (1, 2, 3)])


def by_index(four, bits):
    one, two = bits % 2 == 1, bits // 2 == 1
    a, b, c, d = four
    a, b, c, d = jnp.where(one, b, a), jnp.where(one, a, b), jnp.where(one, d, c), jnp.where(one, c, d)
    return [jnp.where(two, c, a), jnp.where(two, d, b), jnp.where(two, a, c), jnp.where(two, b, d)]


def sum_z(v):
    terms = [v[0]] + [swap_z(v[k], k) for k in (1, 2, 3)]
    return sum(term.astype(F32) for term in terms)


def halve_z(v, far):
    first = [added(v[k], far[k]) for k in range(2)]
    return first[0].astype(F32) + swap_z(first[1], 1).astype(F32)


def added(kept, arrived):
    return (kept.astype(F32) + arrived.astype(F32)).astype(BF)


def fast_shards(tokens, segments, positions, cotangent, attn_gain, w_query, w_key, w_value, w_out,
                mlp_gain, w_gate, w_up, w_down):
    z, x, y, c, b = ids()
    first = c == 0
    x0 = tokens[0]
    ct0 = cotangent[0]

    gain_columns = jnp.pad(jnp.stack([attn_gain, mlp_gain], axis=1), ((0, 0), (64, 62)))
    *parts, x0 = prepare(x0, positions, w_query, w_key, w_value, gain_columns, w_gate, w_up)
    do_own = jnp.concatenate([w_down, w_out], axis=0)
    do_z = [do_own] + [swap_z(do_own, k) for k in (1, 2, 3)]
    from_blk = [parts[0]] + [swap_b(parts[k], k) for k in (1, 2, 3)]

    from_blk, do_z, x0 = lax.optimization_barrier((from_blk, do_z, x0))
    qkv_own = columns(from_blk)
    qkv_z = [qkv_own] + [swap_z(qkv_own, k) for k in (1, 2, 3)]
    do_near = jnp.stack(do_z)
    do_far = swap_x(do_near)
    x2 = swap_y(x0)

    qkv_z, x0, do_far = lax.optimization_barrier((qkv_z, x0, do_far))
    qkv_a = jnp.stack(qkv_z)
    qkv_b = swap_x(qkv_a)
    x1, x3 = swap_core(x0), swap_core(x2)
    xs = (x0, x1, x2, x3)
    tabs = tables(xs)
    out_zx = jnp.stack([do_near[:, 64:], do_far[:, 64:]])
    out_y = swap_y(out_zx)
    gu_near = stack_z(units(xs))

    qkv_b, out_y, tabs, ct0 = lax.optimization_barrier((qkv_b, out_y, tabs, ct0))
    ct2 = swap_y(ct0)
    *saved, gains, a0, a1, a2, a3 = attend(xs, qkv_a, qkv_b, *tabs[:3])

    a1, a2, a3, gu_near, ct2 = lax.optimization_barrier((a1, a2, a3, gu_near, ct2))
    a1, a2, a3 = swap_b(a1, 1), swap_b(a2, 2), swap_b(a3, 3)
    out_own = jnp.stack([out_zx[0], out_y[0], out_zx[1], out_y[1]])
    out_other = swap_core(out_own)
    gu_far = swap_x(after(gu_near, a1))

    a1, a2, a3, out_other, ct0, ct2 = lax.optimization_barrier((a1, a2, a3, out_other, ct0, ct2))
    resid, n0, wo, heads = project((a0, a1, a2, a3), x0, gains, out_own, out_other)
    n2, n1 = swap_y(n0), swap_core(n0)
    ct1, ct3 = swap_core(ct0), swap_core(ct2)
    n2, n1, ct1, ct3, gu_far = lax.optimization_barrier((n2, n1, ct1, ct3, gu_far))
    n3 = swap_core(n2)

    n_all, ct_all, hid, dg, du, wgu, wd = hidden_and_back(
        (n0, n1, n2, n3), (ct0, ct1, ct2, ct3), (gu_near, gu_far, do_near, do_far))
    gn_own, gn_far, gn_send = normed_back(dg, du, wgu)
    gn_in = swap_core(gn_send)
    gu_keep, gu_send, d_keep, d_send = ff_grads(n_all, ct_all, hid, dg, du)
    gn_in, gu_send, d_send, hid = lax.optimization_barrier((gn_in, gu_send, d_send, hid))
    gn_there = swap_y((gn_far + gn_in[1].astype(F32)).astype(BF))
    gn_here = gn_own + gn_in[0].astype(F32)
    out_own, out_far, out_send = down(hid, wd, resid)
    out_in = swap_core(out_send)
    gu_in = swap_x(gu_send)
    gn_there, out_in, d_send = lax.optimization_barrier((gn_there, out_in, d_send))
    out_here, out_2, mid, br0, ga0, ga1, ga2, ga3, gain2 = mid_back(
        gn_here, gn_there, resid, ct0, gains, wo, (out_own, out_far, out_in))
    ga1, ga2, ga3 = swap_b(ga1, 1), swap_b(ga2, 2), swap_b(ga3, 3)
    d_in = swap_x(d_send)
    o_keep, o_send = out_grads(heads, br0)
    o_in = swap_core(o_send)
    o_2 = [added(o_keep[j], o_in[j]) for j in range(2)]
    gu_in = after(gu_in, ga1)
    gu_2 = added(gu_keep, gu_in)
    ga1, ga2, ga3, gu_2, o_2, out_2 = lax.optimization_barrier((ga1, ga2, ga3, gu_2, o_2, out_2))
    gu_far = swap_z(gu_2[2:], 2)
    o_2in = swap_x(o_2[1])
    out_there = swap_y(out_2)
    qkv_keep, qkv_send, gn_keep, gn_keep2, gn_send = attend_back(saved, (tabs[0], tabs[1], tabs[3]), xs, (ga0, ga1, ga2, ga3), gain2)
    qkv_send, gn_send, d_in, o_2in, out_there = lax.optimization_barrier((qkv_send, gn_send, d_in, o_2in, out_there))
    qkv_in = swap_x(qkv_send)
    gn_in2 = swap_core(gn_send)
    d_2 = added(d_keep, d_in)
    d_far = swap_z(d_2[2:], 2)
    o_3 = [added(o_2[0][j], o_2in[j]) for j in range(2)]
    o_3in = swap_y(o_3[1])
    gn_here2 = added(gn_keep, gn_in2[0])
    there_in = swap_y(added(gn_keep2, gn_in2[1]))
    output = (out_here + out_there.astype(F32)).astype(BF)
    qkv_in, o_3in, gu_2, d_2 = lax.optimization_barrier((qkv_in, o_3in, gu_2, d_2))
    o_4 = added(o_3[0], o_3in)
    tail = [
        jnp.concatenate([
            added(qkv_keep[k], qkv_in[k]), o_4[k][:, :640],
            jnp.concatenate([o_4[k][8 * t : 8 * t + 8, 640:] for t in range(3)]
                            + [jnp.zeros((8, 256), BF)], axis=1)], axis=0)
        for k in range(4)
    ]
    tail = [tail[0]] + [swap_z(tail[k], k) for k in (1, 2, 3)]
    gu_rows = halve_z(gu_2, gu_far).astype(BF).reshape(4, 24, 1024)
    gu_order = by_index([gu_rows[j] for j in range(4)], b)
    grad_down = halve_z(d_2, d_far)
    tail, there_in, gu_order, grad_down = lax.optimization_barrier((tail, there_in, gu_order, grad_down))
    rows = sum(term.astype(F32) for term in tail)
    rows96 = rows[:96].astype(BF).reshape(4, 24, 640)
    order = by_index([rows96[j] for j in range(4)], b)
    from_heads = [order[0]] + [swap_b(order[j], j) for j in (1, 2, 3)]
    from_units = [gu_order[0]] + [swap_b(gu_order[j], j) for j in (1, 2, 3)]
    grad_out = jnp.concatenate(
        [rows[96:120], jnp.concatenate([rows[120:128, 128 * t : 128 * t + 128] for t in range(3)], axis=0)], axis=1)
    (grad_input,) = call(last_kernel, [((256, 768), BF)], [gn_here2, there_in, mid, x0, gains],
                         flops=10_000_000, nbytes=3_000_000)

    grad_query, grad_key, grad_value, grad_gate, grad_up, gain_sums = finish(from_heads, from_units)
    return (output[None], grad_input[None], gain_sums[:, 64], grad_query, grad_key, grad_value, grad_out,
            gain_sums[:, 65], grad_gate, grad_up, grad_down)


def solution(mesh):
    fits = dict(mesh.shape) == {"dp": 8, "blk": 4}
    return jax.shard_map(
        fast_shards if fits else shards,
        mesh=mesh,
        in_specs=(
            P("dp", "blk", None),
            P("dp", "blk"),
            P("dp", "blk"),
            P("dp", "blk", None),
            P(("dp", "blk")),
            P(("dp", "blk"), None),
            P(("dp", "blk"), None),
            P(("dp", "blk"), None),
            P(("dp", "blk"), None),
            P(("dp", "blk")),
            P(("dp", "blk"), None),
            P(("dp", "blk"), None),
            P(("dp", "blk"), None),
        ),
        out_specs=(
            P("dp", "blk", None),
            P("dp", "blk", None),
            P(("dp", "blk")),
            P(("dp", "blk"), None),
            P(("dp", "blk"), None),
            P(("dp", "blk"), None),
            P(("dp", "blk"), None),
            P(("dp", "blk")),
            P(("dp", "blk"), None),
            P(("dp", "blk"), None),
            P(("dp", "blk"), None),
        ),
        check_vma=False,
    )
```

```python
import math

import jax
import jax.numpy as jnp
from jax import lax
from jax.experimental import pallas as pl
from jax.experimental.pallas import tpu as pltpu
from jax.sharding import PartitionSpec as P

HEADS = 12
HEAD_DIM = 64


EPS = 1e-05
SCALE = 0.125
NEG = -1e30


def rope_tables(slot_positions, half_dim):
    inverse = jnp.exp(-math.log(10000.0) * jnp.arange(half_dim, dtype=jnp.float32) / half_dim)
    angles = slot_positions.astype(jnp.float32)[:, None] * inverse[None, :]
    return (jnp.cos(angles)[:, None, :], jnp.sin(angles)[:, None, :])


def rotate(tensor, cosine_table, sine_table):
    half_dim = tensor.shape[-1] // 2
    leading = tensor[..., :half_dim]
    trailing = tensor[..., half_dim:]
    return jnp.concatenate(
        [
            leading * cosine_table - trailing * sine_table,
            trailing * cosine_table + leading * sine_table,
        ],
        axis=-1,
    )


def matmul(left_matrix, right_matrix):
    return jnp.dot(left_matrix, right_matrix, preferred_element_type=jnp.float32)


def left_product(left_matrix, right_matrix):
    return lax.dot_general(
        left_matrix, right_matrix, (((0,), (0,)), ((), ())), preferred_element_type=jnp.float32
    )


def right_product(left_matrix, right_matrix):
    return lax.dot_general(
        left_matrix, right_matrix, (((1,), (1,)), ((), ())), preferred_element_type=jnp.float32
    )


def norm_back(grad_normed, values, inverse, gain):
    unit_normed = values * inverse
    scaled = grad_normed * gain
    grad_gain = jnp.sum(grad_normed * unit_normed, axis=0)
    grad_values = inverse * (
        scaled - unit_normed * jnp.mean(scaled * unit_normed, axis=-1, keepdims=True)
    )
    return (grad_values, grad_gain)


def score_mask(query_segments, query_index, key_segments, key_index):
    return (query_segments[:, None] == key_segments[None, :]) & (
        key_index[None, :] <= query_index[:, None]
    )


def block_grads(query_block, grad_block, lse_rows, delta_rows, allowed, key_block, value_block):
    scores = (
        jnp.einsum("qhd,khd->hqk", query_block, key_block, preferred_element_type=jnp.float32)
        * SCALE
    )
    probability = jnp.exp(jnp.where(allowed[None], scores - lse_rows.T[:, :, None], NEG))
    grad_value = jnp.einsum(
        "hqk,qhd->khd",
        probability.astype(jnp.bfloat16),
        grad_block,
        preferred_element_type=jnp.float32,
    )
    grad_probs = jnp.einsum(
        "qhd,khd->hqk", grad_block, value_block, preferred_element_type=jnp.float32
    )
    grad_scores = (probability * (grad_probs - delta_rows.T[:, :, None])).astype(jnp.bfloat16)
    grad_query = (
        jnp.einsum("hqk,khd->qhd", grad_scores, key_block, preferred_element_type=jnp.float32)
        * SCALE
    )
    grad_key = (
        jnp.einsum("hqk,qhd->khd", grad_scores, query_block, preferred_element_type=jnp.float32)
        * SCALE
    )
    return (grad_query, grad_key, grad_value)


def shards(
    tokens,
    segments,
    positions,
    cotangent,
    attn_gain,
    w_query,
    w_key,
    w_value,
    w_out,
    mlp_gain,
    w_gate,
    w_up,
    w_down,
):
    local_rows = tokens.shape[1]
    model_width = tokens.shape[2]
    blocks = lax.axis_size("blk")
    own_start = lax.axis_index("blk") * local_rows
    query_index = own_start + jnp.arange(local_rows, dtype=jnp.int32)
    own_segments = segments[0]
    cosine_table, sine_table = rope_tables(positions[0], HEAD_DIM // 2)
    x_float = tokens[0].astype(jnp.float32)
    gathered = (
        lax.all_gather(attn_gain, ("dp", "blk"), axis=0, tiled=True),
        lax.all_gather(w_query, ("dp", "blk"), axis=0, tiled=True),
        lax.all_gather(w_key, ("dp", "blk"), axis=0, tiled=True),
        lax.all_gather(w_value, ("dp", "blk"), axis=0, tiled=True),
        lax.all_gather(w_out, ("dp", "blk"), axis=0, tiled=True),
        lax.all_gather(mlp_gain, ("dp", "blk"), axis=0, tiled=True),
        lax.all_gather(w_gate, ("dp", "blk"), axis=0, tiled=True),
        lax.all_gather(w_up, ("dp", "blk"), axis=0, tiled=True),
        lax.all_gather(w_down, ("dp", "blk"), axis=0, tiled=True),
    )
    gain_one = gathered[0].astype(jnp.float32)
    gain_two = gathered[5].astype(jnp.float32)
    inverse_one = lax.rsqrt(jnp.mean(x_float * x_float, axis=-1, keepdims=True) + EPS)
    normed = (x_float * inverse_one * gain_one).astype(jnp.bfloat16)
    query_rot = rotate(
        matmul(normed, gathered[1]).reshape(local_rows, HEADS, HEAD_DIM), cosine_table, sine_table
    ).astype(jnp.bfloat16)
    key_rot = rotate(
        matmul(normed, gathered[2]).reshape(local_rows, HEADS, HEAD_DIM), cosine_table, sine_table
    ).astype(jnp.bfloat16)
    value_heads = (
        matmul(normed, gathered[3]).astype(jnp.bfloat16).reshape(local_rows, HEADS, HEAD_DIM)
    )
    key_flat = key_rot.reshape(local_rows, model_width)
    value_flat = value_heads.reshape(local_rows, model_width)
    start_state = (
        jnp.full((HEADS, local_rows), NEG, jnp.float32),
        jnp.zeros((HEADS, local_rows), jnp.float32),
        jnp.zeros((local_rows, HEADS, HEAD_DIM), jnp.float32),
    )
    key_piece = lax.all_gather(key_flat, "blk", axis=0, tiled=True)
    value_piece = lax.all_gather(value_flat, "blk", axis=0, tiled=True)
    seg_piece = lax.all_gather(own_segments, "blk", axis=0, tiled=True)
    piece_rows = key_piece.shape[0]
    needed = (jnp.int32(0) <= own_start + local_rows - 1) & (
        seg_piece[piece_rows - 1] >= own_segments[0]
    )

    def attend_sweep(current):

        def attend_visit(number, partial_value):
            running_max, running_sum, weighted = partial_value
            offset = number * local_rows
            key_block = lax.dynamic_slice_in_dim(key_piece, offset, local_rows, 0).reshape(
                local_rows, HEADS, HEAD_DIM
            )
            value_block = lax.dynamic_slice_in_dim(value_piece, offset, local_rows, 0).reshape(
                local_rows, HEADS, HEAD_DIM
            )
            seg_block = lax.dynamic_slice_in_dim(seg_piece, offset, local_rows, 0)
            key_index = offset + jnp.arange(local_rows, dtype=jnp.int32)
            allowed = score_mask(own_segments, query_index, seg_block, key_index)
            scores = (
                jnp.einsum("qhd,khd->hqk", query_rot, key_block, preferred_element_type=jnp.float32)
                * SCALE
            )
            scores = jnp.where(allowed[None], scores, NEG)
            new_max = jnp.maximum(running_max, jnp.max(scores, axis=-1))
            probability = jnp.where(allowed[None], jnp.exp(scores - new_max[:, :, None]), 0.0)
            factor = jnp.exp(running_max - new_max)
            running_sum = running_sum * factor + jnp.sum(probability, axis=-1)
            weighted = weighted * factor.T[:, :, None] + jnp.einsum(
                "hqk,khd->qhd",
                probability.astype(jnp.bfloat16),
                value_block,
                preferred_element_type=jnp.float32,
            )
            return (new_max, running_sum, weighted)

        return lax.fori_loop(0, piece_rows // local_rows, attend_visit, current)

    final_max, final_sum, final_weighted = lax.cond(
        needed, attend_sweep, lambda unchanged: unchanged, start_state
    )
    attn_heads = (final_weighted / final_sum.T[:, :, None]).astype(jnp.bfloat16)
    lse_rows = (final_max + jnp.log(final_sum)).T
    attn_flat = attn_heads.reshape(local_rows, model_width)
    resid = x_float + matmul(attn_flat, gathered[4])
    inverse_two = lax.rsqrt(jnp.mean(resid * resid, axis=-1, keepdims=True) + EPS)
    normed_two = (resid * inverse_two * gain_two).astype(jnp.bfloat16)
    gate = matmul(normed_two, gathered[6])
    up_values = matmul(normed_two, gathered[7])
    hidden = (jax.nn.silu(gate) * up_values).astype(jnp.bfloat16)
    output = (resid + matmul(hidden, gathered[8])).astype(jnp.bfloat16)
    later = (
        lax.all_gather(attn_gain, ("dp", "blk"), axis=0, tiled=True),
        lax.all_gather(w_query, ("dp", "blk"), axis=0, tiled=True),
        lax.all_gather(w_key, ("dp", "blk"), axis=0, tiled=True),
        lax.all_gather(w_value, ("dp", "blk"), axis=0, tiled=True),
        lax.all_gather(w_out, ("dp", "blk"), axis=0, tiled=True),
        lax.all_gather(mlp_gain, ("dp", "blk"), axis=0, tiled=True),
        lax.all_gather(w_gate, ("dp", "blk"), axis=0, tiled=True),
        lax.all_gather(w_up, ("dp", "blk"), axis=0, tiled=True),
        lax.all_gather(w_down, ("dp", "blk"), axis=0, tiled=True),
    )
    grad_res = cotangent[0].astype(jnp.float32)
    grad_mlp = grad_res.astype(jnp.bfloat16)
    grad_down = left_product(hidden, grad_mlp)
    grad_hidden = right_product(grad_mlp, later[8])
    sigmoid_gate = jax.nn.sigmoid(gate)
    grad_gate_low = (
        grad_hidden * up_values * sigmoid_gate * (1.0 + gate * (1.0 - sigmoid_gate))
    ).astype(jnp.bfloat16)
    grad_up_low = (grad_hidden * gate * sigmoid_gate).astype(jnp.bfloat16)
    grad_gate_w = left_product(normed_two, grad_gate_low)
    grad_up_w = left_product(normed_two, grad_up_low)
    grad_normed_two = right_product(grad_gate_low, later[6]) + right_product(grad_up_low, later[7])
    grad_resid_norm, grad_gain_two = norm_back(grad_normed_two, resid, inverse_two, gain_two)
    grad_mid = grad_res + grad_resid_norm
    grad_branch = grad_mid.astype(jnp.bfloat16)
    grad_out_w = left_product(attn_flat, grad_branch)
    grad_attn = (
        right_product(grad_branch, later[4])
        .astype(jnp.bfloat16)
        .reshape(local_rows, HEADS, HEAD_DIM)
    )
    delta_rows = jnp.sum(grad_attn.astype(jnp.float32) * attn_heads.astype(jnp.float32), axis=-1)
    pack_length = local_rows * blocks
    empty_back = (
        jnp.zeros((local_rows, HEADS, HEAD_DIM), jnp.float32),
        jnp.zeros((pack_length, 2 * model_width), jnp.float32),
    )
    back_key_piece = lax.all_gather(key_flat, "blk", axis=0, tiled=True)
    back_value_piece = lax.all_gather(value_flat, "blk", axis=0, tiled=True)
    back_seg_piece = lax.all_gather(own_segments, "blk", axis=0, tiled=True)
    back_piece_rows = back_key_piece.shape[0]
    needed = (jnp.int32(0) <= own_start + local_rows - 1) & (
        back_seg_piece[back_piece_rows - 1] >= own_segments[0]
    )

    def back_sweep(current):

        def back_visit(number, partial_value):
            grad_query_acc, grad_pairs = partial_value
            offset = number * local_rows
            key_block = lax.dynamic_slice_in_dim(back_key_piece, offset, local_rows, 0).reshape(
                local_rows, HEADS, HEAD_DIM
            )
            value_block = lax.dynamic_slice_in_dim(back_value_piece, offset, local_rows, 0).reshape(
                local_rows, HEADS, HEAD_DIM
            )
            seg_block = lax.dynamic_slice_in_dim(back_seg_piece, offset, local_rows, 0)
            key_index = offset + jnp.arange(local_rows, dtype=jnp.int32)
            allowed = score_mask(own_segments, query_index, seg_block, key_index)
            part_query, part_key, part_value = block_grads(
                query_rot, grad_attn, lse_rows, delta_rows, allowed, key_block, value_block
            )
            new_rows = jnp.concatenate(
                [
                    part_key.reshape(local_rows, model_width),
                    part_value.reshape(local_rows, model_width),
                ],
                axis=1,
            )
            existing = lax.dynamic_slice_in_dim(grad_pairs, offset, local_rows, 0)
            grad_pairs = lax.dynamic_update_slice_in_dim(grad_pairs, existing + new_rows, offset, 0)
            return (grad_query_acc + part_query, grad_pairs)

        return lax.fori_loop(0, back_piece_rows // local_rows, back_visit, current)

    grad_query_rot, grad_pairs_all = lax.cond(
        needed, back_sweep, lambda unchanged: unchanged, empty_back
    )
    own_pairs = lax.psum_scatter(
        grad_pairs_all.astype(jnp.bfloat16), "blk", scatter_dimension=0, tiled=True
    ).astype(jnp.float32)
    grad_key_rot = own_pairs[:, :model_width].reshape(local_rows, HEADS, HEAD_DIM)
    grad_value_heads = own_pairs[:, model_width:].reshape(local_rows, HEADS, HEAD_DIM)
    grad_query_low = (
        rotate(grad_query_rot, cosine_table, -sine_table)
        .reshape(local_rows, model_width)
        .astype(jnp.bfloat16)
    )
    grad_key_low = (
        rotate(grad_key_rot, cosine_table, -sine_table)
        .reshape(local_rows, model_width)
        .astype(jnp.bfloat16)
    )
    grad_value_low = grad_value_heads.reshape(local_rows, model_width).astype(jnp.bfloat16)
    grad_query_w = left_product(normed, grad_query_low)
    grad_key_w = left_product(normed, grad_key_low)
    grad_value_w = left_product(normed, grad_value_low)
    grad_normed = (
        right_product(grad_query_low, later[1])
        + right_product(grad_key_low, later[2])
        + right_product(grad_value_low, later[3])
    )
    grad_x_norm, grad_gain_one = norm_back(grad_normed, x_float, inverse_one, gain_one)
    grad_input = (grad_mid + grad_x_norm).astype(jnp.bfloat16)
    summed = (
        lax.psum_scatter(grad_gain_one, ("dp", "blk"), scatter_dimension=0, tiled=True),
        lax.psum_scatter(grad_query_w, ("dp", "blk"), scatter_dimension=0, tiled=True),
        lax.psum_scatter(grad_key_w, ("dp", "blk"), scatter_dimension=0, tiled=True),
        lax.psum_scatter(grad_value_w, ("dp", "blk"), scatter_dimension=0, tiled=True),
        lax.psum_scatter(grad_out_w, ("dp", "blk"), scatter_dimension=0, tiled=True),
        lax.psum_scatter(grad_gain_two, ("dp", "blk"), scatter_dimension=0, tiled=True),
        lax.psum_scatter(grad_gate_w, ("dp", "blk"), scatter_dimension=0, tiled=True),
        lax.psum_scatter(grad_up_w, ("dp", "blk"), scatter_dimension=0, tiled=True),
        lax.psum_scatter(grad_down, ("dp", "blk"), scatter_dimension=0, tiled=True),
    )
    return (
        output.reshape(1, local_rows, model_width),
        grad_input.reshape(1, local_rows, model_width),
        summed[0],
        summed[1],
        summed[2],
        summed[3],
        summed[4],
        summed[5],
        summed[6],
        summed[7],
        summed[8],
    )


BF = jnp.bfloat16
F32 = jnp.float32
VMEM = pltpu.VMEM
LANES = 256


def ids():
    dp, blk = lax.axis_index("dp"), lax.axis_index("blk")
    return dp // 2, dp % 2, blk // 2, blk % 2, blk


def flip(bit, other):
    total = 0
    weight = 1
    while weight <= 2:
        own = (bit // weight) % 2
        total = total + weight * ((1 - own) if (other // weight) % 2 else own)
        weight *= 2
    return total


def exclusive(a, b):
    low, high = (a + b) % 2, (a // 2 + b // 2) % 2
    return low + 2 * high


def aligned(value, multiple):
    return pl.multiple_of(value, multiple)


def dot(a, b, ca=1, cb=0):
    return lax.dot_general(a, b, (((ca,), (cb,)), ((), ())), preferred_element_type=F32)


HBM = "hbm"


def call(kernel, outs, ins, anys=(), scratch=(), flops=0, nbytes=0, grant=24):
    def place(far):
        return pl.BlockSpec(memory_space=pltpu.MemorySpace.HBM if far else VMEM)

    return pl.pallas_call(
        kernel,
        out_shape=[jax.ShapeDtypeStruct(out[0], out[1]) for out in outs],
        in_specs=[place(i in anys) for i in range(len(ins))],
        out_specs=[place(len(out) > 2) for out in outs],
        scratch_shapes=list(scratch),
        compiler_params=pltpu.CompilerParams(vmem_limit_bytes=grant * 1024 * 1024),
        cost_estimate=pl.CostEstimate(flops=flops, bytes_accessed=nbytes, transcendentals=0),
    )(*ins)


def pair(low, first, second):
    (a, i), (b, j) = first, second
    left = a[:, 128 * (i // 2) : 128 * (i // 2) + 128]
    right = b[:, 128 * (j // 2) : 128 * (j // 2) + 128]
    left = pltpu.roll(left, 64, 1) if i % 2 else left
    right = right if j % 2 else pltpu.roll(right, 64, 1)
    return jnp.where(low, left, right)


def pairs(low, blocks):
    return jnp.concatenate([pair(low, blocks[i], blocks[i + 1]) for i in range(0, len(blocks), 2)], axis=1)


def prepare_kernel(gains, place, wq_h, wk_h, wv_h, wg_h, wu_h, x_h, r0_o, r1_o, r2_o, r3_o, x_o,
                   wq, wk, wv, wg, wu, order, sems):
    z, x, y, c, b = ids()
    far, near = (wq_h, wk_h, wv_h, wg_h, wu_h), (wq, wk, wv, wg, wu)
    copies = [pltpu.make_async_copy(a, d, sems.at[i]) for i, (a, d) in enumerate(zip(far, near))]
    copies.append(pltpu.make_async_copy(x_h, x_o.at[pl.ds(0, 256)], sems.at[5]))
    for copy in copies:
        copy.start()
    for copy in copies[:5]:
        copy.wait()
    low = lax.broadcasted_iota(jnp.int32, (wq.shape[0], 128), 1) < 64
    q, k, v, g, gate, up = (ref[...].astype(F32) for ref in (wq, wk, wv, gains, wg, wu))
    at = jnp.broadcast_to(place[...], (16, 256)).astype(F32)
    tens = jnp.floor(at * (1.0 / 32))
    x_o[256:272, :] = jnp.concatenate([tens, at - 32.0 * tens, jnp.zeros_like(at)], axis=1).astype(BF)
    for j in range(4):
        blocks = [(w, 3 * j + t) for w in (q, k, v) for t in range(3)] + [(g, 1)]
        order[flip(b, j)] = pairs(low, blocks).astype(BF)
        wide = pairs(low, [(w, 4 * i + j) for w in (gate, up) for i in range(8)])
        rest = jnp.concatenate([wide[8 * t : 8 * t + 8, 768:1024] for t in range(3)], axis=1)
        x_o[272 + 32 * j : 304 + 32 * j, :] = jnp.concatenate([wide[:, 0:768], rest], axis=0).astype(BF)
    for k, out in enumerate((r0_o, r1_o, r2_o, r3_o)):
        out[...] = order[k]
    copies[5].wait()


def prepare(tokens, place, wq, wk, wv, gains, wg, wu):
    outs = [((24, 640), BF)] * 4 + [((400, 768), BF)]
    scratch = [*[VMEM((24, 768), BF)] * 3, *[VMEM((24, 2048), BF)] * 2, VMEM((4, 24, 640), BF),
               pltpu.SemaphoreType.DMA((7,))]
    return call(prepare_kernel, outs, [gains, place, wq, wk, wv, wg, wu, tokens], anys=range(2, 8), scratch=scratch,
                flops=1_000_000, nbytes=1_000_000, grant=60)


def columns_kernel(r0, r1, r2, r3, out, rows):
    z, x, y, c, b = ids()
    for k, piece in enumerate((r0, r1, r2, r3)):
        rows[pl.ds(aligned(flip(b, k) * 24, 24), 24), :] = piece[...].astype(F32)
    out[...] = rows[...].astype(BF)


def columns(pieces):
    (out,) = call(columns_kernel, [((96, 640), BF)], pieces, scratch=[VMEM((96, 640), F32)], flops=1_000_000, nbytes=300_000)
    return out


def units_kernel(x0, x1, x2, x3, out, rows):
    z, x, y, c, b = ids()
    for k, piece in enumerate((x0, x1, x2, x3)):
        part = piece[pl.ds(aligned(272 + 32 * b, 16), 32), :].astype(F32)
        rest = jnp.concatenate([part[24:32, 256 * t : 256 * t + 256] for t in range(3)], axis=0)
        rows[pl.ds(aligned(flip(b, k) * 24, 24), 24), :] = jnp.concatenate([part[0:24], rest], axis=1)
    out[...] = rows[...].astype(BF)


def units(xs):
    (out,) = call(units_kernel, [((96, 1024), BF)], xs, scratch=[VMEM((96, 1024), F32)], flops=1_000_000, nbytes=3_000_000)
    return out


def finish_kernel(h0, h1, h2, h3, u0, u1, u2, u3, q_o, k_o, v_o, gate_o, up_o, gains_o, heads, units):
    z, x, y, c, b = ids()
    for k in range(4):
        heads[k] = (h0, h1, h2, h3)[k][...]
        units[k] = (u0, u1, u2, u3)[k][...]
    low = lax.broadcasted_iota(jnp.int32, (heads.shape[1], 128), 1) < 64
    parts = [heads[flip(b, j)].astype(F32) for j in range(4)]
    for t, out in enumerate((q_o, k_o, v_o)):
        out[...] = pairs(low, [(parts[m // 3], 3 * t + m % 3) for m in range(12)])
    gains_o[...] = parts[0][:, 512:640] + parts[1][:, 512:640] + parts[2][:, 512:640] + parts[3][:, 512:640]
    parts = [units[flip(b, j)].astype(F32) for j in range(4)]
    for t, out in enumerate((gate_o, up_o)):
        out[...] = pairs(low, [(parts[m % 4], 8 * t + m // 4) for m in range(32)])


def finish(heads, units):
    outs = [((24, 768), F32)] * 3 + [((24, 2048), F32)] * 2 + [((24, 128), F32)]
    return call(finish_kernel, outs, [*heads, *units], scratch=[VMEM((4, 24, 640), BF), VMEM((4, 24, 1024), BF)],
                flops=1_000_000, nbytes=2_000_000)


def tables_kernel(x0, x1, x2, x3, cos_o, sin_o, start_o, rows_o, marks, cos, sin, start, rows, sems, out_sems):
    z, x, y, c, b = ids()
    copies = [
        pltpu.make_async_copy(piece.at[pl.ds(256, 16)], marks.at[k], sems.at[k])
        for k, piece in enumerate((x0, x1, x2, x3))
    ]
    for copy in copies:
        copy.start()
    for copy in copies:
        copy.wait()
    lane = lax.broadcasted_iota(jnp.int32, (256, 128), 1)
    row = lax.broadcasted_iota(jnp.int32, (256, 128), 0)
    inverse = jnp.exp((lane % 32).astype(F32) * (-math.log(10000.0) / 32))
    sign = jnp.where(lane % 64 < 32, -1.0, 1.0)
    for k in range(4):
        own = marks[k].astype(F32)
        place = (32.0 * own[:, 0:256] + own[:, 256:512])[0:1]
        slot = lax.broadcasted_iota(jnp.int32, (8, 256), 1) + 256 * flip(b, k)
        rows[k] = slot.astype(F32) - jnp.broadcast_to(place, (8, 256))
        place = jnp.broadcast_to(place, (128, 256)).T
        angles = place * inverse
        cos[k] = jnp.cos(angles)
        sin[k] = jnp.sin(angles) * sign
        start[k] = 256 * flip(b, k) + row - place.astype(jnp.int32)
    leaving = [
        pltpu.make_async_copy(ref, out, out_sems.at[i])
        for i, (ref, out) in enumerate(((cos, cos_o), (sin, sin_o), (start, start_o), (rows, rows_o)))
    ]
    for copy in leaving:
        copy.start()
    for copy in leaving:
        copy.wait()


def tables(xs):
    outs = [((4, 256, 128), F32, HBM)] * 2 + [((4, 256, 128), jnp.int32, HBM), ((4, 8, 256), F32, HBM)]
    scratch = [
        VMEM((4, 16, 768), BF), *[VMEM((4, 256, 128), F32)] * 2, VMEM((4, 256, 128), jnp.int32),
        VMEM((4, 8, 256), F32), pltpu.SemaphoreType.DMA((4,)), pltpu.SemaphoreType.DMA((4,)),
    ]
    return call(tables_kernel, outs, xs, anys=range(4), scratch=scratch, flops=10_000_000, nbytes=3_000_000)


def half_swap(tile, lane):
    return jnp.where(lane % 64 < 32, pltpu.roll(tile, 96, 1), pltpu.roll(tile, 32, 1))


def attend_kernel(x0, x1, x2, x3, wa, wb, cos_h, sin_h, start_h,
                  q_o, k_o, v_o, n_o, w_o, attn_o, lse_o, gains_o, a0_o, a1_o, a2_o, a3_o,
                  xs, w, q, k, v, n, attn, lse, cos, sin, start, sems, out_sems):
    z, x, y, c, b = ids()
    copies = []
    for xr, piece in enumerate((wa, wb)):
        for zr in range(4):
            dp = 2 * flip(z, zr) + flip(x, xr)
            copies.append(pltpu.make_async_copy(
                piece.at[zr], w.at[pl.ds(aligned(dp * 96, 96), 96)], sems.at[4 * xr + zr]))
    for kk, piece in enumerate((x0, x1, x2, x3)):
        copies.append(pltpu.make_async_copy(piece.at[pl.ds(0, 272)], xs.at[kk], sems.at[8 + kk]))
    for at, (ref, near) in enumerate(((cos_h, cos), (sin_h, sin), (start_h, start))):
        copies.append(pltpu.make_async_copy(ref, near, sems.at[12 + at]))
    for copy in copies:
        copy.start()
    for copy in copies[:8] + copies[12:14]:
        copy.wait()
    leaving = [pltpu.make_async_copy(w, w_o, out_sems.at[0])]
    leaving[0].start()
    last = w[:, 512:640].astype(F32).T
    gains = last[64:72, :]
    gains_o[...] = gains
    gain = gains[0:1, :]
    lane = lax.broadcasted_iota(jnp.int32, (256, 128), 1)
    low = lane < 64
    for kk in range(4):
        rows = pl.ds(aligned(flip(b, kk) * 256, 256), 256)
        copies[8 + kk].wait()
        values = xs[kk, 0:256, :].astype(F32)
        inverse = lax.rsqrt(jnp.mean(values * values, axis=-1, keepdims=True) + EPS)
        normed = (values * inverse * gain).astype(BF)
        n[rows, :] = normed
        qkv = dot(normed, w[...])
        cosine, sine = cos[kk], sin[kk]
        tiles = []
        for t in range(3):
            tile = qkv[:, 128 * t : 128 * t + 128]
            tiles.append(tile * cosine + half_swap(tile, lane) * sine)
        r1, r2 = pltpu.roll(tiles[1], 64, 1), pltpu.roll(tiles[2], 64, 1)
        zero = jnp.zeros_like(r1)
        q[rows, 0:128] = tiles[0].astype(BF)
        q[rows, 128:256] = jnp.where(low, tiles[1], zero).astype(BF)
        k[rows, 0:128] = jnp.where(low, r1, r2).astype(BF)
        k[rows, 128:256] = jnp.where(low, r2, zero).astype(BF)
        v[rows, 0:128] = qkv[:, 384:512].astype(BF)
        v[rows, 128:256] = jnp.where(low, qkv[:, 512:640], zero).astype(BF)
    for at, (ref, out) in enumerate(((n, n_o), (q, q_o), (k, k_o), (v, v_o))):
        leaving.append(pltpu.make_async_copy(ref, out, out_sems.at[3 + at]))
        leaving[-1].start()
    copies[14].wait()
    head = lax.broadcasted_iota(jnp.int32, (256, LANES), 1) // 64
    for i in range(4):
        width = 256 * (i + 1)
        query = q[256 * i : 256 * i + 256, :]
        begin = start[flip(b, i)][:, 0:1]
        column = lax.broadcasted_iota(jnp.int32, (256, width), 1)
        row = lax.broadcasted_iota(jnp.int32, (256, width), 0) + 256 * i
        allowed = (column <= row) & (column >= begin)
        total = jnp.zeros((256, LANES), F32)
        stats = jnp.zeros((256, 128), F32)
        for h in range(3):
            mine = jnp.where(head == h, query, jnp.zeros_like(query))
            scores = dot(mine, k[0:width, :], 1, 1) * SCALE
            scores = jnp.where(allowed, scores, NEG)
            top = jnp.max(scores, axis=-1, keepdims=True)
            weight = jnp.exp(scores - top)
            norm = jnp.sum(weight, axis=-1, keepdims=True)
            mixed = dot(weight.astype(BF), v[0:width, :]) / norm
            total = jnp.where(head == h, mixed, total)
            stats = jnp.where(lane == h, top + jnp.log(norm), stats)
        attn[256 * i : 256 * i + 256, :] = total.astype(BF)
        lse[:, 256 * i : 256 * i + 256] = stats.T[0:8]
    for at, (ref, out) in enumerate(((attn, attn_o), (lse, lse_o))):
        leaving.append(pltpu.make_async_copy(ref, out, out_sems.at[1 + at]))
        leaving[-1].start()
    for kk, out in enumerate((a0_o, a1_o, a2_o, a3_o)):
        out[...] = attn[pl.ds(aligned(flip(b, kk) * 256, 256), 256), :]
    for copy in leaving:
        copy.wait()


def attend(xs, wa, wb, cos, sin, start):
    outs = [
        *[((1024, LANES), BF, HBM)] * 3, ((1024, 768), BF, HBM), ((768, 640), BF, HBM), ((1024, LANES), BF, HBM),
        ((8, 1024), F32, HBM), ((8, 768), F32), *[((256, LANES), BF)] * 4,
    ]
    return call(
        attend_kernel, outs, [*xs, wa, wb, cos, sin, start], anys=range(9), grant=60,
        scratch=[
            VMEM((4, 272, 768), BF), VMEM((768, 640), BF), *[VMEM((1024, LANES), BF)] * 3, VMEM((1024, 768), BF),
            VMEM((1024, LANES), BF), VMEM((8, 1024), F32), *[VMEM((4, 256, 128), F32)] * 2, VMEM((4, 256, 128), jnp.int32),
            pltpu.SemaphoreType.DMA((15,)), pltpu.SemaphoreType.DMA((7,)),
        ],
        flops=4_000_000_000, nbytes=8_000_000,
    )


def out_kernel(a0, a1, a2, a3, x0, gains, own, other, resid_o, n_o, wo_o, stack_o, wide):
    z, x, y, c, b = ids()
    for xy in range(4):
        for zr in range(4):
            chip = 8 * flip(z, zr) + 4 * flip(x, xy // 2) + 2 * flip(y, xy % 2)
            for core, pieces in enumerate((own, other)):
                at = aligned((chip + flip(c, core)) * 24, 24)
                wide[pl.ds(at, 24), :] = pieces[xy, zr].astype(F32)
    wo_o[...] = wide[...].astype(BF)
    total = x0[0:256, :].astype(F32)
    for k, piece in enumerate((a0, a1, a2, a3)):
        rows = pl.ds(aligned(flip(b, k) * 192, 192), 192)
        stack_o[k] = piece[...]
        total += dot(piece[:, 0:192], wo_o[rows, :])
    resid_o[...] = total
    inverse = lax.rsqrt(jnp.mean(total * total, axis=-1, keepdims=True) + EPS)
    n_o[...] = (total * inverse * gains[1:2, :]).astype(BF)


def project(a, x0, gains, own, other):
    outs = [((256, 768), F32), ((256, 768), BF), ((768, 768), BF), ((4, 256, LANES), BF)]
    return call(out_kernel, outs, [*a, x0, gains, own, other], scratch=[VMEM((768, 768), F32)],
                flops=400_000_000, nbytes=4_000_000)


def hidden_kernel(n0, n1, n2, n3, ct0, ct1, ct2, ct3, gu_near, gu_far, d_near, d_far,
                  n_o, ct_o, hid_o, dg_o, du_o, wgu_o, wd_o, sems):
    z, x, y, c, b = ids()
    copies = []
    for xr, (gu, d) in enumerate(((gu_near, d_near), (gu_far, d_far))):
        for zr in range(4):
            dp = 2 * flip(z, zr) + flip(x, xr)
            at = 4 * xr + zr
            copies.append(pltpu.make_async_copy(
                gu.at[zr], wgu_o.at[pl.ds(aligned(dp * 96, 96), 96)], sems.at[0, at]))
            copies.append(pltpu.make_async_copy(
                d.at[zr, pl.ds(0, 64)], wd_o.at[pl.ds(aligned(dp * 64, 64), 64)], sems.at[1, at]))
    for copy in copies:
        copy.start()
    for k in range(4):
        n_o[256 * k : 256 * k + 256, :] = (n0, n1, n2, n3)[k][...]
        ct_o[256 * k : 256 * k + 256, :] = (ct0, ct1, ct2, ct3)[k][...]
    for copy in copies:
        copy.wait()
    for k in range(4):
        rows = slice(256 * k, 256 * k + 256)
        normed, cot = n_o[rows, :], ct_o[rows, :]
        for j in range(2):
            cols = slice(256 * j, 256 * j + 256)
            gate = dot(normed, wgu_o[:, 256 * j : 256 * j + 256])
            up = dot(normed, wgu_o[:, 512 + 256 * j : 768 + 256 * j])
            back = dot(cot, wd_o[cols, :], 1, 1)
            sig = 1.0 / (1.0 + jnp.exp(-gate))
            silu = gate * sig
            hid_o[rows, cols] = (silu * up).astype(BF)
            dg_o[rows, cols] = (back * up * sig * (1.0 + gate * (1.0 - sig))).astype(BF)
            du_o[rows, cols] = (back * silu).astype(BF)


def hidden_and_back(n, ct, pieces):
    outs = [((1024, 768), BF)] * 2 + [((1024, 512), BF)] * 3 + [((768, 1024), BF), ((512, 768), BF)]
    return call(
        hidden_kernel, outs, [*n, *ct, *pieces], anys=range(8, 12),
        scratch=[pltpu.SemaphoreType.DMA((3, 8))], flops=2_500_000_000, nbytes=8_000_000,
    )


def normed_back_kernel(dg, du, wgu, own_o, far_o, send_o):
    for k in range(4):
        rows = slice(256 * k, 256 * k + 256)
        grad = dot(dg[rows, :], wgu[:, 0:512], 1, 1) + dot(du[rows, :], wgu[:, 512:1024], 1, 1)
        if k == 0:
            own_o[...] = grad
        elif k == 2:
            far_o[...] = grad
        else:
            send_o[k // 2] = grad.astype(BF)


def normed_back(dg, du, wgu):
    outs = [((256, 768), F32)] * 2 + [((2, 256, 768), BF)]
    return call(normed_back_kernel, outs, [dg, du, wgu], flops=1_600_000_000, nbytes=6_000_000)


def store_by_x(grad, rows, cols, keep_o, send_o, z, x):
    for zp in range(4):
        at = 2 * rows * zp
        low, high = grad[at : at + rows], grad[at + rows : at + 2 * rows]
        keep_o[flip(z, zp), :, cols] = jnp.where(x == 0, low, high).astype(BF)
        send_o[flip(z, zp), :, cols] = jnp.where(x == 0, high, low).astype(BF)


def ff_grads_kernel(n, ct, hid, dg, du, gu_keep_o, gu_send_o, d_keep_o, d_send_o):
    z, x, y, c, b = ids()
    normed = n[...].T
    for j in range(4):
        cols = slice(256 * j, 256 * j + 256)
        part = (dg, du)[j // 2][:, 256 * (j % 2) : 256 * (j % 2) + 256]
        store_by_x(dot(normed, part), 96, cols, gu_keep_o, gu_send_o, z, x)
    hidden = hid[...].T
    for j in range(3):
        cols = slice(256 * j, 256 * j + 256)
        store_by_x(dot(hidden, ct[:, cols]), 64, cols, d_keep_o, d_send_o, z, x)


def ff_grads(n, ct, hid, dg, du):
    outs = [((4, 96, 1024), BF)] * 2 + [((4, 64, 768), BF)] * 2
    return call(ff_grads_kernel, outs, [n, ct, hid, dg, du], flops=2_400_000_000, nbytes=10_000_000)


def mid_kernel(gn_own, gn_in, resid, ct0, gains, wo, out_own, out_far, out_in, here_o, there_o, mid_o, branch_o, g0_o, g1_o, g2_o, g3_o, gain_o):
    z, x, y, c, b = ids()
    here_o[...] = out_own[...] + out_in[0].astype(F32)
    there_o[...] = (out_far[...] + out_in[1].astype(F32)).astype(BF)
    grad = gn_own[...] + gn_in[...].astype(F32)
    values = resid[...]
    inverse = lax.rsqrt(jnp.mean(values * values, axis=-1, keepdims=True) + EPS)
    unit = values * inverse
    scaled = grad * gains[1:2, :]
    gain_o[...] = jnp.broadcast_to(jnp.sum(grad * unit, axis=0, keepdims=True), gain_o.shape)
    mid = ct0[...].astype(F32) + inverse * (
        scaled - unit * jnp.mean(scaled * unit, axis=-1, keepdims=True)
    )
    mid_o[...] = mid
    branch = mid.astype(BF)
    branch_o[...] = branch
    pad = jnp.zeros((256, LANES - 192), BF)
    for k in range(4):
        rows = pl.ds(aligned(flip(b, k) * 192, 192), 192)
        part = dot(branch, wo[rows, :], 1, 1)
        (g0_o, g1_o, g2_o, g3_o)[k][...] = jnp.concatenate([part.astype(BF), pad], axis=1)


def mid_back(gn_own, gn_in, resid, ct0, gains, wo, out):
    outs = [((256, 768), F32), ((256, 768), BF), ((256, 768), F32), ((256, 768), BF), *[((256, LANES), BF)] * 4, ((8, 768), F32)]
    return call(mid_kernel, outs, [gn_own, gn_in, resid, ct0, gains, wo, *out], flops=400_000_000, nbytes=5_000_000)


def out_grads_kernel(stack, branch, keep_o, send_o, wide):
    z, x, y, c, b = ids()
    for k in range(4):
        part = dot(stack[k].T, branch[...])[0:192]
        wide[pl.ds(aligned(exclusive(flip(b, k), z) * 192, 192), 192), :] = part
    for cr, out in enumerate((keep_o, send_o)):
        for yr in range(2):
            for xr in range(2):
                for zr in range(4):
                    at = 4 * (flip(x, xr) % 2) + 2 * (flip(y, yr) % 2) + flip(c, cr) % 2 + 8 * zr
                    out[xr, yr, zr] = wide[pl.ds(aligned(at * 24, 24), 24), :].astype(BF)


def out_grads(stack, branch):
    outs = [((2, 2, 4, 24, 768), BF)] * 2
    return call(out_grads_kernel, outs, [stack, branch], scratch=[VMEM((768, 768), F32)],
                flops=400_000_000, nbytes=3_000_000)


def down_kernel(hid, wd, resid, own_o, far_o, send_o):
    for k in range(4):
        part = dot(hid[256 * k : 256 * k + 256, :], wd[...])
        if k == 0:
            own_o[...] = resid[...] + part
        elif k == 2:
            far_o[...] = part
        else:
            send_o[k // 2] = part.astype(BF)


def down(hid, wd, resid):
    outs = [((256, 768), F32)] * 2 + [((2, 256, 768), BF)]
    return call(down_kernel, outs, [hid, wd, resid], flops=800_000_000, nbytes=5_000_000)


def attend_back_kernel(q_h, k_h, v_h, n_h, w_h, attn_h, lse_h, cos_h, sin_h, start_h, x0, x1, x2, x3, g0, g1, g2, g3, gain2_h,
                       keep_h, send_h, gk0_h, gk1_h, gs_h,
                       q, k, v, n, w, attn, lse, cos, sin, start, xs, do, dq, dk, dv, grads, wide, gain2,
                       keep_o, send_o, gk0_o, gk1_o, gs_o, sems, out_sems):
    z, x, y, c, b = ids()
    far = (q_h, k_h, v_h, attn_h, lse_h, start_h, cos_h, sin_h, n_h, w_h)
    near = (q, k, v, attn, lse, start, cos, sin, n, w)
    copies = [pltpu.make_async_copy(a, d, sems.at[i]) for i, (a, d) in enumerate(zip(far, near))]
    copies += [
        pltpu.make_async_copy(a.at[pl.ds(0, 272)], xs.at[i], sems.at[10 + i]) for i, a in enumerate((x0, x1, x2, x3))
    ]
    copies.append(pltpu.make_async_copy(gain2_h, gain2, sems.at[14]))
    first = copies[:6] + [
        pltpu.make_async_copy(a, do.at[pl.ds(aligned(flip(b, i) * 256, 256), 256)], sems.at[15 + i])
        for i, a in enumerate((g0, g1, g2, g3))
    ]
    for copy in first + copies[6:]:
        copy.start()
    dk[...] = jnp.zeros_like(dk)
    dv[...] = jnp.zeros_like(dv)
    for copy in first:
        copy.wait()
    head = lax.broadcasted_iota(jnp.int32, (256, LANES), 1) // 64
    lane = lax.broadcasted_iota(jnp.int32, (256, 128), 1)
    for i in range(4):
        width = 256 * (i + 1)
        rows = slice(256 * i, 256 * i + 256)
        query, out_grad = q[rows, :], do[rows, :]
        product = out_grad.astype(F32) * attn[rows, :].astype(F32)
        delta = jnp.zeros((256, 128), F32)
        for h in range(3):
            delta = jnp.where(
                lane == h, jnp.sum(jnp.where(head == h, product, 0.0), axis=-1, keepdims=True), delta)
        delta = delta.T
        begin = start[flip(b, i)][0:1, :]
        key = lax.broadcasted_iota(jnp.int32, (width, 256), 0)
        slot = lax.broadcasted_iota(jnp.int32, (width, 256), 1) + 256 * i
        allowed = (key <= slot) & (key.astype(F32) >= begin)
        probs, dscores = [], []
        mine = [jnp.where(head == h, query, jnp.zeros_like(query)) for h in range(3)]
        ours = [jnp.where(head == h, out_grad, jnp.zeros_like(out_grad)) for h in range(3)]
        for h in range(3):
            scores = dot(k[0:width, :], mine[h], 1, 1) * SCALE
            prob = jnp.exp(jnp.where(allowed, scores - lse[h : h + 1, rows], NEG))
            dprob = dot(v[0:width, :], ours[h], 1, 1)
            probs.append(prob.astype(BF))
            dscores.append((prob * (dprob - delta[h : h + 1, :])).astype(BF))
        dv[0:width, :] += dot(jnp.concatenate(probs, axis=1), jnp.concatenate(ours, axis=0))
        dk[0:width, :] += dot(jnp.concatenate(dscores, axis=1), jnp.concatenate(mine, axis=0))
        total = jnp.zeros((256, LANES), F32)
        for h in range(3):
            total = jnp.where(head == h, dot(dscores[h], k[0:width, :], 0, 0), total)
        dq[rows, :] = total
    for copy in copies[6:]:
        copy.wait()
    low = lane < 64
    zero = jnp.zeros((256, 128), F32)
    for i in range(4):
        rows = slice(256 * i, 256 * i + 256)
        cosine, sine = cos[flip(b, i)] * SCALE, sin[flip(b, i)] * SCALE
        turned = []
        for ref in (dq, dk):
            for t in range(2):
                tile = ref[rows, 128 * t : 128 * t + 128]
                turned.append(tile * cosine - half_swap(tile, lane) * sine)
        k0, k1 = pltpu.roll(turned[2], 64, 1), pltpu.roll(turned[3], 64, 1)
        grads[rows, 0:128] = turned[0].astype(BF)
        grads[rows, 128:256] = jnp.where(low, turned[1], k0).astype(BF)
        grads[rows, 256:384] = jnp.where(low, k0, k1).astype(BF)
        grads[rows, 384:512] = dv[rows, 0:128].astype(BF)
        grads[rows, 512:640] = jnp.where(low, dv[rows, 128:256], zero).astype(BF)
    leaving = []

    def leave(ref, out):
        leaving.append(pltpu.make_async_copy(ref, out, out_sems.at[len(leaving)]))
        leaving[-1].start()

    gain_sum = jnp.zeros((1, 768), F32)
    for kk in range(4):
        rows = pl.ds(aligned(flip(b, kk) * 256, 256), 256)
        grad = dot(grads[rows, :], w[...], 1, 1)
        values = xs[kk, 0:256, :].astype(F32)
        inverse = lax.rsqrt(jnp.mean(values * values, axis=-1, keepdims=True) + EPS)
        gain_sum += jnp.sum(grad * (values * inverse), axis=0, keepdims=True)
        if kk % 2:
            gs_o[kk // 2] = grad.astype(BF)
        else:
            (gk0_o, gk1_o)[kk // 2][...] = grad.astype(BF)
    for ref, out in ((gs_o, gs_h), (gk0_o, gk0_h), (gk1_o, gk1_h)):
        leave(ref, out)
    row_at = lax.broadcasted_iota(jnp.int32, (128, 768), 0)
    gain_rows = jnp.where(row_at == 64, gain_sum, jnp.where(row_at == 65, gain2[0:1, :], 0.0))
    gain_columns = gain_rows.T
    normed = n[...].T
    for j in range(5):
        cols = slice(128 * j, 128 * j + 128)
        part = dot(normed, grads[:, cols])
        if j == 4:
            part = part + gain_columns
        wide[:, cols] = part
    for xr, (ref, out) in ((1, (send_o, send_h)), (0, (keep_o, keep_h))):
        for zr in range(4):
            dp = 2 * flip(z, zr) + flip(x, xr)
            ref[zr] = wide[pl.ds(aligned(dp * 96, 96), 96), :].astype(BF)
        leave(ref, out)
    for copy in leaving:
        copy.wait()


def attend_back(saved, tabs, xs, g, gain2):
    outs = [((4, 96, 640), BF, HBM)] * 2 + [((256, 768), BF, HBM)] * 2 + [((2, 256, 768), BF, HBM)]
    return call(
        attend_back_kernel, outs, [*saved, *tabs, *xs, *g, gain2], anys=range(19), grant=60,
        scratch=[
            *[VMEM((1024, LANES), BF)] * 3, VMEM((1024, 768), BF), VMEM((768, 640), BF), VMEM((1024, LANES), BF),
            VMEM((8, 1024), F32), *[VMEM((4, 256, 128), F32)] * 2, VMEM((4, 8, 256), F32),
            VMEM((4, 272, 768), BF), VMEM((1024, LANES), BF), *[VMEM((1024, LANES), F32)] * 3,
            VMEM((1024, 640), BF), VMEM((768, 640), F32), VMEM((8, 768), F32),
            *[VMEM(out[0], out[1]) for out in outs], pltpu.SemaphoreType.DMA((19,)), pltpu.SemaphoreType.DMA((5,)),
        ],
        flops=10_000_000_000, nbytes=12_000_000,
    )


def last_kernel(kept, arrived, mid, x0, gains, out):
    grad = kept[...].astype(F32) + arrived[...].astype(F32)
    values = x0[0:256, :].astype(F32)
    inverse = lax.rsqrt(jnp.mean(values * values, axis=-1, keepdims=True) + EPS)
    unit = values * inverse
    scaled = grad * gains[0:1, :]
    out[...] = (
        mid[...] + inverse * (scaled - unit * jnp.mean(scaled * unit, axis=-1, keepdims=True))
    ).astype(BF)


def swap_z(v, k):
    return lax.ppermute(v, "dp", [(i, i ^ (2 * k)) for i in range(8)])


def swap_x(v):
    return lax.ppermute(v, "dp", [(i, i ^ 1) for i in range(8)])


def swap_b(v, k):
    return lax.ppermute(v, "blk", [(i, i ^ k) for i in range(4)])


def swap_core(v):
    return swap_b(v, 1)


def swap_y(v):
    return swap_b(v, 2)


def after(value, *tokens):
    return lax.optimization_barrier((value, tokens))[0]


def stack_z(v):
    return jnp.stack([v] + [swap_z(v, k) for k in (1, 2, 3)])


def by_index(four, bits):
    one, two = bits % 2 == 1, bits // 2 == 1
    a, b, c, d = four
    a, b, c, d = jnp.where(one, b, a), jnp.where(one, a, b), jnp.where(one, d, c), jnp.where(one, c, d)
    return [jnp.where(two, c, a), jnp.where(two, d, b), jnp.where(two, a, c), jnp.where(two, b, d)]


def sum_z(v):
    terms = [v[0]] + [swap_z(v[k], k) for k in (1, 2, 3)]
    return sum(term.astype(F32) for term in terms)


def halve_z(v, far):
    first = [added(v[k], far[k]) for k in range(2)]
    return first[0].astype(F32) + swap_z(first[1], 1).astype(F32)


def added(kept, arrived):
    return (kept.astype(F32) + arrived.astype(F32)).astype(BF)


def fast_shards(tokens, segments, positions, cotangent, attn_gain, w_query, w_key, w_value, w_out,
                mlp_gain, w_gate, w_up, w_down):
    z, x, y, c, b = ids()
    first = c == 0
    x0 = tokens[0]
    ct0 = cotangent[0]

    gain_columns = jnp.pad(jnp.stack([attn_gain, mlp_gain], axis=1), ((0, 0), (64, 62)))
    *parts, x0 = prepare(x0, positions, w_query, w_key, w_value, gain_columns, w_gate, w_up)
    do_own = jnp.concatenate([w_down, w_out], axis=0)
    do_z = [do_own] + [swap_z(do_own, k) for k in (1, 2, 3)]
    from_blk = [parts[0]] + [swap_b(parts[k], k) for k in (1, 2, 3)]

    from_blk, do_z, x0 = lax.optimization_barrier((from_blk, do_z, x0))
    qkv_own = columns(from_blk)
    qkv_z = [qkv_own] + [swap_z(qkv_own, k) for k in (1, 2, 3)]
    do_near = jnp.stack(do_z)
    do_far = swap_x(do_near)
    x2 = swap_y(x0)

    qkv_z, x0, do_far = lax.optimization_barrier((qkv_z, x0, do_far))
    qkv_a = jnp.stack(qkv_z)
    qkv_b = swap_x(qkv_a)
    x1, x3 = swap_core(x0), swap_core(x2)
    xs = (x0, x1, x2, x3)
    tabs = tables(xs)
    out_zx = jnp.stack([do_near[:, 64:], do_far[:, 64:]])
    out_y = swap_y(out_zx)
    gu_near = stack_z(units(xs))

    qkv_b, out_y, tabs, ct0 = lax.optimization_barrier((qkv_b, out_y, tabs, ct0))
    ct2 = swap_y(ct0)
    *saved, gains, a0, a1, a2, a3 = attend(xs, qkv_a, qkv_b, *tabs[:3])

    a1, a2, a3, gu_near, ct2 = lax.optimization_barrier((a1, a2, a3, gu_near, ct2))
    a1, a2, a3 = swap_b(a1, 1), swap_b(a2, 2), swap_b(a3, 3)
    out_own = jnp.stack([out_zx[0], out_y[0], out_zx[1], out_y[1]])
    out_other = swap_core(out_own)
    gu_far = swap_x(after(gu_near, a1))

    a1, a2, a3, out_other, ct0, ct2 = lax.optimization_barrier((a1, a2, a3, out_other, ct0, ct2))
    resid, n0, wo, heads = project((a0, a1, a2, a3), x0, gains, out_own, out_other)
    n2, n1 = swap_y(n0), swap_core(n0)
    ct1, ct3 = swap_core(ct0), swap_core(ct2)
    n2, n1, ct1, ct3, gu_far = lax.optimization_barrier((n2, n1, ct1, ct3, gu_far))
    n3 = swap_core(n2)

    n_all, ct_all, hid, dg, du, wgu, wd = hidden_and_back(
        (n0, n1, n2, n3), (ct0, ct1, ct2, ct3), (gu_near, gu_far, do_near, do_far))
    gn_own, gn_far, gn_send = normed_back(dg, du, wgu)
    gn_in = swap_core(gn_send)
    gu_keep, gu_send, d_keep, d_send = ff_grads(n_all, ct_all, hid, dg, du)
    gn_in, gu_send, d_send, hid = lax.optimization_barrier((gn_in, gu_send, d_send, hid))
    gn_there = swap_y((gn_far + gn_in[1].astype(F32)).astype(BF))
    gn_here = gn_own + gn_in[0].astype(F32)
    out_own, out_far, out_send = down(hid, wd, resid)
    out_in = swap_core(out_send)
    gu_in = swap_x(gu_send)
    gn_there, out_in, d_send = lax.optimization_barrier((gn_there, out_in, d_send))
    out_here, out_2, mid, br0, ga0, ga1, ga2, ga3, gain2 = mid_back(
        gn_here, gn_there, resid, ct0, gains, wo, (out_own, out_far, out_in))
    ga1, ga2, ga3 = swap_b(ga1, 1), swap_b(ga2, 2), swap_b(ga3, 3)
    d_in = swap_x(d_send)
    o_keep, o_send = out_grads(heads, br0)
    o_in = swap_core(o_send)
    o_2 = [added(o_keep[j], o_in[j]) for j in range(2)]
    gu_in = after(gu_in, ga1)
    gu_2 = added(gu_keep, gu_in)
    ga1, ga2, ga3, gu_2, o_2, out_2 = lax.optimization_barrier((ga1, ga2, ga3, gu_2, o_2, out_2))
    gu_far = swap_z(gu_2[2:], 2)
    o_2in = swap_x(o_2[1])
    out_there = swap_y(out_2)
    qkv_keep, qkv_send, gn_keep, gn_keep2, gn_send = attend_back(saved, (tabs[0], tabs[1], tabs[3]), xs, (ga0, ga1, ga2, ga3), gain2)
    qkv_send, gn_send, d_in, o_2in, out_there = lax.optimization_barrier((qkv_send, gn_send, d_in, o_2in, out_there))
    qkv_in = swap_x(qkv_send)
    gn_in2 = swap_core(gn_send)
    d_2 = added(d_keep, d_in)
    d_far = swap_z(d_2[2:], 2)
    o_3 = [added(o_2[0][j], o_2in[j]) for j in range(2)]
    o_3in = swap_y(o_3[1])
    gn_here2 = added(gn_keep, gn_in2[0])
    there_in = swap_y(added(gn_keep2, gn_in2[1]))
    output = (out_here + out_there.astype(F32)).astype(BF)
    qkv_in, o_3in, gu_2, d_2 = lax.optimization_barrier((qkv_in, o_3in, gu_2, d_2))
    o_4 = added(o_3[0], o_3in)
    tail = [
        jnp.concatenate([
            added(qkv_keep[k], qkv_in[k]), o_4[k][:, :640],
            jnp.concatenate([o_4[k][8 * t : 8 * t + 8, 640:] for t in range(3)]
                            + [jnp.zeros((8, 256), BF)], axis=1)], axis=0)
        for k in range(4)
    ]
    tail = [tail[0]] + [swap_z(tail[k], k) for k in (1, 2, 3)]
    gu_rows = halve_z(gu_2, gu_far).astype(BF).reshape(4, 24, 1024)
    gu_order = by_index([gu_rows[j] for j in range(4)], b)
    grad_down = halve_z(d_2, d_far)
    tail, there_in, gu_order, grad_down = lax.optimization_barrier((tail, there_in, gu_order, grad_down))
    rows = sum(term.astype(F32) for term in tail)
    rows96 = rows[:96].astype(BF).reshape(4, 24, 640)
    order = by_index([rows96[j] for j in range(4)], b)
    from_heads = [order[0]] + [swap_b(order[j], j) for j in (1, 2, 3)]
    from_units = [gu_order[0]] + [swap_b(gu_order[j], j) for j in (1, 2, 3)]
    grad_out = jnp.concatenate(
        [rows[96:120], jnp.concatenate([rows[120:128, 128 * t : 128 * t + 128] for t in range(3)], axis=0)], axis=1)
    (grad_input,) = call(last_kernel, [((256, 768), BF)], [gn_here2, there_in, mid, x0, gains],
                         flops=10_000_000, nbytes=3_000_000)

    grad_query, grad_key, grad_value, grad_gate, grad_up, gain_sums = finish(from_heads, from_units)
    return (output[None], grad_input[None], gain_sums[:, 64], grad_query, grad_key, grad_value, grad_out,
            gain_sums[:, 65], grad_gate, grad_up, grad_down)


def solution(mesh):
    fits = dict(mesh.shape) == {"dp": 8, "blk": 4}
    return jax.shard_map(
        fast_shards if fits else shards,
        mesh=mesh,
        in_specs=(
            P("dp", "blk", None),
            P("dp", "blk"),
            P("dp", "blk"),
            P("dp", "blk", None),
            P(("dp", "blk")),
            P(("dp", "blk"), None),
            P(("dp", "blk"), None),
            P(("dp", "blk"), None),
            P(("dp", "blk"), None),
            P(("dp", "blk")),
            P(("dp", "blk"), None),
            P(("dp", "blk"), None),
            P(("dp", "blk"), None),
        ),
        out_specs=(
            P("dp", "blk", None),
            P("dp", "blk", None),
            P(("dp", "blk")),
            P(("dp", "blk"), None),
            P(("dp", "blk"), None),
            P(("dp", "blk"), None),
            P(("dp", "blk"), None),
            P(("dp", "blk")),
            P(("dp", "blk"), None),
            P(("dp", "blk"), None),
            P(("dp", "blk"), None),
        ),
        check_vma=False,
    )
```

```python
import math

import jax
import jax.numpy as jnp
from jax import lax
from jax.experimental import pallas as pl
from jax.experimental.pallas import tpu as pltpu
from jax.sharding import PartitionSpec as P

HEADS = 12
HEAD_DIM = 64


EPS = 1e-05
SCALE = 0.125
NEG = -1e30


def rope_tables(slot_positions, half_dim):
    inverse = jnp.exp(-math.log(10000.0) * jnp.arange(half_dim, dtype=jnp.float32) / half_dim)
    angles = slot_positions.astype(jnp.float32)[:, None] * inverse[None, :]
    return (jnp.cos(angles)[:, None, :], jnp.sin(angles)[:, None, :])


def rotate(tensor, cosine_table, sine_table):
    half_dim = tensor.shape[-1] // 2
    leading = tensor[..., :half_dim]
    trailing = tensor[..., half_dim:]
    return jnp.concatenate(
        [
            leading * cosine_table - trailing * sine_table,
            trailing * cosine_table + leading * sine_table,
        ],
        axis=-1,
    )


def matmul(left_matrix, right_matrix):
    return jnp.dot(left_matrix, right_matrix, preferred_element_type=jnp.float32)


def left_product(left_matrix, right_matrix):
    return lax.dot_general(
        left_matrix, right_matrix, (((0,), (0,)), ((), ())), preferred_element_type=jnp.float32
    )


def right_product(left_matrix, right_matrix):
    return lax.dot_general(
        left_matrix, right_matrix, (((1,), (1,)), ((), ())), preferred_element_type=jnp.float32
    )


def norm_back(grad_normed, values, inverse, gain):
    unit_normed = values * inverse
    scaled = grad_normed * gain
    grad_gain = jnp.sum(grad_normed * unit_normed, axis=0)
    grad_values = inverse * (
        scaled - unit_normed * jnp.mean(scaled * unit_normed, axis=-1, keepdims=True)
    )
    return (grad_values, grad_gain)


def score_mask(query_segments, query_index, key_segments, key_index):
    return (query_segments[:, None] == key_segments[None, :]) & (
        key_index[None, :] <= query_index[:, None]
    )


def block_grads(query_block, grad_block, lse_rows, delta_rows, allowed, key_block, value_block):
    scores = (
        jnp.einsum("qhd,khd->hqk", query_block, key_block, preferred_element_type=jnp.float32)
        * SCALE
    )
    probability = jnp.exp(jnp.where(allowed[None], scores - lse_rows.T[:, :, None], NEG))
    grad_value = jnp.einsum(
        "hqk,qhd->khd",
        probability.astype(jnp.bfloat16),
        grad_block,
        preferred_element_type=jnp.float32,
    )
    grad_probs = jnp.einsum(
        "qhd,khd->hqk", grad_block, value_block, preferred_element_type=jnp.float32
    )
    grad_scores = (probability * (grad_probs - delta_rows.T[:, :, None])).astype(jnp.bfloat16)
    grad_query = (
        jnp.einsum("hqk,khd->qhd", grad_scores, key_block, preferred_element_type=jnp.float32)
        * SCALE
    )
    grad_key = (
        jnp.einsum("hqk,qhd->khd", grad_scores, query_block, preferred_element_type=jnp.float32)
        * SCALE
    )
    return (grad_query, grad_key, grad_value)


def shards(
    tokens,
    segments,
    positions,
    cotangent,
    attn_gain,
    w_query,
    w_key,
    w_value,
    w_out,
    mlp_gain,
    w_gate,
    w_up,
    w_down,
):
    local_rows = tokens.shape[1]
    model_width = tokens.shape[2]
    blocks = lax.axis_size("blk")
    own_start = lax.axis_index("blk") * local_rows
    query_index = own_start + jnp.arange(local_rows, dtype=jnp.int32)
    own_segments = segments[0]
    cosine_table, sine_table = rope_tables(positions[0], HEAD_DIM // 2)
    x_float = tokens[0].astype(jnp.float32)
    gathered = (
        lax.all_gather(attn_gain, ("dp", "blk"), axis=0, tiled=True),
        lax.all_gather(w_query, ("dp", "blk"), axis=0, tiled=True),
        lax.all_gather(w_key, ("dp", "blk"), axis=0, tiled=True),
        lax.all_gather(w_value, ("dp", "blk"), axis=0, tiled=True),
        lax.all_gather(w_out, ("dp", "blk"), axis=0, tiled=True),
        lax.all_gather(mlp_gain, ("dp", "blk"), axis=0, tiled=True),
        lax.all_gather(w_gate, ("dp", "blk"), axis=0, tiled=True),
        lax.all_gather(w_up, ("dp", "blk"), axis=0, tiled=True),
        lax.all_gather(w_down, ("dp", "blk"), axis=0, tiled=True),
    )
    gain_one = gathered[0].astype(jnp.float32)
    gain_two = gathered[5].astype(jnp.float32)
    inverse_one = lax.rsqrt(jnp.mean(x_float * x_float, axis=-1, keepdims=True) + EPS)
    normed = (x_float * inverse_one * gain_one).astype(jnp.bfloat16)
    query_rot = rotate(
        matmul(normed, gathered[1]).reshape(local_rows, HEADS, HEAD_DIM), cosine_table, sine_table
    ).astype(jnp.bfloat16)
    key_rot = rotate(
        matmul(normed, gathered[2]).reshape(local_rows, HEADS, HEAD_DIM), cosine_table, sine_table
    ).astype(jnp.bfloat16)
    value_heads = (
        matmul(normed, gathered[3]).astype(jnp.bfloat16).reshape(local_rows, HEADS, HEAD_DIM)
    )
    key_flat = key_rot.reshape(local_rows, model_width)
    value_flat = value_heads.reshape(local_rows, model_width)
    start_state = (
        jnp.full((HEADS, local_rows), NEG, jnp.float32),
        jnp.zeros((HEADS, local_rows), jnp.float32),
        jnp.zeros((local_rows, HEADS, HEAD_DIM), jnp.float32),
    )
    key_piece = lax.all_gather(key_flat, "blk", axis=0, tiled=True)
    value_piece = lax.all_gather(value_flat, "blk", axis=0, tiled=True)
    seg_piece = lax.all_gather(own_segments, "blk", axis=0, tiled=True)
    piece_rows = key_piece.shape[0]
    needed = (jnp.int32(0) <= own_start + local_rows - 1) & (
        seg_piece[piece_rows - 1] >= own_segments[0]
    )

    def attend_sweep(current):

        def attend_visit(number, partial_value):
            running_max, running_sum, weighted = partial_value
            offset = number * local_rows
            key_block = lax.dynamic_slice_in_dim(key_piece, offset, local_rows, 0).reshape(
                local_rows, HEADS, HEAD_DIM
            )
            value_block = lax.dynamic_slice_in_dim(value_piece, offset, local_rows, 0).reshape(
                local_rows, HEADS, HEAD_DIM
            )
            seg_block = lax.dynamic_slice_in_dim(seg_piece, offset, local_rows, 0)
            key_index = offset + jnp.arange(local_rows, dtype=jnp.int32)
            allowed = score_mask(own_segments, query_index, seg_block, key_index)
            scores = (
                jnp.einsum("qhd,khd->hqk", query_rot, key_block, preferred_element_type=jnp.float32)
                * SCALE
            )
            scores = jnp.where(allowed[None], scores, NEG)
            new_max = jnp.maximum(running_max, jnp.max(scores, axis=-1))
            probability = jnp.where(allowed[None], jnp.exp(scores - new_max[:, :, None]), 0.0)
            factor = jnp.exp(running_max - new_max)
            running_sum = running_sum * factor + jnp.sum(probability, axis=-1)
            weighted = weighted * factor.T[:, :, None] + jnp.einsum(
                "hqk,khd->qhd",
                probability.astype(jnp.bfloat16),
                value_block,
                preferred_element_type=jnp.float32,
            )
            return (new_max, running_sum, weighted)

        return lax.fori_loop(0, piece_rows // local_rows, attend_visit, current)

    final_max, final_sum, final_weighted = lax.cond(
        needed, attend_sweep, lambda unchanged: unchanged, start_state
    )
    attn_heads = (final_weighted / final_sum.T[:, :, None]).astype(jnp.bfloat16)
    lse_rows = (final_max + jnp.log(final_sum)).T
    attn_flat = attn_heads.reshape(local_rows, model_width)
    resid = x_float + matmul(attn_flat, gathered[4])
    inverse_two = lax.rsqrt(jnp.mean(resid * resid, axis=-1, keepdims=True) + EPS)
    normed_two = (resid * inverse_two * gain_two).astype(jnp.bfloat16)
    gate = matmul(normed_two, gathered[6])
    up_values = matmul(normed_two, gathered[7])
    hidden = (jax.nn.silu(gate) * up_values).astype(jnp.bfloat16)
    output = (resid + matmul(hidden, gathered[8])).astype(jnp.bfloat16)
    later = (
        lax.all_gather(attn_gain, ("dp", "blk"), axis=0, tiled=True),
        lax.all_gather(w_query, ("dp", "blk"), axis=0, tiled=True),
        lax.all_gather(w_key, ("dp", "blk"), axis=0, tiled=True),
        lax.all_gather(w_value, ("dp", "blk"), axis=0, tiled=True),
        lax.all_gather(w_out, ("dp", "blk"), axis=0, tiled=True),
        lax.all_gather(mlp_gain, ("dp", "blk"), axis=0, tiled=True),
        lax.all_gather(w_gate, ("dp", "blk"), axis=0, tiled=True),
        lax.all_gather(w_up, ("dp", "blk"), axis=0, tiled=True),
        lax.all_gather(w_down, ("dp", "blk"), axis=0, tiled=True),
    )
    grad_res = cotangent[0].astype(jnp.float32)
    grad_mlp = grad_res.astype(jnp.bfloat16)
    grad_down = left_product(hidden, grad_mlp)
    grad_hidden = right_product(grad_mlp, later[8])
    sigmoid_gate = jax.nn.sigmoid(gate)
    grad_gate_low = (
        grad_hidden * up_values * sigmoid_gate * (1.0 + gate * (1.0 - sigmoid_gate))
    ).astype(jnp.bfloat16)
    grad_up_low = (grad_hidden * gate * sigmoid_gate).astype(jnp.bfloat16)
    grad_gate_w = left_product(normed_two, grad_gate_low)
    grad_up_w = left_product(normed_two, grad_up_low)
    grad_normed_two = right_product(grad_gate_low, later[6]) + right_product(grad_up_low, later[7])
    grad_resid_norm, grad_gain_two = norm_back(grad_normed_two, resid, inverse_two, gain_two)
    grad_mid = grad_res + grad_resid_norm
    grad_branch = grad_mid.astype(jnp.bfloat16)
    grad_out_w = left_product(attn_flat, grad_branch)
    grad_attn = (
        right_product(grad_branch, later[4])
        .astype(jnp.bfloat16)
        .reshape(local_rows, HEADS, HEAD_DIM)
    )
    delta_rows = jnp.sum(grad_attn.astype(jnp.float32) * attn_heads.astype(jnp.float32), axis=-1)
    pack_length = local_rows * blocks
    empty_back = (
        jnp.zeros((local_rows, HEADS, HEAD_DIM), jnp.float32),
        jnp.zeros((pack_length, 2 * model_width), jnp.float32),
    )
    back_key_piece = lax.all_gather(key_flat, "blk", axis=0, tiled=True)
    back_value_piece = lax.all_gather(value_flat, "blk", axis=0, tiled=True)
    back_seg_piece = lax.all_gather(own_segments, "blk", axis=0, tiled=True)
    back_piece_rows = back_key_piece.shape[0]
    needed = (jnp.int32(0) <= own_start + local_rows - 1) & (
        back_seg_piece[back_piece_rows - 1] >= own_segments[0]
    )

    def back_sweep(current):

        def back_visit(number, partial_value):
            grad_query_acc, grad_pairs = partial_value
            offset = number * local_rows
            key_block = lax.dynamic_slice_in_dim(back_key_piece, offset, local_rows, 0).reshape(
                local_rows, HEADS, HEAD_DIM
            )
            value_block = lax.dynamic_slice_in_dim(back_value_piece, offset, local_rows, 0).reshape(
                local_rows, HEADS, HEAD_DIM
            )
            seg_block = lax.dynamic_slice_in_dim(back_seg_piece, offset, local_rows, 0)
            key_index = offset + jnp.arange(local_rows, dtype=jnp.int32)
            allowed = score_mask(own_segments, query_index, seg_block, key_index)
            part_query, part_key, part_value = block_grads(
                query_rot, grad_attn, lse_rows, delta_rows, allowed, key_block, value_block
            )
            new_rows = jnp.concatenate(
                [
                    part_key.reshape(local_rows, model_width),
                    part_value.reshape(local_rows, model_width),
                ],
                axis=1,
            )
            existing = lax.dynamic_slice_in_dim(grad_pairs, offset, local_rows, 0)
            grad_pairs = lax.dynamic_update_slice_in_dim(grad_pairs, existing + new_rows, offset, 0)
            return (grad_query_acc + part_query, grad_pairs)

        return lax.fori_loop(0, back_piece_rows // local_rows, back_visit, current)

    grad_query_rot, grad_pairs_all = lax.cond(
        needed, back_sweep, lambda unchanged: unchanged, empty_back
    )
    own_pairs = lax.psum_scatter(
        grad_pairs_all.astype(jnp.bfloat16), "blk", scatter_dimension=0, tiled=True
    ).astype(jnp.float32)
    grad_key_rot = own_pairs[:, :model_width].reshape(local_rows, HEADS, HEAD_DIM)
    grad_value_heads = own_pairs[:, model_width:].reshape(local_rows, HEADS, HEAD_DIM)
    grad_query_low = (
        rotate(grad_query_rot, cosine_table, -sine_table)
        .reshape(local_rows, model_width)
        .astype(jnp.bfloat16)
    )
    grad_key_low = (
        rotate(grad_key_rot, cosine_table, -sine_table)
        .reshape(local_rows, model_width)
        .astype(jnp.bfloat16)
    )
    grad_value_low = grad_value_heads.reshape(local_rows, model_width).astype(jnp.bfloat16)
    grad_query_w = left_product(normed, grad_query_low)
    grad_key_w = left_product(normed, grad_key_low)
    grad_value_w = left_product(normed, grad_value_low)
    grad_normed = (
        right_product(grad_query_low, later[1])
        + right_product(grad_key_low, later[2])
        + right_product(grad_value_low, later[3])
    )
    grad_x_norm, grad_gain_one = norm_back(grad_normed, x_float, inverse_one, gain_one)
    grad_input = (grad_mid + grad_x_norm).astype(jnp.bfloat16)
    summed = (
        lax.psum_scatter(grad_gain_one, ("dp", "blk"), scatter_dimension=0, tiled=True),
        lax.psum_scatter(grad_query_w, ("dp", "blk"), scatter_dimension=0, tiled=True),
        lax.psum_scatter(grad_key_w, ("dp", "blk"), scatter_dimension=0, tiled=True),
        lax.psum_scatter(grad_value_w, ("dp", "blk"), scatter_dimension=0, tiled=True),
        lax.psum_scatter(grad_out_w, ("dp", "blk"), scatter_dimension=0, tiled=True),
        lax.psum_scatter(grad_gain_two, ("dp", "blk"), scatter_dimension=0, tiled=True),
        lax.psum_scatter(grad_gate_w, ("dp", "blk"), scatter_dimension=0, tiled=True),
        lax.psum_scatter(grad_up_w, ("dp", "blk"), scatter_dimension=0, tiled=True),
        lax.psum_scatter(grad_down, ("dp", "blk"), scatter_dimension=0, tiled=True),
    )
    return (
        output.reshape(1, local_rows, model_width),
        grad_input.reshape(1, local_rows, model_width),
        summed[0],
        summed[1],
        summed[2],
        summed[3],
        summed[4],
        summed[5],
        summed[6],
        summed[7],
        summed[8],
    )


BF = jnp.bfloat16
F32 = jnp.float32
VMEM = pltpu.VMEM
LANES = 256


def ids():
    dp, blk = lax.axis_index("dp"), lax.axis_index("blk")
    return dp // 2, dp % 2, blk // 2, blk % 2, blk


def flip(bit, other):
    total = 0
    weight = 1
    while weight <= 2:
        own = (bit // weight) % 2
        total = total + weight * ((1 - own) if (other // weight) % 2 else own)
        weight *= 2
    return total


def exclusive(a, b):
    low, high = (a + b) % 2, (a // 2 + b // 2) % 2
    return low + 2 * high


def aligned(value, multiple):
    return pl.multiple_of(value, multiple)


def dot(a, b, ca=1, cb=0):
    return lax.dot_general(a, b, (((ca,), (cb,)), ((), ())), preferred_element_type=F32)


HBM = "hbm"


def call(kernel, outs, ins, anys=(), scratch=(), flops=0, nbytes=0, grant=24):
    def place(far):
        return pl.BlockSpec(memory_space=pltpu.MemorySpace.HBM if far else VMEM)

    return pl.pallas_call(
        kernel,
        out_shape=[jax.ShapeDtypeStruct(out[0], out[1]) for out in outs],
        in_specs=[place(i in anys) for i in range(len(ins))],
        out_specs=[place(len(out) > 2) for out in outs],
        scratch_shapes=list(scratch),
        compiler_params=pltpu.CompilerParams(vmem_limit_bytes=grant * 1024 * 1024),
        cost_estimate=pl.CostEstimate(flops=flops, bytes_accessed=nbytes, transcendentals=0),
    )(*ins)


def pair(low, first, second):
    (a, i), (b, j) = first, second
    left = a[:, 128 * (i // 2) : 128 * (i // 2) + 128]
    right = b[:, 128 * (j // 2) : 128 * (j // 2) + 128]
    left = pltpu.roll(left, 64, 1) if i % 2 else left
    right = right if j % 2 else pltpu.roll(right, 64, 1)
    return jnp.where(low, left, right)


def pairs(low, blocks):
    return jnp.concatenate([pair(low, blocks[i], blocks[i + 1]) for i in range(0, len(blocks), 2)], axis=1)


def prepare_kernel(gains, place, wq_h, wk_h, wv_h, wg_h, wu_h, x_h, r0_o, r1_o, r2_o, r3_o, x_o,
                   wq, wk, wv, wg, wu, order, sems):
    z, x, y, c, b = ids()
    far, near = (wq_h, wk_h, wv_h, wg_h, wu_h), (wq, wk, wv, wg, wu)
    copies = [pltpu.make_async_copy(a, d, sems.at[i]) for i, (a, d) in enumerate(zip(far, near))]
    copies.append(pltpu.make_async_copy(x_h, x_o.at[pl.ds(0, 256)], sems.at[5]))
    for copy in copies:
        copy.start()
    for copy in copies[:5]:
        copy.wait()
    low = lax.broadcasted_iota(jnp.int32, (wq.shape[0], 128), 1) < 64
    q, k, v, g, gate, up = (ref[...].astype(F32) for ref in (wq, wk, wv, gains, wg, wu))
    at = jnp.broadcast_to(place[...], (16, 256)).astype(F32)
    tens = jnp.floor(at * (1.0 / 32))
    x_o[256:272, :] = jnp.concatenate([tens, at - 32.0 * tens, jnp.zeros_like(at)], axis=1).astype(BF)
    for j in range(4):
        blocks = [(w, 3 * j + t) for w in (q, k, v) for t in range(3)] + [(g, 1)]
        order[flip(b, j)] = pairs(low, blocks).astype(BF)
        wide = pairs(low, [(w, 4 * i + j) for w in (gate, up) for i in range(8)])
        rest = jnp.concatenate([wide[8 * t : 8 * t + 8, 768:1024] for t in range(3)], axis=1)
        x_o[272 + 32 * j : 304 + 32 * j, :] = jnp.concatenate([wide[:, 0:768], rest], axis=0).astype(BF)
    for k, out in enumerate((r0_o, r1_o, r2_o, r3_o)):
        out[...] = order[k]
    copies[5].wait()


def prepare(tokens, place, wq, wk, wv, gains, wg, wu):
    outs = [((24, 640), BF)] * 4 + [((400, 768), BF)]
    scratch = [*[VMEM((24, 768), BF)] * 3, *[VMEM((24, 2048), BF)] * 2, VMEM((4, 24, 640), BF),
               pltpu.SemaphoreType.DMA((7,))]
    return call(prepare_kernel, outs, [gains, place, wq, wk, wv, wg, wu, tokens], anys=range(2, 8), scratch=scratch,
                flops=1_000_000, nbytes=1_000_000, grant=60)


def columns_kernel(r0, r1, r2, r3, out, rows):
    z, x, y, c, b = ids()
    for k, piece in enumerate((r0, r1, r2, r3)):
        rows[pl.ds(aligned(flip(b, k) * 24, 24), 24), :] = piece[...].astype(F32)
    out[...] = rows[...].astype(BF)


def columns(pieces):
    (out,) = call(columns_kernel, [((96, 640), BF)], pieces, scratch=[VMEM((96, 640), F32)], flops=1_000_000, nbytes=300_000)
    return out


def units_kernel(x0, x1, x2, x3, gate_o, up_o, rows):
    z, x, y, c, b = ids()
    for k, piece in enumerate((x0, x1, x2, x3)):
        part = piece[pl.ds(aligned(272 + 32 * b, 16), 32), :].astype(F32)
        rest = jnp.concatenate([part[24:32, 256 * t : 256 * t + 256] for t in range(3)], axis=0)
        rows[pl.ds(aligned(flip(b, k) * 24, 24), 24), :] = jnp.concatenate([part[0:24], rest], axis=1)
    gate_o[...] = rows[:, 0:512].astype(BF)
    up_o[...] = rows[:, 512:1024].astype(BF)


def units(xs):
    outs = [((96, 512), BF)] * 2
    return call(units_kernel, outs, xs, scratch=[VMEM((96, 1024), F32)], flops=1_000_000, nbytes=3_000_000)


def finish_kernel(h0, h1, h2, h3, u0, u1, u2, u3, q_o, k_o, v_o, gate_o, up_o, gains_o, heads, units):
    z, x, y, c, b = ids()
    for k in range(4):
        heads[k] = (h0, h1, h2, h3)[k][...]
        units[k] = (u0, u1, u2, u3)[k][...]
    low = lax.broadcasted_iota(jnp.int32, (heads.shape[1], 128), 1) < 64
    parts = [heads[flip(b, j)].astype(F32) for j in range(4)]
    for t, out in enumerate((q_o, k_o, v_o)):
        out[...] = pairs(low, [(parts[m // 3], 3 * t + m % 3) for m in range(12)])
    gains_o[...] = parts[0][:, 512:640] + parts[1][:, 512:640] + parts[2][:, 512:640] + parts[3][:, 512:640]
    parts = [units[flip(b, j)].astype(F32) for j in range(4)]
    for t, out in enumerate((gate_o, up_o)):
        out[...] = pairs(low, [(parts[m % 4], 8 * t + m // 4) for m in range(32)])


def finish(heads, units):
    outs = [((24, 768), F32)] * 3 + [((24, 2048), F32)] * 2 + [((24, 128), F32)]
    return call(finish_kernel, outs, [*heads, *units], scratch=[VMEM((4, 24, 640), BF), VMEM((4, 24, 1024), BF)],
                flops=1_000_000, nbytes=2_000_000)


def tables_kernel(x0, x1, x2, x3, table_o, rows_o, marks, table, rows, sems, out_sems):
    z, x, y, c, b = ids()
    copies = [
        pltpu.make_async_copy(piece.at[pl.ds(256, 16)], marks.at[k], sems.at[k])
        for k, piece in enumerate((x0, x1, x2, x3))
    ]
    for copy in copies:
        copy.start()
    for copy in copies:
        copy.wait()
    lane = lax.broadcasted_iota(jnp.int32, (256, 128), 1)
    inverse = jnp.exp((lane % 32).astype(F32) * (-math.log(10000.0) / 32))
    for k in range(4):
        own = marks[k].astype(F32)
        place = (32.0 * own[:, 0:256] + own[:, 256:512])[0:1]
        slot = lax.broadcasted_iota(jnp.int32, (8, 256), 1) + 256 * flip(b, k)
        rows[k] = slot.astype(F32) - jnp.broadcast_to(place, (8, 256))
        angles = jnp.broadcast_to(place, (128, 256)).T * inverse
        sine = jnp.sin(angles)
        table[k] = jnp.where(lane < 64, jnp.cos(angles), jnp.where(lane < 96, -sine, sine))
    leaving = [
        pltpu.make_async_copy(ref, out, out_sems.at[i])
        for i, (ref, out) in enumerate(((table, table_o), (rows, rows_o)))
    ]
    for copy in leaving:
        copy.start()
    for copy in leaving:
        copy.wait()


def tables(xs):
    outs = [((4, 256, 128), F32, HBM), ((4, 8, 256), F32, HBM)]
    scratch = [
        VMEM((4, 16, 768), BF), VMEM((4, 256, 128), F32), VMEM((4, 8, 256), F32),
        pltpu.SemaphoreType.DMA((4,)), pltpu.SemaphoreType.DMA((2,)),
    ]
    return call(tables_kernel, outs, xs, anys=range(4), scratch=scratch, flops=10_000_000, nbytes=3_000_000)


def turns(table, low):
    turned = pltpu.roll(table, 64, 1)
    return jnp.where(low, table, turned), jnp.where(low, turned, table)


def half_swap(tile, lane):
    return jnp.where(lane % 64 < 32, pltpu.roll(tile, 96, 1), pltpu.roll(tile, 32, 1))


def pack(block):
    low = lax.broadcasted_iota(jnp.int32, (128, 128), 1) < 64
    last = block[:, 128:256].astype(F32)
    last = jnp.where(low, last[0:128], pltpu.roll(last[128:256], 64, 1))
    return jnp.concatenate([block[:, 0:128].astype(BF), last.astype(BF)], axis=0)


def unpack(block):
    low = lax.broadcasted_iota(jnp.int32, (128, 128), 1) < 64
    last = block[256:384].astype(F32)
    zero = jnp.zeros_like(last)
    last = jnp.concatenate([jnp.where(low, last, zero), jnp.where(low, pltpu.roll(last, 64, 1), zero)], axis=0)
    return jnp.concatenate([block[0:256], last.astype(BF)], axis=1)


def attend_kernel(x0, x1, x2, x3, wa, wb, table_h, rows_h,
                  qkva_o, n_o, w_o, lse_o, gains_o, a0_o, a1_o, a2_o, a3_o,
                  xs, w, qkva, n, lse, table, begins, a0, a1, a2, a3, sems, out_sems):
    z, x, y, c, b = ids()
    q, k, v, attn = (qkva.at[i] for i in range(4))
    copies = []
    for xr, piece in enumerate((wa, wb)):
        for zr in range(4):
            dp = 2 * flip(z, zr) + flip(x, xr)
            copies.append(pltpu.make_async_copy(
                piece.at[zr], w.at[pl.ds(aligned(dp * 96, 96), 96)], sems.at[4 * xr + zr]))
    copies.append(pltpu.make_async_copy(table_h, table, sems.at[8]))
    for kk, piece in enumerate((x0, x1, x2, x3)):
        copies.append(pltpu.make_async_copy(piece.at[pl.ds(0, 272)], xs.at[kk], sems.at[9 + kk]))
    copies.append(pltpu.make_async_copy(rows_h, begins, sems.at[13]))
    for copy in copies:
        copy.start()
    for copy in copies[:9]:
        copy.wait()
    leaving = [pltpu.make_async_copy(w, w_o, out_sems.at[0])]
    leaving[0].start()
    last = w[:, 512:640].astype(F32).T
    gains = last[64:72, :]
    gains_o[...] = gains
    gain = gains[0:1, :]
    lane = lax.broadcasted_iota(jnp.int32, (256, 128), 1)
    low = lane < 64
    for kk in range(4):
        rows = pl.ds(aligned(flip(b, kk) * 256, 256), 256)
        copies[9 + kk].wait()
        values = xs[kk, 0:256, :].astype(F32)
        inverse = lax.rsqrt(jnp.mean(values * values, axis=-1, keepdims=True) + EPS)
        normed = (values * inverse * gain).astype(BF)
        n[rows, :] = normed
        qkv = dot(normed, w[...])
        cosine, sine = turns(table[kk], low)
        tiles = []
        for t in range(3):
            tile = qkv[:, 128 * t : 128 * t + 128]
            tiles.append(tile * cosine + half_swap(tile, lane) * sine)
        r1, r2 = pltpu.roll(tiles[1], 64, 1), pltpu.roll(tiles[2], 64, 1)
        zero = jnp.zeros_like(r1)
        q[rows, 0:128] = tiles[0].astype(BF)
        q[rows, 128:256] = jnp.where(low, tiles[1], zero).astype(BF)
        k[rows, 0:128] = jnp.where(low, r1, r2).astype(BF)
        k[rows, 128:256] = jnp.where(low, r2, zero).astype(BF)
        v[rows, 0:128] = qkv[:, 384:512].astype(BF)
        v[rows, 128:256] = jnp.where(low, qkv[:, 512:640], zero).astype(BF)
    for at, (ref, out) in enumerate(((n, n_o), (qkva.at[pl.ds(0, 3)], qkva_o.at[pl.ds(0, 3)]))):
        leaving.append(pltpu.make_async_copy(ref, out, out_sems.at[3 + at]))
        leaving[-1].start()
    copies[13].wait()
    head = lax.broadcasted_iota(jnp.int32, (256, LANES), 1) // 64
    for i in range(4):
        width = 256 * (i + 1)
        query = q[256 * i : 256 * i + 256, :]
        begin = jnp.broadcast_to(begins[flip(b, i)][0:1, :], (128, 256)).T[:, 0:1]
        column = lax.broadcasted_iota(jnp.int32, (256, width), 1)
        row = lax.broadcasted_iota(jnp.int32, (256, width), 0) + 256 * i
        allowed = (column <= row) & (column.astype(F32) >= begin)
        total = jnp.zeros((256, LANES), F32)
        stats = jnp.zeros((256, 128), F32)
        for h in range(3):
            mine = jnp.where(head == h, query, jnp.zeros_like(query))
            scores = dot(mine, k[0:width, :], 1, 1) * SCALE
            scores = jnp.where(allowed, scores, NEG)
            top = jnp.max(scores, axis=-1, keepdims=True)
            weight = jnp.exp(scores - top)
            norm = jnp.sum(weight, axis=-1, keepdims=True)
            mixed = dot(weight.astype(BF), v[0:width, :]) / norm
            total = jnp.where(head == h, mixed, total)
            stats = jnp.where(lane == h, top + jnp.log(norm), stats)
        attn[256 * i : 256 * i + 256, :] = total.astype(BF)
        lse[:, 256 * i : 256 * i + 256] = stats.T[0:8]
    for at, (ref, out) in enumerate(((attn, qkva_o.at[3]), (lse, lse_o))):
        leaving.append(pltpu.make_async_copy(ref, out, out_sems.at[1 + at]))
        leaving[-1].start()
    for kk, (out, far) in enumerate(((a0, a0_o), (a1, a1_o), (a2, a2_o), (a3, a3_o))):
        for t in range(2):
            out[t] = pack(attn[pl.ds(aligned(flip(flip(b, kk), 2 * t) * 256, 256), 256), :])
        leaving.append(pltpu.make_async_copy(out, far, out_sems.at[5 + kk]))
        leaving[-1].start()
    for copy in leaving:
        copy.wait()


def attend(xs, wa, wb, tabs):
    outs = [
        ((4, 1024, LANES), BF, HBM), ((1024, 768), BF, HBM), ((768, 640), BF, HBM),
        ((8, 1024), F32, HBM), ((8, 768), F32), *[((2, 384, 128), BF, HBM)] * 4,
    ]
    return call(
        attend_kernel, outs, [*xs, wa, wb, *tabs], anys=range(8), grant=60,
        scratch=[
            VMEM((4, 272, 768), BF), VMEM((768, 640), BF), VMEM((4, 1024, LANES), BF), VMEM((1024, 768), BF),
            VMEM((8, 1024), F32), VMEM((4, 256, 128), F32), VMEM((4, 8, 256), F32),
            *[VMEM((2, 384, 128), BF)] * 4, pltpu.SemaphoreType.DMA((14,)), pltpu.SemaphoreType.DMA((9,)),
        ],
        flops=1000, nbytes=1000,
    )


def out_kernel(a0, a1, a2, a3, x0, x2, gains, own, other, resid_o, n_o, wo_o, stack_o, wide):
    z, x, y, c, b = ids()
    for xy in range(4):
        for zr in range(4):
            chip = 8 * flip(z, zr) + 4 * flip(x, xy // 2) + 2 * flip(y, xy % 2)
            for core, pieces in enumerate((own, other)):
                at = aligned((chip + flip(c, core)) * 24, 24)
                wide[pl.ds(at, 24), :] = pieces[xy, zr].astype(F32)
    wo_o[...] = wide[...].astype(BF)
    for t, band in enumerate((x0, x2)):
        total = band[0:256, :].astype(F32)
        for k, piece in enumerate((a0, a1, a2, a3)):
            heads = unpack(piece[t])
            if t == 0:
                stack_o[k] = heads
            rows = pl.ds(aligned(flip(b, k) * 192, 192), 192)
            total += dot(heads[:, 0:192], wo_o[rows, :])
        if t == 0:
            resid_o[...] = total
        inverse = lax.rsqrt(jnp.mean(total * total, axis=-1, keepdims=True) + EPS)
        n_o[t] = (total * inverse * gains[1:2, :]).astype(BF)


def project(a, x0, x2, gains, own, other):
    outs = [((256, 768), F32), ((2, 256, 768), BF), ((768, 768), BF), ((4, 256, LANES), BF)]
    return call(out_kernel, outs, [*a, x0, x2, gains, own, other], scratch=[VMEM((768, 768), F32)],
                flops=800_000_000, nbytes=4_000_000)


def hidden_kernel(n02, n13, ct0, ct1, ct2, ct3, g_near, g_far, u_near, u_far, d_near, d_far,
                  n_o, ct_o, hid_o, dg_o, du_o, wgu_o, wd_o, sems):
    z, x, y, c, b = ids()
    copies = []
    for xr, (g, u, d) in enumerate(((g_near, u_near, d_near), (g_far, u_far, d_far))):
        for zr in range(4):
            dp = 2 * flip(z, zr) + flip(x, xr)
            at = 4 * xr + zr
            for i, w in enumerate((g, u)):
                copies.append(pltpu.make_async_copy(
                    w.at[zr], wgu_o.at[pl.ds(aligned(dp * 96, 96), 96), pl.ds(512 * i, 512)], sems.at[2 * i, at]))
            copies.append(pltpu.make_async_copy(
                d.at[zr, pl.ds(0, 64)], wd_o.at[pl.ds(aligned(dp * 64, 64), 64)], sems.at[1, at]))
    for copy in copies:
        copy.start()
    for k in range(4):
        n_o[256 * k : 256 * k + 256, :] = (n02, n13)[k % 2][k // 2]
        ct_o[256 * k : 256 * k + 256, :] = (ct0, ct1, ct2, ct3)[k][...]
    for copy in copies:
        copy.wait()
    for k in range(4):
        rows = slice(256 * k, 256 * k + 256)
        normed, cot = n_o[rows, :], ct_o[rows, :]
        for j in range(2):
            cols = slice(256 * j, 256 * j + 256)
            gate = dot(normed, wgu_o[:, 256 * j : 256 * j + 256])
            up = dot(normed, wgu_o[:, 512 + 256 * j : 768 + 256 * j])
            back = dot(cot, wd_o[cols, :], 1, 1)
            sig = 1.0 / (1.0 + jnp.exp(-gate))
            silu = gate * sig
            hid_o[rows, cols] = (silu * up).astype(BF)
            dg_o[rows, cols] = (back * up * sig * (1.0 + gate * (1.0 - sig))).astype(BF)
            du_o[rows, cols] = (back * silu).astype(BF)


def hidden_and_back(n, ct, pieces):
    outs = [((1024, 768), BF)] * 2 + [((1024, 512), BF)] * 3 + [((768, 1024), BF), ((512, 768), BF)]
    return call(
        hidden_kernel, outs, [*n, *ct, *pieces], anys=range(6, 12),
        scratch=[pltpu.SemaphoreType.DMA((3, 8))], flops=2_500_000_000, nbytes=8_000_000,
    )


def normed_back_kernel(dg, du, wgu, own_o, far_o, send_o):
    for k in range(4):
        rows = slice(256 * k, 256 * k + 256)
        grad = dot(dg[rows, :], wgu[:, 0:512], 1, 1) + dot(du[rows, :], wgu[:, 512:1024], 1, 1)
        if k == 0:
            own_o[...] = grad
        elif k == 2:
            far_o[...] = grad
        else:
            send_o[k // 2] = grad.astype(BF)


def normed_back(dg, du, wgu):
    outs = [((256, 768), F32)] * 2 + [((2, 256, 768), BF)]
    return call(normed_back_kernel, outs, [dg, du, wgu], flops=1_600_000_000, nbytes=6_000_000)


def store_by_x(grad, rows, cols, keep_o, send_o, z, x):
    for zp in range(4):
        at = 2 * rows * zp
        low, high = grad[at : at + rows], grad[at + rows : at + 2 * rows]
        keep_o[flip(z, zp), :, cols] = jnp.where(x == 0, low, high).astype(BF)
        send_o[flip(z, zp), :, cols] = jnp.where(x == 0, high, low).astype(BF)


def ff_grads_kernel(n, ct, hid, dg, du, gu_keep_o, gu_send_o, d_keep_o, d_send_o):
    z, x, y, c, b = ids()
    normed = n[...].T
    for j in range(4):
        cols = slice(256 * j, 256 * j + 256)
        part = (dg, du)[j // 2][:, 256 * (j % 2) : 256 * (j % 2) + 256]
        store_by_x(dot(normed, part), 96, cols, gu_keep_o, gu_send_o, z, x)
    hidden = hid[...].T
    for j in range(3):
        cols = slice(256 * j, 256 * j + 256)
        store_by_x(dot(hidden, ct[:, cols]), 64, cols, d_keep_o, d_send_o, z, x)


def ff_grads(n, ct, hid, dg, du):
    outs = [((4, 96, 1024), BF)] * 2 + [((4, 64, 768), BF)] * 2
    return call(ff_grads_kernel, outs, [n, ct, hid, dg, du], flops=2_400_000_000, nbytes=10_000_000)


def mid_kernel(gn_own, gn_in, resid, ct0, gains, wo, out_own, out_far, out_in, here_o, there_o, mid_o, branch_o, g0_o, g1_o, g2_o, g3_o, gain_o):
    z, x, y, c, b = ids()
    here_o[...] = out_own[...] + out_in[0].astype(F32)
    there_o[...] = (out_far[...] + out_in[1].astype(F32)).astype(BF)
    grad = gn_own[...] + gn_in[...].astype(F32)
    values = resid[...]
    inverse = lax.rsqrt(jnp.mean(values * values, axis=-1, keepdims=True) + EPS)
    unit = values * inverse
    scaled = grad * gains[1:2, :]
    gain_o[...] = jnp.broadcast_to(jnp.sum(grad * unit, axis=0, keepdims=True), gain_o.shape)
    mid = ct0[...].astype(F32) + inverse * (
        scaled - unit * jnp.mean(scaled * unit, axis=-1, keepdims=True)
    )
    mid_o[...] = mid
    branch = mid.astype(BF)
    branch_o[...] = branch
    pad = jnp.zeros((256, LANES - 192), F32)
    for k in range(4):
        rows = pl.ds(aligned(flip(b, k) * 192, 192), 192)
        part = dot(branch, wo[rows, :], 1, 1)
        (g0_o, g1_o, g2_o, g3_o)[k][...] = pack(jnp.concatenate([part, pad], axis=1))


def mid_back(gn_own, gn_in, resid, ct0, gains, wo, out):
    outs = [((256, 768), F32), ((256, 768), BF), ((256, 768), F32), ((256, 768), BF), *[((384, 128), BF)] * 4, ((8, 768), F32)]
    return call(mid_kernel, outs, [gn_own, gn_in, resid, ct0, gains, wo, *out], flops=400_000_000, nbytes=5_000_000)


def out_grads_kernel(stack, branch, keep_o, send_o, wide):
    z, x, y, c, b = ids()
    for k in range(4):
        part = dot(stack[k].T, branch[...])[0:192]
        wide[pl.ds(aligned(exclusive(flip(b, k), z) * 192, 192), 192), :] = part
    for cr, out in enumerate((keep_o, send_o)):
        for yr in range(2):
            for xr in range(2):
                for zr in range(4):
                    at = 4 * (flip(x, xr) % 2) + 2 * (flip(y, yr) % 2) + flip(c, cr) % 2 + 8 * zr
                    out[xr, yr, zr] = wide[pl.ds(aligned(at * 24, 24), 24), :].astype(BF)


def out_grads(stack, branch):
    outs = [((2, 2, 4, 24, 768), BF)] * 2
    return call(out_grads_kernel, outs, [stack, branch], scratch=[VMEM((768, 768), F32)],
                flops=400_000_000, nbytes=3_000_000)


def down_kernel(hid, wd, resid, own_o, far_o, send_o):
    for k in range(4):
        part = dot(hid[256 * k : 256 * k + 256, :], wd[...])
        if k == 0:
            own_o[...] = resid[...] + part
        elif k == 2:
            far_o[...] = part
        else:
            send_o[k // 2] = part.astype(BF)


def down(hid, wd, resid):
    outs = [((256, 768), F32)] * 2 + [((2, 256, 768), BF)]
    return call(down_kernel, outs, [hid, wd, resid], flops=800_000_000, nbytes=5_000_000)


def attend_back_kernel(qkva_h, n_h, w_h, lse_h, table_h, start_h, x0, x1, x2, x3, g0, g1, g2, g3, gain2_h,
                       keep_h, send_h, gk0_h, gk1_h, gs_h,
                       qkva, n, w, lse, table, start, xs, packed, do, dq, dk, dv, grads, wide, gain2,
                       keep_o, send_o, gk0_o, gk1_o, gs_o, sems, out_sems):
    z, x, y, c, b = ids()
    q, k, v, attn = (qkva.at[i] for i in range(4))
    first = [
        pltpu.make_async_copy(a, d, sems.at[i])
        for i, (a, d) in enumerate(((lse_h, lse), (start_h, start), (qkva_h, qkva)))
    ] + [pltpu.make_async_copy(a, packed.at[i], sems.at[3 + i]) for i, a in enumerate((g0, g1, g2, g3))]
    rest = [
        pltpu.make_async_copy(a, d, sems.at[7 + i])
        for i, (a, d) in enumerate(((table_h, table), (n_h, n), (w_h, w), (gain2_h, gain2)))
    ] + [pltpu.make_async_copy(a.at[pl.ds(0, 272)], xs.at[i], sems.at[11 + i]) for i, a in enumerate((x0, x1, x2, x3))]
    for copy in first + rest:
        copy.start()
    dk[...] = jnp.zeros_like(dk)
    dv[...] = jnp.zeros_like(dv)
    for copy in first:
        copy.wait()
    for i in range(4):
        do[pl.ds(aligned(flip(b, i) * 256, 256), 256), :] = unpack(packed[i])
    head = lax.broadcasted_iota(jnp.int32, (256, LANES), 1) // 64
    lane = lax.broadcasted_iota(jnp.int32, (256, 128), 1)
    for i in range(4):
        width = 256 * (i + 1)
        rows = slice(256 * i, 256 * i + 256)
        query, out_grad = q[rows, :] * SCALE, do[rows, :]
        product = out_grad.astype(F32) * attn[rows, :].astype(F32)
        delta = jnp.zeros((256, 128), F32)
        for h in range(3):
            delta = jnp.where(
                lane == h, jnp.sum(jnp.where(head == h, product, 0.0), axis=-1, keepdims=True), delta)
        delta = delta.T
        begin = start[flip(b, i)][0:1, :]
        key = lax.broadcasted_iota(jnp.int32, (width, 256), 0)
        slot = lax.broadcasted_iota(jnp.int32, (width, 256), 1) + 256 * i
        allowed = (key <= slot) & (key.astype(F32) >= begin)
        probs, dscores = [], []
        mine = [jnp.where(head == h, query, jnp.zeros_like(query)) for h in range(3)]
        ours = [jnp.where(head == h, out_grad, jnp.zeros_like(out_grad)) for h in range(3)]
        for h in range(3):
            scores = dot(k[0:width, :], mine[h], 1, 1)
            prob = jnp.exp(jnp.where(allowed, scores - lse[h : h + 1, rows], NEG))
            dprob = dot(v[0:width, :], ours[h], 1, 1)
            probs.append(prob.astype(BF))
            dscores.append((prob * (dprob - delta[h : h + 1, :])).astype(BF))
        dv[0:width, :] += dot(jnp.concatenate(probs, axis=1), jnp.concatenate(ours, axis=0))
        dk[0:width, :] += dot(jnp.concatenate(dscores, axis=1), jnp.concatenate(mine, axis=0))
        total = jnp.zeros((256, LANES), F32)
        for h in range(3):
            total = jnp.where(head == h, dot(dscores[h], k[0:width, :], 0, 0), total)
        dq[rows, :] = total
    for copy in rest:
        copy.wait()
    low = lane < 64
    zero = jnp.zeros((256, 128), F32)
    for i in range(4):
        rows = slice(256 * i, 256 * i + 256)
        cosine, sine = turns(table[flip(b, i)], low)
        turned = []
        for ref, factor in ((dq, SCALE), (dk, 1.0)):
            for t in range(2):
                tile = ref[rows, 128 * t : 128 * t + 128] * factor
                turned.append(tile * cosine - half_swap(tile, lane) * sine)
        k0, k1 = pltpu.roll(turned[2], 64, 1), pltpu.roll(turned[3], 64, 1)
        grads[rows, 0:128] = turned[0].astype(BF)
        grads[rows, 128:256] = jnp.where(low, turned[1], k0).astype(BF)
        grads[rows, 256:384] = jnp.where(low, k0, k1).astype(BF)
        grads[rows, 384:512] = dv[rows, 0:128].astype(BF)
        grads[rows, 512:640] = jnp.where(low, dv[rows, 128:256], zero).astype(BF)
    leaving = []

    def leave(ref, out):
        leaving.append(pltpu.make_async_copy(ref, out, out_sems.at[len(leaving)]))
        leaving[-1].start()

    gain_sum = jnp.zeros((1, 768), F32)
    for kk in range(4):
        rows = pl.ds(aligned(flip(b, kk) * 256, 256), 256)
        grad = dot(grads[rows, :], w[...], 1, 1)
        values = xs[kk, 0:256, :].astype(F32)
        inverse = lax.rsqrt(jnp.mean(values * values, axis=-1, keepdims=True) + EPS)
        gain_sum += jnp.sum(grad * (values * inverse), axis=0, keepdims=True)
        if kk % 2:
            gs_o[kk // 2] = grad.astype(BF)
        else:
            (gk0_o, gk1_o)[kk // 2][...] = grad.astype(BF)
    for ref, out in ((gs_o, gs_h), (gk0_o, gk0_h), (gk1_o, gk1_h)):
        leave(ref, out)
    row_at = lax.broadcasted_iota(jnp.int32, (128, 768), 0)
    gain_rows = jnp.where(row_at == 64, gain_sum, jnp.where(row_at == 65, gain2[0:1, :], 0.0))
    gain_columns = gain_rows.T
    normed = n[...].T
    for j in range(5):
        cols = slice(128 * j, 128 * j + 128)
        part = dot(normed, grads[:, cols])
        if j == 4:
            part = part + gain_columns
        wide[:, cols] = part
    for xr, (ref, out) in ((1, (send_o, send_h)), (0, (keep_o, keep_h))):
        for zr in range(4):
            dp = 2 * flip(z, zr) + flip(x, xr)
            ref[zr] = wide[pl.ds(aligned(dp * 96, 96), 96), :].astype(BF)
        leave(ref, out)
    for copy in leaving:
        copy.wait()


def attend_back(saved, tabs, xs, g, gain2):
    outs = [((4, 96, 640), BF, HBM)] * 2 + [((256, 768), BF, HBM)] * 2 + [((2, 256, 768), BF, HBM)]
    return call(
        attend_back_kernel, outs, [*saved, *tabs, *xs, *g, gain2], anys=range(15), grant=60,
        scratch=[
            VMEM((4, 1024, LANES), BF), VMEM((1024, 768), BF), VMEM((768, 640), BF),
            VMEM((8, 1024), F32), VMEM((4, 256, 128), F32), VMEM((4, 8, 256), F32),
            VMEM((4, 272, 768), BF), VMEM((4, 384, 128), BF), VMEM((1024, LANES), BF), *[VMEM((1024, LANES), F32)] * 3,
            VMEM((1024, 640), BF), VMEM((768, 640), F32), VMEM((8, 768), F32),
            *[VMEM(out[0], out[1]) for out in outs], pltpu.SemaphoreType.DMA((15,)), pltpu.SemaphoreType.DMA((5,)),
        ],
        flops=1000, nbytes=1000,
    )


def last_kernel(kept, arrived, mid, x0, gains, out):
    grad = kept[...].astype(F32) + arrived[...].astype(F32)
    values = x0[0:256, :].astype(F32)
    inverse = lax.rsqrt(jnp.mean(values * values, axis=-1, keepdims=True) + EPS)
    unit = values * inverse
    scaled = grad * gains[0:1, :]
    out[...] = (
        mid[...] + inverse * (scaled - unit * jnp.mean(scaled * unit, axis=-1, keepdims=True))
    ).astype(BF)


def swap_z(v, k):
    return lax.ppermute(v, "dp", [(i, i ^ (2 * k)) for i in range(8)])


def swap_x(v):
    return lax.ppermute(v, "dp", [(i, i ^ 1) for i in range(8)])


def swap_b(v, k):
    return lax.ppermute(v, "blk", [(i, i ^ k) for i in range(4)])


def swap_core(v):
    return swap_b(v, 1)


def swap_y(v):
    return swap_b(v, 2)


def after(value, *tokens):
    return lax.optimization_barrier((value, tokens))[0]


def stack_z(v):
    return jnp.stack([v] + [swap_z(v, k) for k in (1, 2, 3)])


def by_index(four, bits):
    one, two = bits % 2 == 1, bits // 2 == 1
    a, b, c, d = four
    a, b, c, d = jnp.where(one, b, a), jnp.where(one, a, b), jnp.where(one, d, c), jnp.where(one, c, d)
    return [jnp.where(two, c, a), jnp.where(two, d, b), jnp.where(two, a, c), jnp.where(two, b, d)]


def sum_z(v):
    terms = [v[0]] + [swap_z(v[k], k) for k in (1, 2, 3)]
    return sum(term.astype(F32) for term in terms)


def halve_z(v, far):
    first = [added(v[k], far[k]) for k in range(2)]
    return first[0].astype(F32) + swap_z(first[1], 1).astype(F32)


def added(kept, arrived):
    return (kept.astype(F32) + arrived.astype(F32)).astype(BF)


def fast_shards(tokens, segments, positions, cotangent, attn_gain, w_query, w_key, w_value, w_out,
                mlp_gain, w_gate, w_up, w_down):
    z, x, y, c, b = ids()
    first = c == 0
    x0 = tokens[0]
    ct0 = cotangent[0]

    gain_columns = jnp.pad(jnp.stack([attn_gain, mlp_gain], axis=1), ((0, 0), (64, 62)))
    *parts, x0 = prepare(x0, positions, w_query, w_key, w_value, gain_columns, w_gate, w_up)
    do_own = jnp.concatenate([w_down, w_out], axis=0)
    do_z = [do_own] + [swap_z(do_own, k) for k in (1, 2, 3)]
    from_blk = [parts[0]] + [swap_b(parts[k], k) for k in (1, 2, 3)]

    from_blk, do_z, x0 = lax.optimization_barrier((from_blk, do_z, x0))
    qkv_own = columns(from_blk)
    qkv_z = [qkv_own] + [swap_z(qkv_own, k) for k in (1, 2, 3)]
    do_near = jnp.stack(do_z)
    do_far = swap_x(do_near)
    x2 = swap_y(x0)

    qkv_z, x0, do_far = lax.optimization_barrier((qkv_z, x0, do_far))
    qkv_a = jnp.stack(qkv_z)
    qkv_b = swap_x(qkv_a)
    x1, x3 = swap_core(x0), swap_core(x2)
    xs = (x0, x1, x2, x3)
    tabs = tables(xs)
    out_zx = jnp.stack([do_near[:, 64:], do_far[:, 64:]])
    out_y = swap_y(out_zx)
    g_own, u_own = units(xs)
    g_near = stack_z(g_own)

    qkv_b, out_y, tabs, ct0, g_near, u_own = lax.optimization_barrier((qkv_b, out_y, tabs, ct0, g_near, u_own))
    ct2 = swap_y(ct0)
    g_far = swap_x(g_near)
    u_near = stack_z(u_own)
    *saved, gains, a0, a1, a2, a3 = attend(xs, qkv_a, qkv_b, tabs)

    a1, a2, a3, u_near, ct2, g_far, out_zx, out_y = lax.optimization_barrier(
        (a1, a2, a3, u_near, ct2, g_far, out_zx, out_y))
    a1, a2, a3 = swap_b(a1, 1), swap_b(a2, 2), swap_b(a3, 3)
    out_own = jnp.stack([out_zx[0], out_y[0], out_zx[1], out_y[1]])
    out_other = swap_core(out_own)
    u_far = swap_x(after(u_near, a1))

    a1, a2, a3, out_other, ct0, ct2, u_far = lax.optimization_barrier((a1, a2, a3, out_other, ct0, ct2, u_far))
    resid, n02, wo, heads = project((a0, a1, a2, a3), x0, x2, gains, out_own, out_other)
    n13 = swap_core(n02)
    ct1, ct3 = swap_core(ct0), swap_core(ct2)

    n_all, ct_all, hid, dg, du, wgu, wd = hidden_and_back(
        (n02, n13), (ct0, ct1, ct2, ct3), (g_near, g_far, u_near, u_far, do_near, do_far))
    gn_own, gn_far, gn_send = normed_back(dg, du, wgu)
    gn_in = swap_core(gn_send)
    gu_keep, gu_send, d_keep, d_send = ff_grads(n_all, ct_all, hid, dg, du)
    gn_in, gu_send, d_send, hid = lax.optimization_barrier((gn_in, gu_send, d_send, hid))
    gn_there = swap_y((gn_far + gn_in[1].astype(F32)).astype(BF))
    gn_here = gn_own + gn_in[0].astype(F32)
    out_own, out_far, out_send = down(hid, wd, resid)
    out_in = swap_core(out_send)
    gu_in = swap_x(gu_send)
    gn_there, out_in, d_send = lax.optimization_barrier((gn_there, out_in, d_send))
    out_here, out_2, mid, br0, ga0, ga1, ga2, ga3, gain2 = mid_back(
        gn_here, gn_there, resid, ct0, gains, wo, (out_own, out_far, out_in))
    ga1, ga2, ga3 = swap_b(ga1, 1), swap_b(ga2, 2), swap_b(ga3, 3)
    d_in = swap_x(d_send)
    o_keep, o_send = out_grads(heads, br0)
    o_in = swap_core(o_send)
    o_2 = [added(o_keep[j], o_in[j]) for j in range(2)]
    gu_in = after(gu_in, ga1)
    gu_2 = added(gu_keep, gu_in)
    ga1, ga2, ga3, gu_2, o_2, out_2 = lax.optimization_barrier((ga1, ga2, ga3, gu_2, o_2, out_2))
    gu_far = swap_z(gu_2[2:], 2)
    o_2in = swap_x(o_2[1])
    out_there = swap_y(out_2)
    qkv_keep, qkv_send, gn_keep, gn_keep2, gn_send = attend_back(saved, tabs, xs, (ga0, ga1, ga2, ga3), gain2)
    qkv_send, gn_send, d_in, o_2in, out_there = lax.optimization_barrier((qkv_send, gn_send, d_in, o_2in, out_there))
    qkv_in = swap_x(qkv_send)
    gn_in2 = swap_core(gn_send)
    d_2 = added(d_keep, d_in)
    d_far = swap_z(d_2[2:], 2)
    o_3 = [added(o_2[0][j], o_2in[j]) for j in range(2)]
    o_3in = swap_y(o_3[1])
    gn_here2 = added(gn_keep, gn_in2[0])
    there_in = swap_y(added(gn_keep2, gn_in2[1]))
    output = (out_here + out_there.astype(F32)).astype(BF)
    qkv_in, o_3in, gu_2, d_2 = lax.optimization_barrier((qkv_in, o_3in, gu_2, d_2))
    o_4 = added(o_3[0], o_3in)
    tail = [
        jnp.concatenate([
            added(qkv_keep[k], qkv_in[k]), o_4[k][:, :640],
            jnp.concatenate([o_4[k][8 * t : 8 * t + 8, 640:] for t in range(3)]
                            + [jnp.zeros((8, 256), BF)], axis=1)], axis=0)
        for k in range(4)
    ]
    tail = [tail[0]] + [swap_z(tail[k], k) for k in (1, 2, 3)]
    gu_rows = halve_z(gu_2, gu_far).astype(BF).reshape(4, 24, 1024)
    gu_order = by_index([gu_rows[j] for j in range(4)], b)
    grad_down = halve_z(d_2, d_far)
    tail, there_in, gu_order, grad_down = lax.optimization_barrier((tail, there_in, gu_order, grad_down))
    rows = sum(term.astype(F32) for term in tail)
    rows96 = rows[:96].astype(BF).reshape(4, 24, 640)
    order = by_index([rows96[j] for j in range(4)], b)
    from_heads = [order[0]] + [swap_b(order[j], j) for j in (1, 2, 3)]
    from_units = [gu_order[0]] + [swap_b(gu_order[j], j) for j in (1, 2, 3)]
    grad_out = jnp.concatenate(
        [rows[96:120], jnp.concatenate([rows[120:128, 128 * t : 128 * t + 128] for t in range(3)], axis=0)], axis=1)
    (grad_input,) = call(last_kernel, [((256, 768), BF)], [gn_here2, there_in, mid, x0, gains],
                         flops=10_000_000, nbytes=3_000_000)

    grad_query, grad_key, grad_value, grad_gate, grad_up, gain_sums = finish(from_heads, from_units)
    return (output[None], grad_input[None], gain_sums[:, 64], grad_query, grad_key, grad_value, grad_out,
            gain_sums[:, 65], grad_gate, grad_up, grad_down)


def solution(mesh):
    fits = dict(mesh.shape) == {"dp": 8, "blk": 4}
    return jax.shard_map(
        fast_shards if fits else shards,
        mesh=mesh,
        in_specs=(
            P("dp", "blk", None),
            P("dp", "blk"),
            P("dp", "blk"),
            P("dp", "blk", None),
            P(("dp", "blk")),
            P(("dp", "blk"), None),
            P(("dp", "blk"), None),
            P(("dp", "blk"), None),
            P(("dp", "blk"), None),
            P(("dp", "blk")),
            P(("dp", "blk"), None),
            P(("dp", "blk"), None),
            P(("dp", "blk"), None),
        ),
        out_specs=(
            P("dp", "blk", None),
            P("dp", "blk", None),
            P(("dp", "blk")),
            P(("dp", "blk"), None),
            P(("dp", "blk"), None),
            P(("dp", "blk"), None),
            P(("dp", "blk"), None),
            P(("dp", "blk")),
            P(("dp", "blk"), None),
            P(("dp", "blk"), None),
            P(("dp", "blk"), None),
        ),
        check_vma=False,
    )
```

```python
import math

import jax
import jax.numpy as jnp
from jax import lax
from jax.experimental import pallas as pl
from jax.experimental.pallas import tpu as pltpu
from jax.sharding import PartitionSpec as P

HEADS = 12
HEAD_DIM = 64


EPS = 1e-05
SCALE = 0.125
NEG = -1e30


def rope_tables(slot_positions, half_dim):
    inverse = jnp.exp(-math.log(10000.0) * jnp.arange(half_dim, dtype=jnp.float32) / half_dim)
    angles = slot_positions.astype(jnp.float32)[:, None] * inverse[None, :]
    return (jnp.cos(angles)[:, None, :], jnp.sin(angles)[:, None, :])


def rotate(tensor, cosine_table, sine_table):
    half_dim = tensor.shape[-1] // 2
    leading = tensor[..., :half_dim]
    trailing = tensor[..., half_dim:]
    return jnp.concatenate(
        [
            leading * cosine_table - trailing * sine_table,
            trailing * cosine_table + leading * sine_table,
        ],
        axis=-1,
    )


def matmul(left_matrix, right_matrix):
    return jnp.dot(left_matrix, right_matrix, preferred_element_type=jnp.float32)


def left_product(left_matrix, right_matrix):
    return lax.dot_general(
        left_matrix, right_matrix, (((0,), (0,)), ((), ())), preferred_element_type=jnp.float32
    )


def right_product(left_matrix, right_matrix):
    return lax.dot_general(
        left_matrix, right_matrix, (((1,), (1,)), ((), ())), preferred_element_type=jnp.float32
    )


def norm_back(grad_normed, values, inverse, gain):
    unit_normed = values * inverse
    scaled = grad_normed * gain
    grad_gain = jnp.sum(grad_normed * unit_normed, axis=0)
    grad_values = inverse * (
        scaled - unit_normed * jnp.mean(scaled * unit_normed, axis=-1, keepdims=True)
    )
    return (grad_values, grad_gain)


def score_mask(query_segments, query_index, key_segments, key_index):
    return (query_segments[:, None] == key_segments[None, :]) & (
        key_index[None, :] <= query_index[:, None]
    )


def block_grads(query_block, grad_block, lse_rows, delta_rows, allowed, key_block, value_block):
    scores = (
        jnp.einsum("qhd,khd->hqk", query_block, key_block, preferred_element_type=jnp.float32)
        * SCALE
    )
    probability = jnp.exp(jnp.where(allowed[None], scores - lse_rows.T[:, :, None], NEG))
    grad_value = jnp.einsum(
        "hqk,qhd->khd",
        probability.astype(jnp.bfloat16),
        grad_block,
        preferred_element_type=jnp.float32,
    )
    grad_probs = jnp.einsum(
        "qhd,khd->hqk", grad_block, value_block, preferred_element_type=jnp.float32
    )
    grad_scores = (probability * (grad_probs - delta_rows.T[:, :, None])).astype(jnp.bfloat16)
    grad_query = (
        jnp.einsum("hqk,khd->qhd", grad_scores, key_block, preferred_element_type=jnp.float32)
        * SCALE
    )
    grad_key = (
        jnp.einsum("hqk,qhd->khd", grad_scores, query_block, preferred_element_type=jnp.float32)
        * SCALE
    )
    return (grad_query, grad_key, grad_value)


def shards(
    tokens,
    segments,
    positions,
    cotangent,
    attn_gain,
    w_query,
    w_key,
    w_value,
    w_out,
    mlp_gain,
    w_gate,
    w_up,
    w_down,
):
    local_rows = tokens.shape[1]
    model_width = tokens.shape[2]
    blocks = lax.axis_size("blk")
    own_start = lax.axis_index("blk") * local_rows
    query_index = own_start + jnp.arange(local_rows, dtype=jnp.int32)
    own_segments = segments[0]
    cosine_table, sine_table = rope_tables(positions[0], HEAD_DIM // 2)
    x_float = tokens[0].astype(jnp.float32)
    gathered = (
        lax.all_gather(attn_gain, ("dp", "blk"), axis=0, tiled=True),
        lax.all_gather(w_query, ("dp", "blk"), axis=0, tiled=True),
        lax.all_gather(w_key, ("dp", "blk"), axis=0, tiled=True),
        lax.all_gather(w_value, ("dp", "blk"), axis=0, tiled=True),
        lax.all_gather(w_out, ("dp", "blk"), axis=0, tiled=True),
        lax.all_gather(mlp_gain, ("dp", "blk"), axis=0, tiled=True),
        lax.all_gather(w_gate, ("dp", "blk"), axis=0, tiled=True),
        lax.all_gather(w_up, ("dp", "blk"), axis=0, tiled=True),
        lax.all_gather(w_down, ("dp", "blk"), axis=0, tiled=True),
    )
    gain_one = gathered[0].astype(jnp.float32)
    gain_two = gathered[5].astype(jnp.float32)
    inverse_one = lax.rsqrt(jnp.mean(x_float * x_float, axis=-1, keepdims=True) + EPS)
    normed = (x_float * inverse_one * gain_one).astype(jnp.bfloat16)
    query_rot = rotate(
        matmul(normed, gathered[1]).reshape(local_rows, HEADS, HEAD_DIM), cosine_table, sine_table
    ).astype(jnp.bfloat16)
    key_rot = rotate(
        matmul(normed, gathered[2]).reshape(local_rows, HEADS, HEAD_DIM), cosine_table, sine_table
    ).astype(jnp.bfloat16)
    value_heads = (
        matmul(normed, gathered[3]).astype(jnp.bfloat16).reshape(local_rows, HEADS, HEAD_DIM)
    )
    key_flat = key_rot.reshape(local_rows, model_width)
    value_flat = value_heads.reshape(local_rows, model_width)
    start_state = (
        jnp.full((HEADS, local_rows), NEG, jnp.float32),
        jnp.zeros((HEADS, local_rows), jnp.float32),
        jnp.zeros((local_rows, HEADS, HEAD_DIM), jnp.float32),
    )
    key_piece = lax.all_gather(key_flat, "blk", axis=0, tiled=True)
    value_piece = lax.all_gather(value_flat, "blk", axis=0, tiled=True)
    seg_piece = lax.all_gather(own_segments, "blk", axis=0, tiled=True)
    piece_rows = key_piece.shape[0]
    needed = (jnp.int32(0) <= own_start + local_rows - 1) & (
        seg_piece[piece_rows - 1] >= own_segments[0]
    )

    def attend_sweep(current):

        def attend_visit(number, partial_value):
            running_max, running_sum, weighted = partial_value
            offset = number * local_rows
            key_block = lax.dynamic_slice_in_dim(key_piece, offset, local_rows, 0).reshape(
                local_rows, HEADS, HEAD_DIM
            )
            value_block = lax.dynamic_slice_in_dim(value_piece, offset, local_rows, 0).reshape(
                local_rows, HEADS, HEAD_DIM
            )
            seg_block = lax.dynamic_slice_in_dim(seg_piece, offset, local_rows, 0)
            key_index = offset + jnp.arange(local_rows, dtype=jnp.int32)
            allowed = score_mask(own_segments, query_index, seg_block, key_index)
            scores = (
                jnp.einsum("qhd,khd->hqk", query_rot, key_block, preferred_element_type=jnp.float32)
                * SCALE
            )
            scores = jnp.where(allowed[None], scores, NEG)
            new_max = jnp.maximum(running_max, jnp.max(scores, axis=-1))
            probability = jnp.where(allowed[None], jnp.exp(scores - new_max[:, :, None]), 0.0)
            factor = jnp.exp(running_max - new_max)
            running_sum = running_sum * factor + jnp.sum(probability, axis=-1)
            weighted = weighted * factor.T[:, :, None] + jnp.einsum(
                "hqk,khd->qhd",
                probability.astype(jnp.bfloat16),
                value_block,
                preferred_element_type=jnp.float32,
            )
            return (new_max, running_sum, weighted)

        return lax.fori_loop(0, piece_rows // local_rows, attend_visit, current)

    final_max, final_sum, final_weighted = lax.cond(
        needed, attend_sweep, lambda unchanged: unchanged, start_state
    )
    attn_heads = (final_weighted / final_sum.T[:, :, None]).astype(jnp.bfloat16)
    lse_rows = (final_max + jnp.log(final_sum)).T
    attn_flat = attn_heads.reshape(local_rows, model_width)
    resid = x_float + matmul(attn_flat, gathered[4])
    inverse_two = lax.rsqrt(jnp.mean(resid * resid, axis=-1, keepdims=True) + EPS)
    normed_two = (resid * inverse_two * gain_two).astype(jnp.bfloat16)
    gate = matmul(normed_two, gathered[6])
    up_values = matmul(normed_two, gathered[7])
    hidden = (jax.nn.silu(gate) * up_values).astype(jnp.bfloat16)
    output = (resid + matmul(hidden, gathered[8])).astype(jnp.bfloat16)
    later = (
        lax.all_gather(attn_gain, ("dp", "blk"), axis=0, tiled=True),
        lax.all_gather(w_query, ("dp", "blk"), axis=0, tiled=True),
        lax.all_gather(w_key, ("dp", "blk"), axis=0, tiled=True),
        lax.all_gather(w_value, ("dp", "blk"), axis=0, tiled=True),
        lax.all_gather(w_out, ("dp", "blk"), axis=0, tiled=True),
        lax.all_gather(mlp_gain, ("dp", "blk"), axis=0, tiled=True),
        lax.all_gather(w_gate, ("dp", "blk"), axis=0, tiled=True),
        lax.all_gather(w_up, ("dp", "blk"), axis=0, tiled=True),
        lax.all_gather(w_down, ("dp", "blk"), axis=0, tiled=True),
    )
    grad_res = cotangent[0].astype(jnp.float32)
    grad_mlp = grad_res.astype(jnp.bfloat16)
    grad_down = left_product(hidden, grad_mlp)
    grad_hidden = right_product(grad_mlp, later[8])
    sigmoid_gate = jax.nn.sigmoid(gate)
    grad_gate_low = (
        grad_hidden * up_values * sigmoid_gate * (1.0 + gate * (1.0 - sigmoid_gate))
    ).astype(jnp.bfloat16)
    grad_up_low = (grad_hidden * gate * sigmoid_gate).astype(jnp.bfloat16)
    grad_gate_w = left_product(normed_two, grad_gate_low)
    grad_up_w = left_product(normed_two, grad_up_low)
    grad_normed_two = right_product(grad_gate_low, later[6]) + right_product(grad_up_low, later[7])
    grad_resid_norm, grad_gain_two = norm_back(grad_normed_two, resid, inverse_two, gain_two)
    grad_mid = grad_res + grad_resid_norm
    grad_branch = grad_mid.astype(jnp.bfloat16)
    grad_out_w = left_product(attn_flat, grad_branch)
    grad_attn = (
        right_product(grad_branch, later[4])
        .astype(jnp.bfloat16)
        .reshape(local_rows, HEADS, HEAD_DIM)
    )
    delta_rows = jnp.sum(grad_attn.astype(jnp.float32) * attn_heads.astype(jnp.float32), axis=-1)
    pack_length = local_rows * blocks
    empty_back = (
        jnp.zeros((local_rows, HEADS, HEAD_DIM), jnp.float32),
        jnp.zeros((pack_length, 2 * model_width), jnp.float32),
    )
    back_key_piece = lax.all_gather(key_flat, "blk", axis=0, tiled=True)
    back_value_piece = lax.all_gather(value_flat, "blk", axis=0, tiled=True)
    back_seg_piece = lax.all_gather(own_segments, "blk", axis=0, tiled=True)
    back_piece_rows = back_key_piece.shape[0]
    needed = (jnp.int32(0) <= own_start + local_rows - 1) & (
        back_seg_piece[back_piece_rows - 1] >= own_segments[0]
    )

    def back_sweep(current):

        def back_visit(number, partial_value):
            grad_query_acc, grad_pairs = partial_value
            offset = number * local_rows
            key_block = lax.dynamic_slice_in_dim(back_key_piece, offset, local_rows, 0).reshape(
                local_rows, HEADS, HEAD_DIM
            )
            value_block = lax.dynamic_slice_in_dim(back_value_piece, offset, local_rows, 0).reshape(
                local_rows, HEADS, HEAD_DIM
            )
            seg_block = lax.dynamic_slice_in_dim(back_seg_piece, offset, local_rows, 0)
            key_index = offset + jnp.arange(local_rows, dtype=jnp.int32)
            allowed = score_mask(own_segments, query_index, seg_block, key_index)
            part_query, part_key, part_value = block_grads(
                query_rot, grad_attn, lse_rows, delta_rows, allowed, key_block, value_block
            )
            new_rows = jnp.concatenate(
                [
                    part_key.reshape(local_rows, model_width),
                    part_value.reshape(local_rows, model_width),
                ],
                axis=1,
            )
            existing = lax.dynamic_slice_in_dim(grad_pairs, offset, local_rows, 0)
            grad_pairs = lax.dynamic_update_slice_in_dim(grad_pairs, existing + new_rows, offset, 0)
            return (grad_query_acc + part_query, grad_pairs)

        return lax.fori_loop(0, back_piece_rows // local_rows, back_visit, current)

    grad_query_rot, grad_pairs_all = lax.cond(
        needed, back_sweep, lambda unchanged: unchanged, empty_back
    )
    own_pairs = lax.psum_scatter(
        grad_pairs_all.astype(jnp.bfloat16), "blk", scatter_dimension=0, tiled=True
    ).astype(jnp.float32)
    grad_key_rot = own_pairs[:, :model_width].reshape(local_rows, HEADS, HEAD_DIM)
    grad_value_heads = own_pairs[:, model_width:].reshape(local_rows, HEADS, HEAD_DIM)
    grad_query_low = (
        rotate(grad_query_rot, cosine_table, -sine_table)
        .reshape(local_rows, model_width)
        .astype(jnp.bfloat16)
    )
    grad_key_low = (
        rotate(grad_key_rot, cosine_table, -sine_table)
        .reshape(local_rows, model_width)
        .astype(jnp.bfloat16)
    )
    grad_value_low = grad_value_heads.reshape(local_rows, model_width).astype(jnp.bfloat16)
    grad_query_w = left_product(normed, grad_query_low)
    grad_key_w = left_product(normed, grad_key_low)
    grad_value_w = left_product(normed, grad_value_low)
    grad_normed = (
        right_product(grad_query_low, later[1])
        + right_product(grad_key_low, later[2])
        + right_product(grad_value_low, later[3])
    )
    grad_x_norm, grad_gain_one = norm_back(grad_normed, x_float, inverse_one, gain_one)
    grad_input = (grad_mid + grad_x_norm).astype(jnp.bfloat16)
    summed = (
        lax.psum_scatter(grad_gain_one, ("dp", "blk"), scatter_dimension=0, tiled=True),
        lax.psum_scatter(grad_query_w, ("dp", "blk"), scatter_dimension=0, tiled=True),
        lax.psum_scatter(grad_key_w, ("dp", "blk"), scatter_dimension=0, tiled=True),
        lax.psum_scatter(grad_value_w, ("dp", "blk"), scatter_dimension=0, tiled=True),
        lax.psum_scatter(grad_out_w, ("dp", "blk"), scatter_dimension=0, tiled=True),
        lax.psum_scatter(grad_gain_two, ("dp", "blk"), scatter_dimension=0, tiled=True),
        lax.psum_scatter(grad_gate_w, ("dp", "blk"), scatter_dimension=0, tiled=True),
        lax.psum_scatter(grad_up_w, ("dp", "blk"), scatter_dimension=0, tiled=True),
        lax.psum_scatter(grad_down, ("dp", "blk"), scatter_dimension=0, tiled=True),
    )
    return (
        output.reshape(1, local_rows, model_width),
        grad_input.reshape(1, local_rows, model_width),
        summed[0],
        summed[1],
        summed[2],
        summed[3],
        summed[4],
        summed[5],
        summed[6],
        summed[7],
        summed[8],
    )


BF = jnp.bfloat16
F32 = jnp.float32
VMEM = pltpu.VMEM
LANES = 256


def ids():
    dp, blk = lax.axis_index("dp"), lax.axis_index("blk")
    return dp // 2, dp % 2, blk // 2, blk % 2, blk


def flip(bit, other):
    total = 0
    weight = 1
    while weight <= 2:
        own = (bit // weight) % 2
        total = total + weight * ((1 - own) if (other // weight) % 2 else own)
        weight *= 2
    return total


def exclusive(a, b):
    low, high = (a + b) % 2, (a // 2 + b // 2) % 2
    return low + 2 * high


def aligned(value, multiple):
    return pl.multiple_of(value, multiple)


def dot(a, b, ca=1, cb=0):
    return lax.dot_general(a, b, (((ca,), (cb,)), ((), ())), preferred_element_type=F32)


HBM = "hbm"


def call(kernel, outs, ins, anys=(), scratch=(), flops=0, nbytes=0, grant=24):
    def place(far):
        return pl.BlockSpec(memory_space=pltpu.MemorySpace.HBM if far else VMEM)

    return pl.pallas_call(
        kernel,
        out_shape=[jax.ShapeDtypeStruct(out[0], out[1]) for out in outs],
        in_specs=[place(i in anys) for i in range(len(ins))],
        out_specs=[place(len(out) > 2) for out in outs],
        scratch_shapes=list(scratch),
        compiler_params=pltpu.CompilerParams(vmem_limit_bytes=grant * 1024 * 1024),
        cost_estimate=pl.CostEstimate(flops=flops, bytes_accessed=nbytes, transcendentals=0),
    )(*ins)


def pair(low, first, second):
    (a, i), (b, j) = first, second
    left = a[:, 128 * (i // 2) : 128 * (i // 2) + 128]
    right = b[:, 128 * (j // 2) : 128 * (j // 2) + 128]
    left = pltpu.roll(left, 64, 1) if i % 2 else left
    right = right if j % 2 else pltpu.roll(right, 64, 1)
    return jnp.where(low, left, right)


def pairs(low, blocks):
    return jnp.concatenate([pair(low, blocks[i], blocks[i + 1]) for i in range(0, len(blocks), 2)], axis=1)


def prepare_kernel(gain1, gain2, place, wq_h, wk_h, wv_h, wg_h, wu_h, x_h, r0_o, r1_o, r2_o, r3_o, x_o,
                   wq, wk, wv, wg, wu, order, sems):
    z, x, y, c, b = ids()
    far, near = (wq_h, wk_h, wv_h, wg_h, wu_h), (wq, wk, wv, wg, wu)
    copies = [pltpu.make_async_copy(a, d, sems.at[i]) for i, (a, d) in enumerate(zip(far, near))]
    copies.append(pltpu.make_async_copy(x_h, x_o.at[pl.ds(0, 256)], sems.at[5]))
    for copy in copies:
        copy.start()
    for copy in copies[:5]:
        copy.wait()
    low = lax.broadcasted_iota(jnp.int32, (wq.shape[0], 128), 1) < 64
    q, k, v, gate, up = (ref[...].astype(F32) for ref in (wq, wk, wv, wg, wu))
    rows = wq.shape[0]
    here = lax.broadcasted_iota(jnp.int32, (rows, rows), 0) == lax.broadcasted_iota(jnp.int32, (rows, rows), 1)
    lane = lax.broadcasted_iota(jnp.int32, (rows, 128), 1)
    g = jnp.zeros((rows, 128), F32)
    for at, ref in ((64, gain1), (65, gain2)):
        row = jnp.broadcast_to(ref[...].astype(F32), (rows, rows))
        g = jnp.where(lane == at, jnp.sum(jnp.where(here, row, 0.0), axis=1, keepdims=True), g)
    at = jnp.broadcast_to(place[...], (16, 256)).astype(F32)
    tens = jnp.floor(at * (1.0 / 32))
    x_o[256:272, :] = jnp.concatenate([tens, at - 32.0 * tens, jnp.zeros_like(at)], axis=1).astype(BF)
    for j in range(4):
        blocks = [(w, 3 * j + t) for w in (q, k, v) for t in range(3)] + [(g, 1)]
        order[flip(b, j)] = pairs(low, blocks).astype(BF)
        wide = pairs(low, [(w, 4 * i + j) for w in (gate, up) for i in range(8)])
        rest = jnp.concatenate([wide[8 * t : 8 * t + 8, 768:1024] for t in range(3)], axis=1)
        x_o[272 + 32 * j : 304 + 32 * j, :] = jnp.concatenate([wide[:, 0:768], rest], axis=0).astype(BF)
    for k, out in enumerate((r0_o, r1_o, r2_o, r3_o)):
        out[...] = order[k]
    copies[5].wait()


def prepare(tokens, place, wq, wk, wv, gain1, gain2, wg, wu):
    outs = [((24, 640), BF)] * 4 + [((400, 768), BF)]
    scratch = [*[VMEM((24, 768), BF)] * 3, *[VMEM((24, 2048), BF)] * 2, VMEM((4, 24, 640), BF),
               pltpu.SemaphoreType.DMA((7,))]
    return call(prepare_kernel, outs, [gain1, gain2, place, wq, wk, wv, wg, wu, tokens], anys=range(3, 9), scratch=scratch,
                flops=1_000_000, nbytes=1_000_000, grant=60)


def columns_kernel(r0, r1, r2, r3, out, rows):
    z, x, y, c, b = ids()
    for k, piece in enumerate((r0, r1, r2, r3)):
        rows[pl.ds(aligned(flip(b, k) * 24, 24), 24), :] = piece[...].astype(F32)
    out[...] = rows[...].astype(BF)


def columns(pieces):
    (out,) = call(columns_kernel, [((96, 640), BF)], pieces, scratch=[VMEM((96, 640), F32)], flops=1_000_000, nbytes=300_000)
    return out


def units_kernel(x0, x1, x2, x3, gate_o, up_o, rows):
    z, x, y, c, b = ids()
    for k, piece in enumerate((x0, x1, x2, x3)):
        part = piece[pl.ds(aligned(272 + 32 * b, 16), 32), :].astype(F32)
        rest = jnp.concatenate([part[24:32, 256 * t : 256 * t + 256] for t in range(3)], axis=0)
        rows[pl.ds(aligned(flip(b, k) * 24, 24), 24), :] = jnp.concatenate([part[0:24], rest], axis=1)
    gate_o[...] = rows[:, 0:512].astype(BF)
    up_o[...] = rows[:, 512:1024].astype(BF)


def units(xs):
    outs = [((96, 512), BF)] * 2
    return call(units_kernel, outs, xs, scratch=[VMEM((96, 1024), F32)], flops=1_000_000, nbytes=3_000_000)


def finish_kernel(h0, h1, h2, h3, u0, u1, u2, u3, q_o, k_o, v_o, gate_o, up_o, gain1_o, gain2_o, heads, units):
    z, x, y, c, b = ids()
    for k in range(4):
        heads[k] = (h0, h1, h2, h3)[k][...]
        units[k] = (u0, u1, u2, u3)[k][...]
    low = lax.broadcasted_iota(jnp.int32, (heads.shape[1], 128), 1) < 64
    parts = [heads[flip(b, j)].astype(F32) for j in range(4)]
    for t, out in enumerate((q_o, k_o, v_o)):
        out[...] = pairs(low, [(parts[m // 3], 3 * t + m % 3) for m in range(12)])
    total = parts[0][:, 512:640] + parts[1][:, 512:640] + parts[2][:, 512:640] + parts[3][:, 512:640]
    rows = heads.shape[1]
    here = lax.broadcasted_iota(jnp.int32, (rows, rows), 0) == lax.broadcasted_iota(jnp.int32, (rows, rows), 1)
    for at, out in ((64, gain1_o), (65, gain2_o)):
        out[...] = jnp.sum(jnp.where(here, jnp.broadcast_to(total[:, at : at + 1], (rows, rows)), 0.0), axis=0, keepdims=True)
    parts = [units[flip(b, j)].astype(F32) for j in range(4)]
    for t, out in enumerate((gate_o, up_o)):
        out[...] = pairs(low, [(parts[m % 4], 8 * t + m // 4) for m in range(32)])


def finish(heads, units):
    outs = [((24, 768), F32)] * 3 + [((24, 2048), F32)] * 2 + [((1, 24), F32)] * 2
    return call(finish_kernel, outs, [*heads, *units], scratch=[VMEM((4, 24, 640), BF), VMEM((4, 24, 1024), BF)],
                flops=1_000_000, nbytes=2_000_000)


def tables_kernel(x0, x1, x2, x3, table_o, rows_o, marks, table, rows, sems, out_sems):
    z, x, y, c, b = ids()
    copies = [
        pltpu.make_async_copy(piece.at[pl.ds(256, 16)], marks.at[k], sems.at[k])
        for k, piece in enumerate((x0, x1, x2, x3))
    ]
    for copy in copies:
        copy.start()
    for copy in copies:
        copy.wait()
    lane = lax.broadcasted_iota(jnp.int32, (256, 128), 1)
    inverse = jnp.exp((lane % 32).astype(F32) * (-math.log(10000.0) / 32))
    for k in range(4):
        own = marks[k].astype(F32)
        place = (32.0 * own[:, 0:256] + own[:, 256:512])[0:1]
        slot = lax.broadcasted_iota(jnp.int32, (8, 256), 1) + 256 * flip(b, k)
        rows[k] = slot.astype(F32) - jnp.broadcast_to(place, (8, 256))
        angles = jnp.broadcast_to(place, (128, 256)).T * inverse
        sine = jnp.sin(angles)
        table[k] = jnp.where(lane < 64, jnp.cos(angles), jnp.where(lane < 96, -sine, sine))
    leaving = [
        pltpu.make_async_copy(ref, out, out_sems.at[i])
        for i, (ref, out) in enumerate(((table, table_o), (rows, rows_o)))
    ]
    for copy in leaving:
        copy.start()
    for copy in leaving:
        copy.wait()


def tables(xs):
    outs = [((4, 256, 128), F32, HBM), ((4, 8, 256), F32, HBM)]
    scratch = [
        VMEM((4, 16, 768), BF), VMEM((4, 256, 128), F32), VMEM((4, 8, 256), F32),
        pltpu.SemaphoreType.DMA((4,)), pltpu.SemaphoreType.DMA((2,)),
    ]
    return call(tables_kernel, outs, xs, anys=range(4), scratch=scratch, flops=10_000_000, nbytes=3_000_000)


def turns(table, low):
    turned = pltpu.roll(table, 64, 1)
    return jnp.where(low, table, turned), jnp.where(low, turned, table)


def half_swap(tile, lane):
    return jnp.where(lane % 64 < 32, pltpu.roll(tile, 96, 1), pltpu.roll(tile, 32, 1))


def pack(block):
    low = lax.broadcasted_iota(jnp.int32, (128, 128), 1) < 64
    last = block[:, 128:256].astype(F32)
    last = jnp.where(low, last[0:128], pltpu.roll(last[128:256], 64, 1))
    return jnp.concatenate([block[:, 0:128].astype(BF), last.astype(BF)], axis=0)


def unpack(block):
    low = lax.broadcasted_iota(jnp.int32, (128, 128), 1) < 64
    last = block[256:384].astype(F32)
    zero = jnp.zeros_like(last)
    last = jnp.concatenate([jnp.where(low, last, zero), jnp.where(low, pltpu.roll(last, 64, 1), zero)], axis=0)
    return jnp.concatenate([block[0:256], last.astype(BF)], axis=1)


def attend_kernel(x0, x1, x2, x3, wa, wb, table_h, rows_h,
                  qkva_o, n_o, w_o, lse_o, gains_o, a0_o, a1_o, a2_o, a3_o,
                  xs, w, qkva, n, lse, table, begins, a0, a1, a2, a3, sems, out_sems):
    z, x, y, c, b = ids()
    q, k, v, attn = (qkva.at[i] for i in range(4))
    copies = []
    for xr, piece in enumerate((wa, wb)):
        for zr in range(4):
            dp = 2 * flip(z, zr) + flip(x, xr)
            copies.append(pltpu.make_async_copy(
                piece.at[zr], w.at[pl.ds(aligned(dp * 96, 96), 96)], sems.at[4 * xr + zr]))
    copies.append(pltpu.make_async_copy(table_h, table, sems.at[8]))
    for kk, piece in enumerate((x0, x1, x2, x3)):
        copies.append(pltpu.make_async_copy(piece.at[pl.ds(0, 272)], xs.at[kk], sems.at[9 + kk]))
    copies.append(pltpu.make_async_copy(rows_h, begins, sems.at[13]))
    for copy in copies:
        copy.start()
    for copy in copies[:9]:
        copy.wait()
    leaving = [pltpu.make_async_copy(w, w_o, out_sems.at[0])]
    leaving[0].start()
    last = w[:, 512:640].astype(F32).T
    gains = last[64:72, :]
    gains_o[...] = gains
    gain = gains[0:1, :]
    lane = lax.broadcasted_iota(jnp.int32, (256, 128), 1)
    low = lane < 64
    for kk in range(4):
        rows = pl.ds(aligned(flip(b, kk) * 256, 256), 256)
        copies[9 + kk].wait()
        values = xs[kk, 0:256, :].astype(F32)
        inverse = lax.rsqrt(jnp.mean(values * values, axis=-1, keepdims=True) + EPS)
        normed = (values * inverse * gain).astype(BF)
        n[rows, :] = normed
        qkv = dot(normed, w[...])
        cosine, sine = turns(table[kk], low)
        tiles = []
        for t in range(3):
            tile = qkv[:, 128 * t : 128 * t + 128]
            tiles.append(tile * cosine + half_swap(tile, lane) * sine)
        r1, r2 = pltpu.roll(tiles[1], 64, 1), pltpu.roll(tiles[2], 64, 1)
        zero = jnp.zeros_like(r1)
        q[rows, 0:128] = tiles[0].astype(BF)
        q[rows, 128:256] = jnp.where(low, tiles[1], zero).astype(BF)
        k[rows, 0:128] = jnp.where(low, r1, r2).astype(BF)
        k[rows, 128:256] = jnp.where(low, r2, zero).astype(BF)
        v[rows, 0:128] = qkv[:, 384:512].astype(BF)
        v[rows, 128:256] = jnp.where(low, qkv[:, 512:640], zero).astype(BF)
    for at, (ref, out) in enumerate(((n, n_o), (qkva.at[pl.ds(0, 3)], qkva_o.at[pl.ds(0, 3)]))):
        leaving.append(pltpu.make_async_copy(ref, out, out_sems.at[3 + at]))
        leaving[-1].start()
    copies[13].wait()
    head = lax.broadcasted_iota(jnp.int32, (256, LANES), 1) // 64
    for i in range(4):
        width = 256 * (i + 1)
        query = q[256 * i : 256 * i + 256, :]
        begin = jnp.broadcast_to(begins[flip(b, i)][0:1, :], (128, 256)).T[:, 0:1]
        column = lax.broadcasted_iota(jnp.int32, (256, width), 1)
        row = lax.broadcasted_iota(jnp.int32, (256, width), 0) + 256 * i
        allowed = (column <= row) & (column.astype(F32) >= begin)
        total = jnp.zeros((256, LANES), F32)
        stats = jnp.zeros((256, 128), F32)
        for h in range(3):
            mine = jnp.where(head == h, query, jnp.zeros_like(query))
            scores = dot(mine, k[0:width, :], 1, 1) * SCALE
            scores = jnp.where(allowed, scores, NEG)
            top = jnp.max(scores, axis=-1, keepdims=True)
            weight = jnp.exp(scores - top)
            norm = jnp.sum(weight, axis=-1, keepdims=True)
            mixed = dot(weight.astype(BF), v[0:width, :]) / norm
            total = jnp.where(head == h, mixed, total)
            stats = jnp.where(lane == h, top + jnp.log(norm), stats)
        attn[256 * i : 256 * i + 256, :] = total.astype(BF)
        lse[:, 256 * i : 256 * i + 256] = stats.T[0:8]
    for at, (ref, out) in enumerate(((attn, qkva_o.at[3]), (lse, lse_o))):
        leaving.append(pltpu.make_async_copy(ref, out, out_sems.at[1 + at]))
        leaving[-1].start()
    for kk, (out, far) in enumerate(((a0, a0_o), (a1, a1_o), (a2, a2_o), (a3, a3_o))):
        for t in range(2):
            out[t] = pack(attn[pl.ds(aligned(flip(flip(b, kk), 2 * t) * 256, 256), 256), :])
        leaving.append(pltpu.make_async_copy(out, far, out_sems.at[5 + kk]))
        leaving[-1].start()
    for copy in leaving:
        copy.wait()


def attend(xs, wa, wb, tabs):
    outs = [
        ((4, 1024, LANES), BF, HBM), ((1024, 768), BF, HBM), ((768, 640), BF, HBM),
        ((8, 1024), F32, HBM), ((8, 768), F32), *[((2, 384, 128), BF, HBM)] * 4,
    ]
    return call(
        attend_kernel, outs, [*xs, wa, wb, *tabs], anys=range(8), grant=60,
        scratch=[
            VMEM((4, 272, 768), BF), VMEM((768, 640), BF), VMEM((4, 1024, LANES), BF), VMEM((1024, 768), BF),
            VMEM((8, 1024), F32), VMEM((4, 256, 128), F32), VMEM((4, 8, 256), F32),
            *[VMEM((2, 384, 128), BF)] * 4, pltpu.SemaphoreType.DMA((14,)), pltpu.SemaphoreType.DMA((9,)),
        ],
        flops=1000, nbytes=1000,
    )


def out_kernel(a0, a1, a2, a3, x0, x2, gains, own, other, resid_o, n_o, wo_o, stack_o, wide):
    z, x, y, c, b = ids()
    for xy in range(4):
        for zr in range(4):
            chip = 8 * flip(z, zr) + 4 * flip(x, xy // 2) + 2 * flip(y, xy % 2)
            for core, pieces in enumerate((own, other)):
                at = aligned((chip + flip(c, core)) * 24, 24)
                wide[pl.ds(at, 24), :] = pieces[xy, zr].astype(F32)
    wo_o[...] = wide[...].astype(BF)
    for t, band in enumerate((x0, x2)):
        total = band[0:256, :].astype(F32)
        for k, piece in enumerate((a0, a1, a2, a3)):
            heads = unpack(piece[t])
            if t == 0:
                stack_o[k] = heads
            rows = pl.ds(aligned(flip(b, k) * 192, 192), 192)
            total += dot(heads[:, 0:192], wo_o[rows, :])
        if t == 0:
            resid_o[...] = total
        inverse = lax.rsqrt(jnp.mean(total * total, axis=-1, keepdims=True) + EPS)
        n_o[t] = (total * inverse * gains[1:2, :]).astype(BF)


def project(a, x0, x2, gains, own, other):
    outs = [((256, 768), F32), ((2, 256, 768), BF), ((768, 768), BF), ((4, 256, LANES), BF)]
    return call(out_kernel, outs, [*a, x0, x2, gains, own, other], scratch=[VMEM((768, 768), F32)],
                flops=800_000_000, nbytes=4_000_000)


def hidden_kernel(n02, n13, ct0, ct1, ct2, ct3, g_near, g_far, u_near, u_far, d_near, d_far,
                  n_o, ct_o, hid_o, dg_o, du_o, wgu_o, wd_o, sems):
    z, x, y, c, b = ids()
    copies = []
    for xr, (g, u, d) in enumerate(((g_near, u_near, d_near), (g_far, u_far, d_far))):
        for zr in range(4):
            dp = 2 * flip(z, zr) + flip(x, xr)
            at = 4 * xr + zr
            for i, w in enumerate((g, u)):
                copies.append(pltpu.make_async_copy(
                    w.at[zr], wgu_o.at[pl.ds(aligned(dp * 96, 96), 96), pl.ds(512 * i, 512)], sems.at[2 * i, at]))
            copies.append(pltpu.make_async_copy(
                d.at[zr, pl.ds(0, 64)], wd_o.at[pl.ds(aligned(dp * 64, 64), 64)], sems.at[1, at]))
    for copy in copies:
        copy.start()
    for k in range(4):
        n_o[256 * k : 256 * k + 256, :] = (n02, n13)[k % 2][k // 2]
        ct_o[256 * k : 256 * k + 256, :] = (ct0, ct1, ct2, ct3)[k][...]
    for copy in copies:
        copy.wait()
    for k in range(4):
        rows = slice(256 * k, 256 * k + 256)
        normed, cot = n_o[rows, :], ct_o[rows, :]
        for j in range(2):
            cols = slice(256 * j, 256 * j + 256)
            gate = dot(normed, wgu_o[:, 256 * j : 256 * j + 256])
            up = dot(normed, wgu_o[:, 512 + 256 * j : 768 + 256 * j])
            back = dot(cot, wd_o[cols, :], 1, 1)
            sig = 1.0 / (1.0 + jnp.exp(-gate))
            silu = gate * sig
            hid_o[rows, cols] = (silu * up).astype(BF)
            dg_o[rows, cols] = (back * up * sig * (1.0 + gate * (1.0 - sig))).astype(BF)
            du_o[rows, cols] = (back * silu).astype(BF)


def hidden_and_back(n, ct, pieces):
    outs = [((1024, 768), BF)] * 2 + [((1024, 512), BF)] * 3 + [((768, 1024), BF), ((512, 768), BF)]
    return call(
        hidden_kernel, outs, [*n, *ct, *pieces], anys=range(6, 12),
        scratch=[pltpu.SemaphoreType.DMA((3, 8))], flops=2_500_000_000, nbytes=8_000_000,
    )


def normed_back_kernel(dg, du, wgu, own_o, far_o, send_o):
    for k in range(4):
        rows = slice(256 * k, 256 * k + 256)
        grad = dot(dg[rows, :], wgu[:, 0:512], 1, 1) + dot(du[rows, :], wgu[:, 512:1024], 1, 1)
        if k == 0:
            own_o[...] = grad
        elif k == 2:
            far_o[...] = grad
        else:
            send_o[k // 2] = grad.astype(BF)


def normed_back(dg, du, wgu):
    outs = [((256, 768), F32)] * 2 + [((2, 256, 768), BF)]
    return call(normed_back_kernel, outs, [dg, du, wgu], flops=1_600_000_000, nbytes=6_000_000)


def store_by_x(grad, rows, cols, keep_o, send_o, z, x):
    for zp in range(4):
        at = 2 * rows * zp
        low, high = grad[at : at + rows], grad[at + rows : at + 2 * rows]
        keep_o[flip(z, zp), :, cols] = jnp.where(x == 0, low, high).astype(BF)
        send_o[flip(z, zp), :, cols] = jnp.where(x == 0, high, low).astype(BF)


def ff_grads_kernel(n, ct, hid, dg, du, gu_keep_o, gu_send_o, d_keep_o, d_send_o):
    z, x, y, c, b = ids()
    normed = n[...].T
    for j in range(4):
        cols = slice(256 * j, 256 * j + 256)
        part = (dg, du)[j // 2][:, 256 * (j % 2) : 256 * (j % 2) + 256]
        store_by_x(dot(normed, part), 96, cols, gu_keep_o, gu_send_o, z, x)
    hidden = hid[...].T
    for j in range(3):
        cols = slice(256 * j, 256 * j + 256)
        store_by_x(dot(hidden, ct[:, cols]), 64, cols, d_keep_o, d_send_o, z, x)


def ff_grads(n, ct, hid, dg, du):
    outs = [((4, 96, 1024), BF)] * 2 + [((4, 64, 768), BF)] * 2
    return call(ff_grads_kernel, outs, [n, ct, hid, dg, du], flops=2_400_000_000, nbytes=10_000_000)


def mid_kernel(gn_own, gn_in, resid, ct0, gains, wo, out_own, out_far, out_in, here_o, there_o, mid_o, branch_o, g0_o, g1_o, g2_o, g3_o, gain_o):
    z, x, y, c, b = ids()
    here_o[...] = out_own[...] + out_in[0].astype(F32)
    there_o[...] = (out_far[...] + out_in[1].astype(F32)).astype(BF)
    grad = gn_own[...] + gn_in[...].astype(F32)
    values = resid[...]
    inverse = lax.rsqrt(jnp.mean(values * values, axis=-1, keepdims=True) + EPS)
    unit = values * inverse
    scaled = grad * gains[1:2, :]
    gain_o[...] = jnp.broadcast_to(jnp.sum(grad * unit, axis=0, keepdims=True), gain_o.shape)
    mid = ct0[...].astype(F32) + inverse * (
        scaled - unit * jnp.mean(scaled * unit, axis=-1, keepdims=True)
    )
    mid_o[...] = mid
    branch = mid.astype(BF)
    branch_o[...] = branch
    pad = jnp.zeros((256, LANES - 192), F32)
    for k in range(4):
        rows = pl.ds(aligned(flip(b, k) * 192, 192), 192)
        part = dot(branch, wo[rows, :], 1, 1)
        (g0_o, g1_o, g2_o, g3_o)[k][...] = pack(jnp.concatenate([part, pad], axis=1))


def mid_back(gn_own, gn_in, resid, ct0, gains, wo, out):
    outs = [((256, 768), F32), ((256, 768), BF), ((256, 768), F32), ((256, 768), BF), *[((384, 128), BF)] * 4, ((8, 768), F32)]
    return call(mid_kernel, outs, [gn_own, gn_in, resid, ct0, gains, wo, *out], flops=400_000_000, nbytes=5_000_000)


def out_grads_kernel(stack, branch, keep_o, send_o, wide):
    z, x, y, c, b = ids()
    for k in range(4):
        part = dot(stack[k].T, branch[...])[0:192]
        wide[pl.ds(aligned(exclusive(flip(b, k), z) * 192, 192), 192), :] = part
    for cr, out in enumerate((keep_o, send_o)):
        for yr in range(2):
            for xr in range(2):
                for zr in range(4):
                    at = 4 * (flip(x, xr) % 2) + 2 * (flip(y, yr) % 2) + flip(c, cr) % 2 + 8 * zr
                    out[xr, yr, zr] = wide[pl.ds(aligned(at * 24, 24), 24), :].astype(BF)


def out_grads(stack, branch):
    outs = [((2, 2, 4, 24, 768), BF)] * 2
    return call(out_grads_kernel, outs, [stack, branch], scratch=[VMEM((768, 768), F32)],
                flops=400_000_000, nbytes=3_000_000)


def down_kernel(hid, wd, resid, own_o, far_o, send_o):
    for k in range(4):
        part = dot(hid[256 * k : 256 * k + 256, :], wd[...])
        if k == 0:
            own_o[...] = resid[...] + part
        elif k == 2:
            far_o[...] = part
        else:
            send_o[k // 2] = part.astype(BF)


def down(hid, wd, resid):
    outs = [((256, 768), F32)] * 2 + [((2, 256, 768), BF)]
    return call(down_kernel, outs, [hid, wd, resid], flops=800_000_000, nbytes=5_000_000)


def attend_back_kernel(qkva_h, n_h, w_h, lse_h, table_h, start_h, x0, x1, x2, x3, g0, g1, g2, g3, gain2_h,
                       keep_h, send_h, gk0_h, gk1_h, gs_h,
                       qkva, n, w, lse, table, start, xs, packed, do, dq, dk, dv, grads, wide, gain2,
                       keep_o, send_o, gk0_o, gk1_o, gs_o, sems, out_sems):
    z, x, y, c, b = ids()
    q, k, v, attn = (qkva.at[i] for i in range(4))
    first = [
        pltpu.make_async_copy(a, d, sems.at[i])
        for i, (a, d) in enumerate(((lse_h, lse), (start_h, start), (qkva_h, qkva)))
    ] + [pltpu.make_async_copy(a, packed.at[i], sems.at[3 + i]) for i, a in enumerate((g0, g1, g2, g3))]
    rest = [
        pltpu.make_async_copy(a, d, sems.at[7 + i])
        for i, (a, d) in enumerate(((table_h, table), (n_h, n), (w_h, w), (gain2_h, gain2)))
    ] + [pltpu.make_async_copy(a.at[pl.ds(0, 272)], xs.at[i], sems.at[11 + i]) for i, a in enumerate((x0, x1, x2, x3))]
    for copy in first + rest:
        copy.start()
    dk[...] = jnp.zeros_like(dk)
    dv[...] = jnp.zeros_like(dv)
    for copy in first:
        copy.wait()
    for i in range(4):
        do[pl.ds(aligned(flip(b, i) * 256, 256), 256), :] = unpack(packed[i])
    head = lax.broadcasted_iota(jnp.int32, (256, LANES), 1) // 64
    lane = lax.broadcasted_iota(jnp.int32, (256, 128), 1)
    for i in range(4):
        width = 256 * (i + 1)
        rows = slice(256 * i, 256 * i + 256)
        query, out_grad = q[rows, :] * SCALE, do[rows, :]
        product = out_grad.astype(F32) * attn[rows, :].astype(F32)
        delta = jnp.zeros((256, 128), F32)
        for h in range(3):
            delta = jnp.where(
                lane == h, jnp.sum(jnp.where(head == h, product, 0.0), axis=-1, keepdims=True), delta)
        delta = delta.T
        begin = start[flip(b, i)][0:1, :]
        key = lax.broadcasted_iota(jnp.int32, (width, 256), 0)
        slot = lax.broadcasted_iota(jnp.int32, (width, 256), 1) + 256 * i
        allowed = (key <= slot) & (key.astype(F32) >= begin)
        probs, dscores = [], []
        mine = [jnp.where(head == h, query, jnp.zeros_like(query)) for h in range(3)]
        ours = [jnp.where(head == h, out_grad, jnp.zeros_like(out_grad)) for h in range(3)]
        for h in range(3):
            scores = dot(k[0:width, :], mine[h], 1, 1)
            prob = jnp.exp(jnp.where(allowed, scores - lse[h : h + 1, rows], NEG))
            dprob = dot(v[0:width, :], ours[h], 1, 1)
            probs.append(prob.astype(BF))
            dscores.append((prob * (dprob - delta[h : h + 1, :])).astype(BF))
        dv[0:width, :] += dot(jnp.concatenate(probs, axis=1), jnp.concatenate(ours, axis=0))
        dk[0:width, :] += dot(jnp.concatenate(dscores, axis=1), jnp.concatenate(mine, axis=0))
        total = jnp.zeros((256, LANES), F32)
        for h in range(3):
            total = jnp.where(head == h, dot(dscores[h], k[0:width, :], 0, 0), total)
        dq[rows, :] = total
    for copy in rest:
        copy.wait()
    low = lane < 64
    zero = jnp.zeros((256, 128), F32)
    for i in range(4):
        rows = slice(256 * i, 256 * i + 256)
        cosine, sine = turns(table[flip(b, i)], low)
        turned = []
        for ref, factor in ((dq, SCALE), (dk, 1.0)):
            for t in range(2):
                tile = ref[rows, 128 * t : 128 * t + 128] * factor
                turned.append(tile * cosine - half_swap(tile, lane) * sine)
        k0, k1 = pltpu.roll(turned[2], 64, 1), pltpu.roll(turned[3], 64, 1)
        grads[rows, 0:128] = turned[0].astype(BF)
        grads[rows, 128:256] = jnp.where(low, turned[1], k0).astype(BF)
        grads[rows, 256:384] = jnp.where(low, k0, k1).astype(BF)
        grads[rows, 384:512] = dv[rows, 0:128].astype(BF)
        grads[rows, 512:640] = jnp.where(low, dv[rows, 128:256], zero).astype(BF)
    leaving = []

    def leave(ref, out):
        leaving.append(pltpu.make_async_copy(ref, out, out_sems.at[len(leaving)]))
        leaving[-1].start()

    gain_sum = jnp.zeros((1, 768), F32)
    for kk in range(4):
        rows = pl.ds(aligned(flip(b, kk) * 256, 256), 256)
        grad = dot(grads[rows, :], w[...], 1, 1)
        values = xs[kk, 0:256, :].astype(F32)
        inverse = lax.rsqrt(jnp.mean(values * values, axis=-1, keepdims=True) + EPS)
        gain_sum += jnp.sum(grad * (values * inverse), axis=0, keepdims=True)
        if kk % 2:
            gs_o[kk // 2] = grad.astype(BF)
        else:
            (gk0_o, gk1_o)[kk // 2][...] = grad.astype(BF)
    for ref, out in ((gs_o, gs_h), (gk0_o, gk0_h), (gk1_o, gk1_h)):
        leave(ref, out)
    row_at = lax.broadcasted_iota(jnp.int32, (128, 768), 0)
    gain_rows = jnp.where(row_at == 64, gain_sum, jnp.where(row_at == 65, gain2[0:1, :], 0.0))
    gain_columns = gain_rows.T
    normed = n[...].T
    for j in range(5):
        cols = slice(128 * j, 128 * j + 128)
        part = dot(normed, grads[:, cols])
        if j == 4:
            part = part + gain_columns
        wide[:, cols] = part
    for xr, (ref, out) in ((1, (send_o, send_h)), (0, (keep_o, keep_h))):
        for zr in range(4):
            dp = 2 * flip(z, zr) + flip(x, xr)
            ref[zr] = wide[pl.ds(aligned(dp * 96, 96), 96), :].astype(BF)
        leave(ref, out)
    for copy in leaving:
        copy.wait()


def attend_back(saved, tabs, xs, g, gain2):
    outs = [((4, 96, 640), BF, HBM)] * 2 + [((256, 768), BF, HBM)] * 2 + [((2, 256, 768), BF, HBM)]
    return call(
        attend_back_kernel, outs, [*saved, *tabs, *xs, *g, gain2], anys=range(15), grant=60,
        scratch=[
            VMEM((4, 1024, LANES), BF), VMEM((1024, 768), BF), VMEM((768, 640), BF),
            VMEM((8, 1024), F32), VMEM((4, 256, 128), F32), VMEM((4, 8, 256), F32),
            VMEM((4, 272, 768), BF), VMEM((4, 384, 128), BF), VMEM((1024, LANES), BF), *[VMEM((1024, LANES), F32)] * 3,
            VMEM((1024, 640), BF), VMEM((768, 640), F32), VMEM((8, 768), F32),
            *[VMEM(out[0], out[1]) for out in outs], pltpu.SemaphoreType.DMA((15,)), pltpu.SemaphoreType.DMA((5,)),
        ],
        flops=1000, nbytes=1000,
    )


def tail_kernel(kept, arrived, o_kept, o_arrived, t0_o, t1_o, t2_o, t3_o):
    for k, out in enumerate((t0_o, t1_o, t2_o, t3_o)):
        out[0:96, :] = (kept[k].astype(F32) + arrived[k].astype(F32)).astype(BF)
        rows = o_kept[k].astype(F32) + o_arrived[k].astype(F32)
        rest = [rows[8 * t : 8 * t + 8, 640:768] for t in range(3)] + [jnp.zeros((8, 256), F32)]
        out[96:128, :] = jnp.concatenate([rows[:, 0:640], jnp.concatenate(rest, axis=1)], axis=0).astype(BF)


def tail_blocks(kept, arrived, o_kept, o_arrived):
    outs = [((128, 640), BF)] * 4
    return call(tail_kernel, outs, [kept, arrived, o_kept, o_arrived], flops=1_000_000, nbytes=2_000_000)


def last_kernel(kept, arrived, mid, x0, gains, out):
    grad = kept[...].astype(F32) + arrived[...].astype(F32)
    values = x0[0:256, :].astype(F32)
    inverse = lax.rsqrt(jnp.mean(values * values, axis=-1, keepdims=True) + EPS)
    unit = values * inverse
    scaled = grad * gains[0:1, :]
    out[...] = (
        mid[...] + inverse * (scaled - unit * jnp.mean(scaled * unit, axis=-1, keepdims=True))
    ).astype(BF)


def swap_z(v, k):
    return lax.ppermute(v, "dp", [(i, i ^ (2 * k)) for i in range(8)])


def swap_x(v):
    return lax.ppermute(v, "dp", [(i, i ^ 1) for i in range(8)])


def swap_b(v, k):
    return lax.ppermute(v, "blk", [(i, i ^ k) for i in range(4)])


def swap_core(v):
    return swap_b(v, 1)


def swap_y(v):
    return swap_b(v, 2)


def after(value, *tokens):
    return lax.optimization_barrier((value, tokens))[0]


def stack_z(v):
    return jnp.stack([v] + [swap_z(v, k) for k in (1, 2, 3)])


def by_index(four, bits):
    one, two = bits % 2 == 1, bits // 2 == 1
    a, b, c, d = four
    a, b, c, d = jnp.where(one, b, a), jnp.where(one, a, b), jnp.where(one, d, c), jnp.where(one, c, d)
    return [jnp.where(two, c, a), jnp.where(two, d, b), jnp.where(two, a, c), jnp.where(two, b, d)]


def sum_z(v):
    terms = [v[0]] + [swap_z(v[k], k) for k in (1, 2, 3)]
    return sum(term.astype(F32) for term in terms)


def halve_z(v, far):
    first = [added(v[k], far[k]) for k in range(2)]
    return first[0].astype(F32) + swap_z(first[1], 1).astype(F32)


def added(kept, arrived):
    return (kept.astype(F32) + arrived.astype(F32)).astype(BF)


def fast_shards(tokens, segments, positions, cotangent, attn_gain, w_query, w_key, w_value, w_out,
                mlp_gain, w_gate, w_up, w_down):
    z, x, y, c, b = ids()
    first = c == 0
    x0 = tokens[0]
    ct0 = cotangent[0]

    *parts, x0 = prepare(x0, positions, w_query, w_key, w_value, attn_gain[None], mlp_gain[None], w_gate, w_up)
    do_own = jnp.concatenate([w_down, w_out], axis=0)
    do_z = [do_own] + [swap_z(do_own, k) for k in (1, 2, 3)]
    from_blk = [parts[0]] + [swap_b(parts[k], k) for k in (1, 2, 3)]

    from_blk, do_z, x0 = lax.optimization_barrier((from_blk, do_z, x0))
    qkv_own, x0, do_z = lax.optimization_barrier((columns(from_blk), x0, do_z))
    qkv_z = [qkv_own] + [swap_z(qkv_own, k) for k in (1, 2, 3)]
    do_near = jnp.stack(do_z)
    do_far = swap_x(do_near)
    x2 = swap_y(x0)

    qkv_z, x0, do_far = lax.optimization_barrier((qkv_z, x0, do_far))
    qkv_a = jnp.stack(qkv_z)
    qkv_b = swap_x(qkv_a)
    x1, x3 = swap_core(x0), swap_core(x2)
    xs = (x0, x1, x2, x3)
    tabs = tables(xs)
    out_zx = jnp.stack([do_near[:, 64:], do_far[:, 64:]])
    out_y = swap_y(out_zx)
    g_own, u_own = units(xs)
    g_near = stack_z(g_own)
    u_near1 = swap_z(u_own, 1)

    qkv_b, out_y, tabs, ct0, g_near, u_own, u_near1 = lax.optimization_barrier(
        (qkv_b, out_y, tabs, ct0, g_near, u_own, u_near1))
    ct2 = swap_y(ct0)
    g_far = swap_x(g_near)
    u_near = jnp.stack([u_own, u_near1, swap_z(u_own, 2), swap_z(u_own, 3)])
    *saved, gains, a0, a1, a2, a3 = attend(xs, qkv_a, qkv_b, tabs)

    a1, a2, a3, u_near, ct2, g_far, out_zx, out_y = lax.optimization_barrier(
        (a1, a2, a3, u_near, ct2, g_far, out_zx, out_y))
    a1, a2, a3 = swap_b(a1, 1), swap_b(a2, 2), swap_b(a3, 3)
    out_own = jnp.stack([out_zx[0], out_y[0], out_zx[1], out_y[1]])
    out_other = swap_core(out_own)
    u_far = swap_x(after(u_near, a1))

    a1, a2, a3, out_other, ct0, ct2, u_far = lax.optimization_barrier((a1, a2, a3, out_other, ct0, ct2, u_far))
    resid, n02, wo, heads = project((a0, a1, a2, a3), x0, x2, gains, out_own, out_other)
    n13 = swap_core(n02)
    ct1, ct3 = swap_core(ct0), swap_core(ct2)

    n_all, ct_all, hid, dg, du, wgu, wd = hidden_and_back(
        (n02, n13), (ct0, ct1, ct2, ct3), (g_near, g_far, u_near, u_far, do_near, do_far))
    gn_own, gn_far, gn_send = normed_back(dg, du, wgu)
    gn_in = swap_core(gn_send)
    gu_keep, gu_send, d_keep, d_send = ff_grads(n_all, ct_all, hid, dg, du)
    gn_in, gu_send, d_send, hid = lax.optimization_barrier((gn_in, gu_send, d_send, hid))
    gn_there = swap_y((gn_far + gn_in[1].astype(F32)).astype(BF))
    gn_here = gn_own + gn_in[0].astype(F32)
    out_own, out_far, out_send = down(hid, wd, resid)
    out_in = swap_core(out_send)
    gu_in = swap_x(gu_send)
    gn_there, out_in, d_send = lax.optimization_barrier((gn_there, out_in, d_send))
    out_here, out_2, mid, br0, ga0, ga1, ga2, ga3, gain2 = mid_back(
        gn_here, gn_there, resid, ct0, gains, wo, (out_own, out_far, out_in))
    ga1, ga2, ga3 = swap_b(ga1, 1), swap_b(ga2, 2), swap_b(ga3, 3)
    d_in = swap_x(d_send)
    o_keep, o_send = out_grads(heads, br0)
    o_in = swap_core(o_send)
    o_2 = added(o_keep[1], o_in[1])
    gu_in = after(gu_in, ga1)
    gu_2 = added(gu_keep[2:], gu_in[2:])
    ga1, ga2, ga3, gu_2, o_2, out_2 = lax.optimization_barrier((ga1, ga2, ga3, gu_2, o_2, out_2))
    gu_far = swap_z(gu_2, 2)
    o_2in = swap_x(o_2)
    out_there = swap_y(out_2)
    qkv_keep, qkv_send, gn_keep, gn_keep2, gn_send = attend_back(saved, tabs, xs, (ga0, ga1, ga2, ga3), gain2)
    qkv_send, gn_send, d_in, o_2in = lax.optimization_barrier((qkv_send, gn_send, d_in, o_2in))
    qkv_in = swap_x(qkv_send)
    gn_in2 = swap_core(gn_send)
    d_2 = added(d_keep, d_in)
    d_far = swap_z(d_2[2:], 2)
    o_3 = [added(o_keep[0, j].astype(F32) + o_in[0, j].astype(F32), o_2in[j]) for j in range(2)]
    o_3in = swap_y(o_3[1])
    gn_here2 = added(gn_keep, gn_in2[0])
    there_in = swap_y(added(gn_keep2, gn_in2[1]))
    output = (out_here + out_there.astype(F32)).astype(BF)
    qkv_in, o_3in, gu_in, d_2 = lax.optimization_barrier((qkv_in, o_3in, gu_in, d_2))
    tail = list(tail_blocks(qkv_keep, qkv_in, o_3[0], o_3in))
    tail = [tail[0]] + [swap_z(tail[k], k) for k in (1, 2, 3)]
    gu_rows = halve_z(added(gu_keep[:2], gu_in[:2]), gu_far).astype(BF).reshape(4, 24, 1024)
    gu_order = by_index([gu_rows[j] for j in range(4)], b)
    grad_down = halve_z(d_2, d_far)
    tail, there_in, gu_order, grad_down = lax.optimization_barrier((tail, there_in, gu_order, grad_down))
    rows = sum(term.astype(F32) for term in tail)
    rows96 = rows[:96].astype(BF).reshape(4, 24, 640)
    order = by_index([rows96[j] for j in range(4)], b)
    from_heads = [order[0]] + [swap_b(order[j], j) for j in (1, 2, 3)]
    from_units = [gu_order[0]] + [swap_b(gu_order[j], j) for j in (1, 2, 3)]
    grad_out = jnp.concatenate(
        [rows[96:120], jnp.concatenate([rows[120:128, 128 * t : 128 * t + 128] for t in range(3)], axis=0)], axis=1)
    (grad_input,) = call(last_kernel, [((256, 768), BF)], [gn_here2, there_in, mid, x0, gains],
                         flops=10_000_000, nbytes=3_000_000)

    grad_query, grad_key, grad_value, grad_gate, grad_up, grad_gain1, grad_gain2 = finish(from_heads, from_units)
    return (output[None], grad_input[None], grad_gain1[0], grad_query, grad_key, grad_value, grad_out,
            grad_gain2[0], grad_gate, grad_up, grad_down)


def solution(mesh):
    fits = dict(mesh.shape) == {"dp": 8, "blk": 4}
    return jax.shard_map(
        fast_shards if fits else shards,
        mesh=mesh,
        in_specs=(
            P("dp", "blk", None),
            P("dp", "blk"),
            P("dp", "blk"),
            P("dp", "blk", None),
            P(("dp", "blk")),
            P(("dp", "blk"), None),
            P(("dp", "blk"), None),
            P(("dp", "blk"), None),
            P(("dp", "blk"), None),
            P(("dp", "blk")),
            P(("dp", "blk"), None),
            P(("dp", "blk"), None),
            P(("dp", "blk"), None),
        ),
        out_specs=(
            P("dp", "blk", None),
            P("dp", "blk", None),
            P(("dp", "blk")),
            P(("dp", "blk"), None),
            P(("dp", "blk"), None),
            P(("dp", "blk"), None),
            P(("dp", "blk"), None),
            P(("dp", "blk")),
            P(("dp", "blk"), None),
            P(("dp", "blk"), None),
            P(("dp", "blk"), None),
        ),
        check_vma=False,
    )
```

```python
import math

import jax
import jax.numpy as jnp
from jax import lax
from jax.experimental import pallas as pl
from jax.experimental.pallas import tpu as pltpu
from jax.sharding import PartitionSpec as P

HEADS = 12
HEAD_DIM = 64


EPS = 1e-05
SCALE = 0.125
NEG = -1e30


def rope_tables(slot_positions, half_dim):
    inverse = jnp.exp(-math.log(10000.0) * jnp.arange(half_dim, dtype=jnp.float32) / half_dim)
    angles = slot_positions.astype(jnp.float32)[:, None] * inverse[None, :]
    return (jnp.cos(angles)[:, None, :], jnp.sin(angles)[:, None, :])


def rotate(tensor, cosine_table, sine_table):
    half_dim = tensor.shape[-1] // 2
    leading = tensor[..., :half_dim]
    trailing = tensor[..., half_dim:]
    return jnp.concatenate(
        [
            leading * cosine_table - trailing * sine_table,
            trailing * cosine_table + leading * sine_table,
        ],
        axis=-1,
    )


def matmul(left_matrix, right_matrix):
    return jnp.dot(left_matrix, right_matrix, preferred_element_type=jnp.float32)


def left_product(left_matrix, right_matrix):
    return lax.dot_general(
        left_matrix, right_matrix, (((0,), (0,)), ((), ())), preferred_element_type=jnp.float32
    )


def right_product(left_matrix, right_matrix):
    return lax.dot_general(
        left_matrix, right_matrix, (((1,), (1,)), ((), ())), preferred_element_type=jnp.float32
    )


def norm_back(grad_normed, values, inverse, gain):
    unit_normed = values * inverse
    scaled = grad_normed * gain
    grad_gain = jnp.sum(grad_normed * unit_normed, axis=0)
    grad_values = inverse * (
        scaled - unit_normed * jnp.mean(scaled * unit_normed, axis=-1, keepdims=True)
    )
    return (grad_values, grad_gain)


def score_mask(query_segments, query_index, key_segments, key_index):
    return (query_segments[:, None] == key_segments[None, :]) & (
        key_index[None, :] <= query_index[:, None]
    )


def block_grads(query_block, grad_block, lse_rows, delta_rows, allowed, key_block, value_block):
    scores = (
        jnp.einsum("qhd,khd->hqk", query_block, key_block, preferred_element_type=jnp.float32)
        * SCALE
    )
    probability = jnp.exp(jnp.where(allowed[None], scores - lse_rows.T[:, :, None], NEG))
    grad_value = jnp.einsum(
        "hqk,qhd->khd",
        probability.astype(jnp.bfloat16),
        grad_block,
        preferred_element_type=jnp.float32,
    )
    grad_probs = jnp.einsum(
        "qhd,khd->hqk", grad_block, value_block, preferred_element_type=jnp.float32
    )
    grad_scores = (probability * (grad_probs - delta_rows.T[:, :, None])).astype(jnp.bfloat16)
    grad_query = (
        jnp.einsum("hqk,khd->qhd", grad_scores, key_block, preferred_element_type=jnp.float32)
        * SCALE
    )
    grad_key = (
        jnp.einsum("hqk,qhd->khd", grad_scores, query_block, preferred_element_type=jnp.float32)
        * SCALE
    )
    return (grad_query, grad_key, grad_value)


def shards(
    tokens,
    segments,
    positions,
    cotangent,
    attn_gain,
    w_query,
    w_key,
    w_value,
    w_out,
    mlp_gain,
    w_gate,
    w_up,
    w_down,
):
    local_rows = tokens.shape[1]
    model_width = tokens.shape[2]
    blocks = lax.axis_size("blk")
    own_start = lax.axis_index("blk") * local_rows
    query_index = own_start + jnp.arange(local_rows, dtype=jnp.int32)
    own_segments = segments[0]
    cosine_table, sine_table = rope_tables(positions[0], HEAD_DIM // 2)
    x_float = tokens[0].astype(jnp.float32)
    gathered = (
        lax.all_gather(attn_gain, ("dp", "blk"), axis=0, tiled=True),
        lax.all_gather(w_query, ("dp", "blk"), axis=0, tiled=True),
        lax.all_gather(w_key, ("dp", "blk"), axis=0, tiled=True),
        lax.all_gather(w_value, ("dp", "blk"), axis=0, tiled=True),
        lax.all_gather(w_out, ("dp", "blk"), axis=0, tiled=True),
        lax.all_gather(mlp_gain, ("dp", "blk"), axis=0, tiled=True),
        lax.all_gather(w_gate, ("dp", "blk"), axis=0, tiled=True),
        lax.all_gather(w_up, ("dp", "blk"), axis=0, tiled=True),
        lax.all_gather(w_down, ("dp", "blk"), axis=0, tiled=True),
    )
    gain_one = gathered[0].astype(jnp.float32)
    gain_two = gathered[5].astype(jnp.float32)
    inverse_one = lax.rsqrt(jnp.mean(x_float * x_float, axis=-1, keepdims=True) + EPS)
    normed = (x_float * inverse_one * gain_one).astype(jnp.bfloat16)
    query_rot = rotate(
        matmul(normed, gathered[1]).reshape(local_rows, HEADS, HEAD_DIM), cosine_table, sine_table
    ).astype(jnp.bfloat16)
    key_rot = rotate(
        matmul(normed, gathered[2]).reshape(local_rows, HEADS, HEAD_DIM), cosine_table, sine_table
    ).astype(jnp.bfloat16)
    value_heads = (
        matmul(normed, gathered[3]).astype(jnp.bfloat16).reshape(local_rows, HEADS, HEAD_DIM)
    )
    key_flat = key_rot.reshape(local_rows, model_width)
    value_flat = value_heads.reshape(local_rows, model_width)
    start_state = (
        jnp.full((HEADS, local_rows), NEG, jnp.float32),
        jnp.zeros((HEADS, local_rows), jnp.float32),
        jnp.zeros((local_rows, HEADS, HEAD_DIM), jnp.float32),
    )
    key_piece = lax.all_gather(key_flat, "blk", axis=0, tiled=True)
    value_piece = lax.all_gather(value_flat, "blk", axis=0, tiled=True)
    seg_piece = lax.all_gather(own_segments, "blk", axis=0, tiled=True)
    piece_rows = key_piece.shape[0]
    needed = (jnp.int32(0) <= own_start + local_rows - 1) & (
        seg_piece[piece_rows - 1] >= own_segments[0]
    )

    def attend_sweep(current):

        def attend_visit(number, partial_value):
            running_max, running_sum, weighted = partial_value
            offset = number * local_rows
            key_block = lax.dynamic_slice_in_dim(key_piece, offset, local_rows, 0).reshape(
                local_rows, HEADS, HEAD_DIM
            )
            value_block = lax.dynamic_slice_in_dim(value_piece, offset, local_rows, 0).reshape(
                local_rows, HEADS, HEAD_DIM
            )
            seg_block = lax.dynamic_slice_in_dim(seg_piece, offset, local_rows, 0)
            key_index = offset + jnp.arange(local_rows, dtype=jnp.int32)
            allowed = score_mask(own_segments, query_index, seg_block, key_index)
            scores = (
                jnp.einsum("qhd,khd->hqk", query_rot, key_block, preferred_element_type=jnp.float32)
                * SCALE
            )
            scores = jnp.where(allowed[None], scores, NEG)
            new_max = jnp.maximum(running_max, jnp.max(scores, axis=-1))
            probability = jnp.where(allowed[None], jnp.exp(scores - new_max[:, :, None]), 0.0)
            factor = jnp.exp(running_max - new_max)
            running_sum = running_sum * factor + jnp.sum(probability, axis=-1)
            weighted = weighted * factor.T[:, :, None] + jnp.einsum(
                "hqk,khd->qhd",
                probability.astype(jnp.bfloat16),
                value_block,
                preferred_element_type=jnp.float32,
            )
            return (new_max, running_sum, weighted)

        return lax.fori_loop(0, piece_rows // local_rows, attend_visit, current)

    final_max, final_sum, final_weighted = lax.cond(
        needed, attend_sweep, lambda unchanged: unchanged, start_state
    )
    attn_heads = (final_weighted / final_sum.T[:, :, None]).astype(jnp.bfloat16)
    lse_rows = (final_max + jnp.log(final_sum)).T
    attn_flat = attn_heads.reshape(local_rows, model_width)
    resid = x_float + matmul(attn_flat, gathered[4])
    inverse_two = lax.rsqrt(jnp.mean(resid * resid, axis=-1, keepdims=True) + EPS)
    normed_two = (resid * inverse_two * gain_two).astype(jnp.bfloat16)
    gate = matmul(normed_two, gathered[6])
    up_values = matmul(normed_two, gathered[7])
    hidden = (jax.nn.silu(gate) * up_values).astype(jnp.bfloat16)
    output = (resid + matmul(hidden, gathered[8])).astype(jnp.bfloat16)
    later = (
        lax.all_gather(attn_gain, ("dp", "blk"), axis=0, tiled=True),
        lax.all_gather(w_query, ("dp", "blk"), axis=0, tiled=True),
        lax.all_gather(w_key, ("dp", "blk"), axis=0, tiled=True),
        lax.all_gather(w_value, ("dp", "blk"), axis=0, tiled=True),
        lax.all_gather(w_out, ("dp", "blk"), axis=0, tiled=True),
        lax.all_gather(mlp_gain, ("dp", "blk"), axis=0, tiled=True),
        lax.all_gather(w_gate, ("dp", "blk"), axis=0, tiled=True),
        lax.all_gather(w_up, ("dp", "blk"), axis=0, tiled=True),
        lax.all_gather(w_down, ("dp", "blk"), axis=0, tiled=True),
    )
    grad_res = cotangent[0].astype(jnp.float32)
    grad_mlp = grad_res.astype(jnp.bfloat16)
    grad_down = left_product(hidden, grad_mlp)
    grad_hidden = right_product(grad_mlp, later[8])
    sigmoid_gate = jax.nn.sigmoid(gate)
    grad_gate_low = (
        grad_hidden * up_values * sigmoid_gate * (1.0 + gate * (1.0 - sigmoid_gate))
    ).astype(jnp.bfloat16)
    grad_up_low = (grad_hidden * gate * sigmoid_gate).astype(jnp.bfloat16)
    grad_gate_w = left_product(normed_two, grad_gate_low)
    grad_up_w = left_product(normed_two, grad_up_low)
    grad_normed_two = right_product(grad_gate_low, later[6]) + right_product(grad_up_low, later[7])
    grad_resid_norm, grad_gain_two = norm_back(grad_normed_two, resid, inverse_two, gain_two)
    grad_mid = grad_res + grad_resid_norm
    grad_branch = grad_mid.astype(jnp.bfloat16)
    grad_out_w = left_product(attn_flat, grad_branch)
    grad_attn = (
        right_product(grad_branch, later[4])
        .astype(jnp.bfloat16)
        .reshape(local_rows, HEADS, HEAD_DIM)
    )
    delta_rows = jnp.sum(grad_attn.astype(jnp.float32) * attn_heads.astype(jnp.float32), axis=-1)
    pack_length = local_rows * blocks
    empty_back = (
        jnp.zeros((local_rows, HEADS, HEAD_DIM), jnp.float32),
        jnp.zeros((pack_length, 2 * model_width), jnp.float32),
    )
    back_key_piece = lax.all_gather(key_flat, "blk", axis=0, tiled=True)
    back_value_piece = lax.all_gather(value_flat, "blk", axis=0, tiled=True)
    back_seg_piece = lax.all_gather(own_segments, "blk", axis=0, tiled=True)
    back_piece_rows = back_key_piece.shape[0]
    needed = (jnp.int32(0) <= own_start + local_rows - 1) & (
        back_seg_piece[back_piece_rows - 1] >= own_segments[0]
    )

    def back_sweep(current):

        def back_visit(number, partial_value):
            grad_query_acc, grad_pairs = partial_value
            offset = number * local_rows
            key_block = lax.dynamic_slice_in_dim(back_key_piece, offset, local_rows, 0).reshape(
                local_rows, HEADS, HEAD_DIM
            )
            value_block = lax.dynamic_slice_in_dim(back_value_piece, offset, local_rows, 0).reshape(
                local_rows, HEADS, HEAD_DIM
            )
            seg_block = lax.dynamic_slice_in_dim(back_seg_piece, offset, local_rows, 0)
            key_index = offset + jnp.arange(local_rows, dtype=jnp.int32)
            allowed = score_mask(own_segments, query_index, seg_block, key_index)
            part_query, part_key, part_value = block_grads(
                query_rot, grad_attn, lse_rows, delta_rows, allowed, key_block, value_block
            )
            new_rows = jnp.concatenate(
                [
                    part_key.reshape(local_rows, model_width),
                    part_value.reshape(local_rows, model_width),
                ],
                axis=1,
            )
            existing = lax.dynamic_slice_in_dim(grad_pairs, offset, local_rows, 0)
            grad_pairs = lax.dynamic_update_slice_in_dim(grad_pairs, existing + new_rows, offset, 0)
            return (grad_query_acc + part_query, grad_pairs)

        return lax.fori_loop(0, back_piece_rows // local_rows, back_visit, current)

    grad_query_rot, grad_pairs_all = lax.cond(
        needed, back_sweep, lambda unchanged: unchanged, empty_back
    )
    own_pairs = lax.psum_scatter(
        grad_pairs_all.astype(jnp.bfloat16), "blk", scatter_dimension=0, tiled=True
    ).astype(jnp.float32)
    grad_key_rot = own_pairs[:, :model_width].reshape(local_rows, HEADS, HEAD_DIM)
    grad_value_heads = own_pairs[:, model_width:].reshape(local_rows, HEADS, HEAD_DIM)
    grad_query_low = (
        rotate(grad_query_rot, cosine_table, -sine_table)
        .reshape(local_rows, model_width)
        .astype(jnp.bfloat16)
    )
    grad_key_low = (
        rotate(grad_key_rot, cosine_table, -sine_table)
        .reshape(local_rows, model_width)
        .astype(jnp.bfloat16)
    )
    grad_value_low = grad_value_heads.reshape(local_rows, model_width).astype(jnp.bfloat16)
    grad_query_w = left_product(normed, grad_query_low)
    grad_key_w = left_product(normed, grad_key_low)
    grad_value_w = left_product(normed, grad_value_low)
    grad_normed = (
        right_product(grad_query_low, later[1])
        + right_product(grad_key_low, later[2])
        + right_product(grad_value_low, later[3])
    )
    grad_x_norm, grad_gain_one = norm_back(grad_normed, x_float, inverse_one, gain_one)
    grad_input = (grad_mid + grad_x_norm).astype(jnp.bfloat16)
    summed = (
        lax.psum_scatter(grad_gain_one, ("dp", "blk"), scatter_dimension=0, tiled=True),
        lax.psum_scatter(grad_query_w, ("dp", "blk"), scatter_dimension=0, tiled=True),
        lax.psum_scatter(grad_key_w, ("dp", "blk"), scatter_dimension=0, tiled=True),
        lax.psum_scatter(grad_value_w, ("dp", "blk"), scatter_dimension=0, tiled=True),
        lax.psum_scatter(grad_out_w, ("dp", "blk"), scatter_dimension=0, tiled=True),
        lax.psum_scatter(grad_gain_two, ("dp", "blk"), scatter_dimension=0, tiled=True),
        lax.psum_scatter(grad_gate_w, ("dp", "blk"), scatter_dimension=0, tiled=True),
        lax.psum_scatter(grad_up_w, ("dp", "blk"), scatter_dimension=0, tiled=True),
        lax.psum_scatter(grad_down, ("dp", "blk"), scatter_dimension=0, tiled=True),
    )
    return (
        output.reshape(1, local_rows, model_width),
        grad_input.reshape(1, local_rows, model_width),
        summed[0],
        summed[1],
        summed[2],
        summed[3],
        summed[4],
        summed[5],
        summed[6],
        summed[7],
        summed[8],
    )


BF = jnp.bfloat16
F32 = jnp.float32
VMEM = pltpu.VMEM
LANES = 256


def ids():
    dp, blk = lax.axis_index("dp"), lax.axis_index("blk")
    return dp // 2, dp % 2, blk // 2, blk % 2, blk


def flip(bit, other):
    total = 0
    weight = 1
    while weight <= 2:
        own = (bit // weight) % 2
        total = total + weight * ((1 - own) if (other // weight) % 2 else own)
        weight *= 2
    return total


def exclusive(a, b):
    low, high = (a + b) % 2, (a // 2 + b // 2) % 2
    return low + 2 * high


def aligned(value, multiple):
    return pl.multiple_of(value, multiple)


def dot(a, b, ca=1, cb=0):
    return lax.dot_general(a, b, (((ca,), (cb,)), ((), ())), preferred_element_type=F32)


HBM = "hbm"


def call(kernel, outs, ins, anys=(), scratch=(), flops=0, nbytes=0, grant=14):
    def place(far):
        return pl.BlockSpec(memory_space=pltpu.MemorySpace.HBM if far else VMEM)

    return pl.pallas_call(
        kernel,
        out_shape=[jax.ShapeDtypeStruct(out[0], out[1]) for out in outs],
        in_specs=[place(i in anys) for i in range(len(ins))],
        out_specs=[place(len(out) > 2) for out in outs],
        scratch_shapes=list(scratch),
        compiler_params=pltpu.CompilerParams(vmem_limit_bytes=grant * 1024 * 1024),
        cost_estimate=pl.CostEstimate(flops=flops, bytes_accessed=nbytes, transcendentals=0),
    )(*ins)


def pair(low, first, second):
    (a, i), (b, j) = first, second
    left = a[:, 128 * (i // 2) : 128 * (i // 2) + 128]
    right = b[:, 128 * (j // 2) : 128 * (j // 2) + 128]
    left = pltpu.roll(left, 64, 1) if i % 2 else left
    right = right if j % 2 else pltpu.roll(right, 64, 1)
    return jnp.where(low, left, right)


def pairs(low, blocks):
    return jnp.concatenate([pair(low, blocks[i], blocks[i + 1]) for i in range(0, len(blocks), 2)], axis=1)


def prepare_kernel(gain1, gain2, place, wq_h, wk_h, wv_h, wg_h, wu_h, x_h, r0_o, r1_o, r2_o, r3_o, x_o,
                   wq, wk, wv, wg, wu, order, sems):
    z, x, y, c, b = ids()
    far, near = (wq_h, wk_h, wv_h, wg_h, wu_h), (wq, wk, wv, wg, wu)
    copies = [pltpu.make_async_copy(a, d, sems.at[i]) for i, (a, d) in enumerate(zip(far, near))]
    copies.append(pltpu.make_async_copy(x_h, x_o.at[pl.ds(0, 256)], sems.at[5]))
    for copy in copies:
        copy.start()
    for copy in copies[:5]:
        copy.wait()
    low = lax.broadcasted_iota(jnp.int32, (wq.shape[0], 128), 1) < 64
    q, k, v, gate, up = (ref[...].astype(F32) for ref in (wq, wk, wv, wg, wu))
    rows = wq.shape[0]
    here = lax.broadcasted_iota(jnp.int32, (rows, rows), 0) == lax.broadcasted_iota(jnp.int32, (rows, rows), 1)
    lane = lax.broadcasted_iota(jnp.int32, (rows, 128), 1)
    g = jnp.zeros((rows, 128), F32)
    for at, ref in ((64, gain1), (65, gain2)):
        row = jnp.broadcast_to(ref[...].astype(F32), (rows, rows))
        g = jnp.where(lane == at, jnp.sum(jnp.where(here, row, 0.0), axis=1, keepdims=True), g)
    at = jnp.broadcast_to(place[...], (16, 256)).astype(F32)
    tens = jnp.floor(at * (1.0 / 32))
    x_o[256:272, :] = jnp.concatenate([tens, at - 32.0 * tens, jnp.zeros_like(at)], axis=1).astype(BF)
    for j in range(4):
        blocks = [(w, 3 * j + t) for w in (q, k, v) for t in range(3)] + [(g, 1)]
        order[flip(b, j)] = pairs(low, blocks).astype(BF)
        wide = pairs(low, [(w, 4 * i + j) for w in (gate, up) for i in range(8)])
        rest = jnp.concatenate([wide[8 * t : 8 * t + 8, 768:1024] for t in range(3)], axis=1)
        x_o[272 + 32 * j : 304 + 32 * j, :] = jnp.concatenate([wide[:, 0:768], rest], axis=0).astype(BF)
    for k, out in enumerate((r0_o, r1_o, r2_o, r3_o)):
        out[...] = order[k]
    copies[5].wait()


def prepare(tokens, place, wq, wk, wv, gain1, gain2, wg, wu):
    outs = [((24, 640), BF)] * 4 + [((400, 768), BF)]
    scratch = [*[VMEM((24, 768), BF)] * 3, *[VMEM((24, 2048), BF)] * 2, VMEM((4, 24, 640), BF),
               pltpu.SemaphoreType.DMA((7,))]
    return call(prepare_kernel, outs, [gain1, gain2, place, wq, wk, wv, wg, wu, tokens], anys=range(3, 9), scratch=scratch,
                flops=1_000_000, nbytes=1_000_000, grant=60)


def columns_kernel(r0, r1, r2, r3, out, rows):
    z, x, y, c, b = ids()
    for k, piece in enumerate((r0, r1, r2, r3)):
        rows[pl.ds(aligned(flip(b, k) * 24, 24), 24), :] = piece[...].astype(F32)
    out[...] = rows[...].astype(BF)


def columns(pieces):
    (out,) = call(columns_kernel, [((96, 640), BF)], pieces, scratch=[VMEM((96, 640), F32)], flops=1_000_000, nbytes=300_000)
    return out


def units_kernel(x0, x1, x2, x3, gate_o, up_o, rows):
    z, x, y, c, b = ids()
    for k, piece in enumerate((x0, x1, x2, x3)):
        part = piece[pl.ds(aligned(272 + 32 * b, 16), 32), :].astype(F32)
        rest = jnp.concatenate([part[24:32, 256 * t : 256 * t + 256] for t in range(3)], axis=0)
        rows[pl.ds(aligned(flip(b, k) * 24, 24), 24), :] = jnp.concatenate([part[0:24], rest], axis=1)
    gate_o[...] = rows[:, 0:512].astype(BF)
    up_o[...] = rows[:, 512:1024].astype(BF)


def units(xs):
    outs = [((96, 512), BF)] * 2
    return call(units_kernel, outs, xs, scratch=[VMEM((96, 1024), F32)], flops=1_000_000, nbytes=3_000_000)


def finish_kernel(h0, h1, h2, h3, u0, u1, u2, u3, q_o, k_o, v_o, gate_o, up_o, gain1_o, gain2_o, heads, units):
    z, x, y, c, b = ids()
    for k in range(4):
        heads[k] = (h0, h1, h2, h3)[k][...]
        units[k] = (u0, u1, u2, u3)[k][...]
    low = lax.broadcasted_iota(jnp.int32, (heads.shape[1], 128), 1) < 64
    parts = [heads[flip(b, j)].astype(F32) for j in range(4)]
    for t, out in enumerate((q_o, k_o, v_o)):
        out[...] = pairs(low, [(parts[m // 3], 3 * t + m % 3) for m in range(12)])
    total = parts[0][:, 512:640] + parts[1][:, 512:640] + parts[2][:, 512:640] + parts[3][:, 512:640]
    rows = heads.shape[1]
    here = lax.broadcasted_iota(jnp.int32, (rows, rows), 0) == lax.broadcasted_iota(jnp.int32, (rows, rows), 1)
    for at, out in ((64, gain1_o), (65, gain2_o)):
        out[...] = jnp.sum(jnp.where(here, jnp.broadcast_to(total[:, at : at + 1], (rows, rows)), 0.0), axis=0, keepdims=True)
    parts = [units[flip(b, j)].astype(F32) for j in range(4)]
    for t, out in enumerate((gate_o, up_o)):
        out[...] = pairs(low, [(parts[m % 4], 8 * t + m // 4) for m in range(32)])


def finish(heads, units):
    outs = [((24, 768), F32)] * 3 + [((24, 2048), F32)] * 2 + [((1, 24), F32)] * 2
    return call(finish_kernel, outs, [*heads, *units], scratch=[VMEM((4, 24, 640), BF), VMEM((4, 24, 1024), BF)],
                flops=1_000_000, nbytes=2_000_000)


def tables_kernel(x0, x1, x2, x3, table_o, rows_o, marks, table, rows, sems, out_sems):
    z, x, y, c, b = ids()
    copies = [
        pltpu.make_async_copy(piece.at[pl.ds(256, 16)], marks.at[k], sems.at[k])
        for k, piece in enumerate((x0, x1, x2, x3))
    ]
    for copy in copies:
        copy.start()
    for copy in copies:
        copy.wait()
    lane = lax.broadcasted_iota(jnp.int32, (256, 128), 1)
    inverse = jnp.exp((lane % 32).astype(F32) * (-math.log(10000.0) / 32))
    for k in range(4):
        own = marks[k].astype(F32)
        place = (32.0 * own[:, 0:256] + own[:, 256:512])[0:1]
        slot = lax.broadcasted_iota(jnp.int32, (8, 256), 1) + 256 * flip(b, k)
        rows[k] = slot.astype(F32) - jnp.broadcast_to(place, (8, 256))
        angles = jnp.broadcast_to(place, (128, 256)).T * inverse
        sine = jnp.sin(angles)
        table[k] = jnp.where(lane < 64, jnp.cos(angles), jnp.where(lane < 96, -sine, sine))
    leaving = [
        pltpu.make_async_copy(ref, out, out_sems.at[i])
        for i, (ref, out) in enumerate(((table, table_o), (rows, rows_o)))
    ]
    for copy in leaving:
        copy.start()
    for copy in leaving:
        copy.wait()


def tables(xs):
    outs = [((4, 256, 128), F32, HBM), ((4, 8, 256), F32, HBM)]
    scratch = [
        VMEM((4, 16, 768), BF), VMEM((4, 256, 128), F32), VMEM((4, 8, 256), F32),
        pltpu.SemaphoreType.DMA((4,)), pltpu.SemaphoreType.DMA((2,)),
    ]
    return call(tables_kernel, outs, xs, anys=range(4), scratch=scratch, flops=10_000_000, nbytes=3_000_000)


def turns(table, low):
    turned = pltpu.roll(table, 64, 1)
    return jnp.where(low, table, turned), jnp.where(low, turned, table)


def half_swap(tile, lane):
    return jnp.where(lane % 64 < 32, pltpu.roll(tile, 96, 1), pltpu.roll(tile, 32, 1))


def pack(block):
    low = lax.broadcasted_iota(jnp.int32, (128, 128), 1) < 64
    last = block[:, 128:256].astype(F32)
    last = jnp.where(low, last[0:128], pltpu.roll(last[128:256], 64, 1))
    return jnp.concatenate([block[:, 0:128].astype(BF), last.astype(BF)], axis=0)


def unpack(block):
    low = lax.broadcasted_iota(jnp.int32, (128, 128), 1) < 64
    last = block[256:384].astype(F32)
    zero = jnp.zeros_like(last)
    last = jnp.concatenate([jnp.where(low, last, zero), jnp.where(low, pltpu.roll(last, 64, 1), zero)], axis=0)
    return jnp.concatenate([block[0:256], last.astype(BF)], axis=1)


def attend_kernel(x0, x1, x2, x3, wa, wb, table_h, rows_h,
                  qkva_o, n_o, w_o, lse_o, gains_o, a0_o, a1_o, a2_o, a3_o,
                  xs, w, qkva, n, lse, table, begins, a0, a1, a2, a3, sems, out_sems):
    z, x, y, c, b = ids()
    q, k, v, attn = (qkva.at[i] for i in range(4))
    copies = []
    for xr, piece in enumerate((wa, wb)):
        for zr in range(4):
            dp = 2 * flip(z, zr) + flip(x, xr)
            copies.append(pltpu.make_async_copy(
                piece.at[zr], w.at[pl.ds(aligned(dp * 96, 96), 96)], sems.at[4 * xr + zr]))
    copies.append(pltpu.make_async_copy(table_h, table, sems.at[8]))
    for kk, piece in enumerate((x0, x1, x2, x3)):
        copies.append(pltpu.make_async_copy(piece.at[pl.ds(0, 272)], xs.at[kk], sems.at[9 + kk]))
    copies.append(pltpu.make_async_copy(rows_h, begins, sems.at[13]))
    for copy in copies:
        copy.start()
    for copy in copies[:9]:
        copy.wait()
    leaving = [pltpu.make_async_copy(w, w_o, out_sems.at[0])]
    leaving[0].start()
    last = w[:, 512:640].astype(F32).T
    gains = last[64:72, :]
    gains_o[...] = gains
    gain = gains[0:1, :]
    lane = lax.broadcasted_iota(jnp.int32, (256, 128), 1)
    low = lane < 64
    for kk in range(4):
        rows = pl.ds(aligned(flip(b, kk) * 256, 256), 256)
        copies[9 + kk].wait()
        values = xs[kk, 0:256, :].astype(F32)
        inverse = lax.rsqrt(jnp.mean(values * values, axis=-1, keepdims=True) + EPS)
        normed = (values * inverse * gain).astype(BF)
        n[rows, :] = normed
        qkv = dot(normed, w[...])
        cosine, sine = turns(table[kk], low)
        tiles = []
        for t in range(3):
            tile = qkv[:, 128 * t : 128 * t + 128]
            tiles.append(tile * cosine + half_swap(tile, lane) * sine)
        r1, r2 = pltpu.roll(tiles[1], 64, 1), pltpu.roll(tiles[2], 64, 1)
        zero = jnp.zeros_like(r1)
        q[rows, 0:128] = tiles[0].astype(BF)
        q[rows, 128:256] = jnp.where(low, tiles[1], zero).astype(BF)
        k[rows, 0:128] = jnp.where(low, r1, r2).astype(BF)
        k[rows, 128:256] = jnp.where(low, r2, zero).astype(BF)
        v[rows, 0:128] = qkv[:, 384:512].astype(BF)
        v[rows, 128:256] = jnp.where(low, qkv[:, 512:640], zero).astype(BF)
    for at, (ref, out) in enumerate(((n, n_o), (qkva.at[pl.ds(0, 3)], qkva_o.at[pl.ds(0, 3)]))):
        leaving.append(pltpu.make_async_copy(ref, out, out_sems.at[3 + at]))
        leaving[-1].start()
    copies[13].wait()
    head = lax.broadcasted_iota(jnp.int32, (256, LANES), 1) // 64
    for i in range(4):
        width = 256 * (i + 1)
        query = q[256 * i : 256 * i + 256, :]
        begin = jnp.broadcast_to(begins[flip(b, i)][0:1, :], (128, 256)).T[:, 0:1]
        column = lax.broadcasted_iota(jnp.int32, (256, width), 1)
        row = lax.broadcasted_iota(jnp.int32, (256, width), 0) + 256 * i
        allowed = (column <= row) & (column.astype(F32) >= begin)
        total = jnp.zeros((256, LANES), F32)
        stats = jnp.zeros((256, 128), F32)
        for h in range(3):
            mine = jnp.where(head == h, query, jnp.zeros_like(query))
            scores = dot(mine, k[0:width, :], 1, 1) * SCALE
            scores = jnp.where(allowed, scores, NEG)
            top = jnp.max(scores, axis=-1, keepdims=True)
            weight = jnp.exp(scores - top)
            norm = jnp.sum(weight, axis=-1, keepdims=True)
            mixed = dot(weight.astype(BF), v[0:width, :]) / norm
            total = jnp.where(head == h, mixed, total)
            stats = jnp.where(lane == h, top + jnp.log(norm), stats)
        attn[256 * i : 256 * i + 256, :] = total.astype(BF)
        lse[:, 256 * i : 256 * i + 256] = stats.T[0:8]
    for at, (ref, out) in enumerate(((attn, qkva_o.at[3]), (lse, lse_o))):
        leaving.append(pltpu.make_async_copy(ref, out, out_sems.at[1 + at]))
        leaving[-1].start()
    for kk, (out, far) in enumerate(((a0, a0_o), (a1, a1_o), (a2, a2_o), (a3, a3_o))):
        for t in range(2):
            out[t] = pack(attn[pl.ds(aligned(flip(flip(b, kk), 2 * t) * 256, 256), 256), :])
        leaving.append(pltpu.make_async_copy(out, far, out_sems.at[5 + kk]))
        leaving[-1].start()
    for copy in leaving:
        copy.wait()


def attend(xs, wa, wb, tabs):
    outs = [
        ((4, 1024, LANES), BF, HBM), ((1024, 768), BF, HBM), ((768, 640), BF, HBM),
        ((8, 1024), F32, HBM), ((8, 768), F32), *[((2, 384, 128), BF, HBM)] * 4,
    ]
    return call(
        attend_kernel, outs, [*xs, wa, wb, *tabs], anys=range(8), grant=60,
        scratch=[
            VMEM((4, 272, 768), BF), VMEM((768, 640), BF), VMEM((4, 1024, LANES), BF), VMEM((1024, 768), BF),
            VMEM((8, 1024), F32), VMEM((4, 256, 128), F32), VMEM((4, 8, 256), F32),
            *[VMEM((2, 384, 128), BF)] * 4, pltpu.SemaphoreType.DMA((14,)), pltpu.SemaphoreType.DMA((9,)),
        ],
        flops=1000, nbytes=1000,
    )


def out_kernel(a0, a1, a2, a3, x0, x2, gains, own, other, resid_o, n_o, wo_o, stack_o, wide):
    z, x, y, c, b = ids()
    for xy in range(4):
        for zr in range(4):
            chip = 8 * flip(z, zr) + 4 * flip(x, xy // 2) + 2 * flip(y, xy % 2)
            for core, pieces in enumerate((own, other)):
                at = aligned((chip + flip(c, core)) * 24, 24)
                wide[pl.ds(at, 24), :] = pieces[xy, zr].astype(F32)
    wo_o[...] = wide[...].astype(BF)
    for t, band in enumerate((x0, x2)):
        total = band[0:256, :].astype(F32)
        for k, piece in enumerate((a0, a1, a2, a3)):
            heads = unpack(piece[t])
            if t == 0:
                stack_o[k] = heads
            rows = pl.ds(aligned(flip(b, k) * 192, 192), 192)
            total += dot(heads[:, 0:192], wo_o[rows, :])
        if t == 0:
            resid_o[...] = total
        inverse = lax.rsqrt(jnp.mean(total * total, axis=-1, keepdims=True) + EPS)
        n_o[t] = (total * inverse * gains[1:2, :]).astype(BF)


def project(a, x0, x2, gains, own, other):
    outs = [((256, 768), F32), ((2, 256, 768), BF), ((768, 768), BF), ((4, 256, LANES), BF)]
    return call(out_kernel, outs, [*a, x0, x2, gains, own, other], scratch=[VMEM((768, 768), F32)],
                flops=800_000_000, nbytes=4_000_000)


def hidden_kernel(n02, n13, ct0, ct1, ct2, ct3, g_near, g_far, u_near, u_far, d_near, d_far,
                  n_o, ct_o, hid_o, dg_o, du_o, wgu_o, wd_o, sems):
    z, x, y, c, b = ids()
    copies = []
    for xr, (g, u, d) in enumerate(((g_near, u_near, d_near), (g_far, u_far, d_far))):
        for zr in range(4):
            dp = 2 * flip(z, zr) + flip(x, xr)
            at = 4 * xr + zr
            for i, w in enumerate((g, u)):
                copies.append(pltpu.make_async_copy(
                    w.at[zr], wgu_o.at[pl.ds(aligned(dp * 96, 96), 96), pl.ds(512 * i, 512)], sems.at[2 * i, at]))
            copies.append(pltpu.make_async_copy(
                d.at[zr, pl.ds(0, 64)], wd_o.at[pl.ds(aligned(dp * 64, 64), 64)], sems.at[1, at]))
    for copy in copies:
        copy.start()
    for k in range(4):
        n_o[256 * k : 256 * k + 256, :] = (n02, n13)[k % 2][k // 2]
        ct_o[256 * k : 256 * k + 256, :] = (ct0, ct1, ct2, ct3)[k][...]
    for copy in copies:
        copy.wait()
    for k in range(4):
        rows = slice(256 * k, 256 * k + 256)
        normed, cot = n_o[rows, :], ct_o[rows, :]
        for j in range(2):
            cols = slice(256 * j, 256 * j + 256)
            gate = dot(normed, wgu_o[:, 256 * j : 256 * j + 256])
            up = dot(normed, wgu_o[:, 512 + 256 * j : 768 + 256 * j])
            back = dot(cot, wd_o[cols, :], 1, 1)
            sig = 1.0 / (1.0 + jnp.exp(-gate))
            silu = gate * sig
            hid_o[rows, cols] = (silu * up).astype(BF)
            dg_o[rows, cols] = (back * up * sig * (1.0 + gate * (1.0 - sig))).astype(BF)
            du_o[rows, cols] = (back * silu).astype(BF)


def hidden_and_back(n, ct, pieces):
    outs = [((1024, 768), BF)] * 2 + [((1024, 512), BF)] * 3 + [((768, 1024), BF), ((512, 768), BF)]
    return call(
        hidden_kernel, outs, [*n, *ct, *pieces], anys=range(6, 12),
        scratch=[pltpu.SemaphoreType.DMA((3, 8))], flops=2_500_000_000, nbytes=8_000_000,
    )


def normed_back_kernel(dg, du, wgu, own_o, far_o, send_o):
    for k in range(4):
        rows = slice(256 * k, 256 * k + 256)
        grad = dot(dg[rows, :], wgu[:, 0:512], 1, 1) + dot(du[rows, :], wgu[:, 512:1024], 1, 1)
        if k == 0:
            own_o[...] = grad
        elif k == 2:
            far_o[...] = grad
        else:
            send_o[k // 2] = grad.astype(BF)


def normed_back(dg, du, wgu):
    outs = [((256, 768), F32)] * 2 + [((2, 256, 768), BF)]
    return call(normed_back_kernel, outs, [dg, du, wgu], flops=1_600_000_000, nbytes=6_000_000)


def store_by_x(grad, rows, cols, keep_o, send_o, z, x):
    for zp in range(4):
        at = 2 * rows * zp
        low, high = grad[at : at + rows], grad[at + rows : at + 2 * rows]
        keep_o[flip(z, zp), :, cols] = jnp.where(x == 0, low, high).astype(BF)
        send_o[flip(z, zp), :, cols] = jnp.where(x == 0, high, low).astype(BF)


def ff_grads_kernel(n, ct, hid, dg, du, gu_keep_o, gu_send_o, d_keep_o, d_send_o):
    z, x, y, c, b = ids()
    normed = n[...].T
    for j in range(4):
        cols = slice(256 * j, 256 * j + 256)
        part = (dg, du)[j // 2][:, 256 * (j % 2) : 256 * (j % 2) + 256]
        store_by_x(dot(normed, part), 96, cols, gu_keep_o, gu_send_o, z, x)
    hidden = hid[...].T
    for j in range(3):
        cols = slice(256 * j, 256 * j + 256)
        store_by_x(dot(hidden, ct[:, cols]), 64, cols, d_keep_o, d_send_o, z, x)


def ff_grads(n, ct, hid, dg, du):
    outs = [((4, 96, 1024), BF)] * 2 + [((4, 64, 768), BF)] * 2
    return call(ff_grads_kernel, outs, [n, ct, hid, dg, du], flops=2_400_000_000, nbytes=10_000_000)


def mid_kernel(gn_own, gn_in, resid, ct0, gains, wo, out_own, out_far, out_in, here_o, there_o, mid_o, branch_o, g0_o, g1_o, g2_o, g3_o):
    z, x, y, c, b = ids()
    here_o[...] = out_own[...] + out_in[0].astype(F32)
    there_o[...] = (out_far[...] + out_in[1].astype(F32)).astype(BF)
    grad = gn_own[...] + gn_in[...].astype(F32)
    values = resid[...]
    inverse = lax.rsqrt(jnp.mean(values * values, axis=-1, keepdims=True) + EPS)
    unit = values * inverse
    scaled = grad * gains[1:2, :]
    gain = jnp.sum(grad * unit, axis=0, keepdims=True)
    rows = [gain[:, 128 * t : 128 * t + 128] for t in range(6)] + [jnp.zeros((10, 128), F32)]
    g0_o[384:400, :] = jnp.concatenate(rows, axis=0).astype(BF)
    mid = ct0[...].astype(F32) + inverse * (
        scaled - unit * jnp.mean(scaled * unit, axis=-1, keepdims=True)
    )
    mid_o[...] = mid
    branch = mid.astype(BF)
    branch_o[...] = branch
    pad = jnp.zeros((256, LANES - 192), F32)
    for k in range(4):
        rows = pl.ds(aligned(flip(b, k) * 192, 192), 192)
        part = dot(branch, wo[rows, :], 1, 1)
        (g0_o, g1_o, g2_o, g3_o)[k][0:384, :] = pack(jnp.concatenate([part, pad], axis=1))


def mid_back(gn_own, gn_in, resid, ct0, gains, wo, out):
    outs = [((256, 768), F32), ((256, 768), BF), ((256, 768), F32), ((256, 768), BF), ((400, 128), BF), *[((384, 128), BF)] * 3]
    return call(mid_kernel, outs, [gn_own, gn_in, resid, ct0, gains, wo, *out], flops=400_000_000, nbytes=5_000_000)


def out_grads_kernel(stack, branch, keep_o, send_o, wide):
    z, x, y, c, b = ids()
    for k in range(4):
        part = dot(stack[k].T, branch[...])[0:192]
        wide[pl.ds(aligned(exclusive(flip(b, k), z) * 192, 192), 192), :] = part
    for cr, out in enumerate((keep_o, send_o)):
        for yr in range(2):
            for xr in range(2):
                for zr in range(4):
                    at = 4 * (flip(x, xr) % 2) + 2 * (flip(y, yr) % 2) + flip(c, cr) % 2 + 8 * zr
                    out[xr, yr, zr] = wide[pl.ds(aligned(at * 24, 24), 24), :].astype(BF)


def out_grads(stack, branch):
    outs = [((2, 2, 4, 24, 768), BF)] * 2
    return call(out_grads_kernel, outs, [stack, branch], scratch=[VMEM((768, 768), F32)],
                flops=400_000_000, nbytes=3_000_000)


def down_kernel(hid, wd, resid, own_o, far_o, send_o):
    for k in range(4):
        part = dot(hid[256 * k : 256 * k + 256, :], wd[...])
        if k == 0:
            own_o[...] = resid[...] + part
        elif k == 2:
            far_o[...] = part
        else:
            send_o[k // 2] = part.astype(BF)


def down(hid, wd, resid):
    outs = [((256, 768), F32)] * 2 + [((2, 256, 768), BF)]
    return call(down_kernel, outs, [hid, wd, resid], flops=800_000_000, nbytes=5_000_000)


def attend_back_kernel(qkva_h, n_h, w_h, lse_h, table_h, start_h, x0, x1, x2, x3, g0, g1, g2, g3,
                       keep_h, send_h, gk0_h, gk1_h, gs_h,
                       qkva, n, w, lse, table, start, xs, packed, do, dq, dk, dv, grads, wide,
                       keep_o, send_o, gk0_o, gk1_o, gs_o, sems, out_sems):
    z, x, y, c, b = ids()
    q, k, v, attn = (qkva.at[i] for i in range(4))
    first = [
        pltpu.make_async_copy(a, d, sems.at[i])
        for i, (a, d) in enumerate(((lse_h, lse), (start_h, start), (qkva_h, qkva)))
    ] + [pltpu.make_async_copy(g0, packed.at[0], sems.at[3])] + [
        pltpu.make_async_copy(a, packed.at[1 + i, pl.ds(0, 384)], sems.at[4 + i]) for i, a in enumerate((g1, g2, g3))
    ]
    rest = [
        pltpu.make_async_copy(a, d, sems.at[7 + i])
        for i, (a, d) in enumerate(((table_h, table), (n_h, n), (w_h, w)))
    ] + [pltpu.make_async_copy(a.at[pl.ds(0, 272)], xs.at[i], sems.at[11 + i]) for i, a in enumerate((x0, x1, x2, x3))]
    for copy in first + rest:
        copy.start()
    dk[...] = jnp.zeros_like(dk)
    dv[...] = jnp.zeros_like(dv)
    for copy in first:
        copy.wait()
    for i in range(4):
        do[pl.ds(aligned(flip(b, i) * 256, 256), 256), :] = unpack(packed[i, 0:384, :])
    below = packed[0, 384:400, :].astype(F32)
    gain2 = jnp.concatenate([below[t : t + 1, :] for t in range(6)], axis=1)
    head = lax.broadcasted_iota(jnp.int32, (256, LANES), 1) // 64
    lane = lax.broadcasted_iota(jnp.int32, (256, 128), 1)
    for i in range(4):
        width = 256 * (i + 1)
        rows = slice(256 * i, 256 * i + 256)
        query, out_grad = q[rows, :] * SCALE, do[rows, :]
        product = out_grad.astype(F32) * attn[rows, :].astype(F32)
        delta = jnp.zeros((256, 128), F32)
        for h in range(3):
            delta = jnp.where(
                lane == h, jnp.sum(jnp.where(head == h, product, 0.0), axis=-1, keepdims=True), delta)
        delta = delta.T
        begin = start[flip(b, i)][0:1, :]
        key = lax.broadcasted_iota(jnp.int32, (width, 256), 0)
        slot = lax.broadcasted_iota(jnp.int32, (width, 256), 1) + 256 * i
        allowed = (key <= slot) & (key.astype(F32) >= begin)
        probs, dscores = [], []
        mine = [jnp.where(head == h, query, jnp.zeros_like(query)) for h in range(3)]
        ours = [jnp.where(head == h, out_grad, jnp.zeros_like(out_grad)) for h in range(3)]
        for h in range(3):
            scores = dot(k[0:width, :], mine[h], 1, 1)
            prob = jnp.exp(jnp.where(allowed, scores - lse[h : h + 1, rows], NEG))
            dprob = dot(v[0:width, :], ours[h], 1, 1)
            probs.append(prob.astype(BF))
            dscores.append((prob * (dprob - delta[h : h + 1, :])).astype(BF))
        dv[0:width, :] += dot(jnp.concatenate(probs, axis=1), jnp.concatenate(ours, axis=0))
        dk[0:width, :] += dot(jnp.concatenate(dscores, axis=1), jnp.concatenate(mine, axis=0))
        total = jnp.zeros((256, LANES), F32)
        for h in range(3):
            total = jnp.where(head == h, dot(dscores[h], k[0:width, :], 0, 0), total)
        dq[rows, :] = total
    for copy in rest:
        copy.wait()
    low = lane < 64
    zero = jnp.zeros((256, 128), F32)
    for i in range(4):
        rows = slice(256 * i, 256 * i + 256)
        cosine, sine = turns(table[flip(b, i)], low)
        turned = []
        for ref, factor in ((dq, SCALE), (dk, 1.0)):
            for t in range(2):
                tile = ref[rows, 128 * t : 128 * t + 128] * factor
                turned.append(tile * cosine - half_swap(tile, lane) * sine)
        k0, k1 = pltpu.roll(turned[2], 64, 1), pltpu.roll(turned[3], 64, 1)
        grads[rows, 0:128] = turned[0].astype(BF)
        grads[rows, 128:256] = jnp.where(low, turned[1], k0).astype(BF)
        grads[rows, 256:384] = jnp.where(low, k0, k1).astype(BF)
        grads[rows, 384:512] = dv[rows, 0:128].astype(BF)
        grads[rows, 512:640] = jnp.where(low, dv[rows, 128:256], zero).astype(BF)
    leaving = []

    def leave(ref, out):
        leaving.append(pltpu.make_async_copy(ref, out, out_sems.at[len(leaving)]))
        leaving[-1].start()

    gain_sum = jnp.zeros((1, 768), F32)
    for kk in range(4):
        rows = pl.ds(aligned(flip(b, kk) * 256, 256), 256)
        grad = dot(grads[rows, :], w[...], 1, 1)
        values = xs[kk, 0:256, :].astype(F32)
        inverse = lax.rsqrt(jnp.mean(values * values, axis=-1, keepdims=True) + EPS)
        gain_sum += jnp.sum(grad * (values * inverse), axis=0, keepdims=True)
        if kk % 2:
            gs_o[kk // 2] = grad.astype(BF)
        else:
            (gk0_o, gk1_o)[kk // 2][...] = grad.astype(BF)
    for ref, out in ((gs_o, gs_h), (gk0_o, gk0_h), (gk1_o, gk1_h)):
        leave(ref, out)
    row_at = lax.broadcasted_iota(jnp.int32, (128, 768), 0)
    gain_rows = jnp.where(row_at == 64, gain_sum, jnp.where(row_at == 65, gain2, 0.0))
    gain_columns = gain_rows.T
    normed = n[...].T
    for j in range(5):
        cols = slice(128 * j, 128 * j + 128)
        part = dot(normed, grads[:, cols])
        if j == 4:
            part = part + gain_columns
        wide[:, cols] = part
    for xr, (ref, out) in ((1, (send_o, send_h)), (0, (keep_o, keep_h))):
        for zr in range(4):
            dp = 2 * flip(z, zr) + flip(x, xr)
            ref[zr] = wide[pl.ds(aligned(dp * 96, 96), 96), :].astype(BF)
        leave(ref, out)
    for copy in leaving:
        copy.wait()


def attend_back(saved, tabs, xs, g):
    outs = [((4, 96, 640), BF, HBM)] * 2 + [((256, 768), BF, HBM)] * 2 + [((2, 256, 768), BF, HBM)]
    return call(
        attend_back_kernel, outs, [*saved, *tabs, *xs, *g], anys=range(14), grant=60,
        scratch=[
            VMEM((4, 1024, LANES), BF), VMEM((1024, 768), BF), VMEM((768, 640), BF),
            VMEM((8, 1024), F32), VMEM((4, 256, 128), F32), VMEM((4, 8, 256), F32),
            VMEM((4, 272, 768), BF), VMEM((4, 400, 128), BF), VMEM((1024, LANES), BF), *[VMEM((1024, LANES), F32)] * 3,
            VMEM((1024, 640), BF), VMEM((768, 640), F32),
            *[VMEM(out[0], out[1]) for out in outs], pltpu.SemaphoreType.DMA((15,)), pltpu.SemaphoreType.DMA((5,)),
        ],
        flops=1000, nbytes=1000,
    )


def tail_kernel(kept, arrived, o_kept, o_arrived, t0_o, t1_o, t2_o, t3_o):
    for k, out in enumerate((t0_o, t1_o, t2_o, t3_o)):
        out[0:96, :] = (kept[k].astype(F32) + arrived[k].astype(F32)).astype(BF)
        rows = o_kept[k].astype(F32) + o_arrived[k].astype(F32)
        rest = [rows[8 * t : 8 * t + 8, 640:768] for t in range(3)] + [jnp.zeros((8, 256), F32)]
        out[96:128, :] = jnp.concatenate([rows[:, 0:640], jnp.concatenate(rest, axis=1)], axis=0).astype(BF)


def tail_blocks(kept, arrived, o_kept, o_arrived):
    outs = [((128, 640), BF)] * 4
    return call(tail_kernel, outs, [kept, arrived, o_kept, o_arrived], flops=1_000_000, nbytes=2_000_000)


def last_kernel(kept, arrived, mid, x0, gains, out):
    grad = kept[...].astype(F32) + arrived[...].astype(F32)
    values = x0[0:256, :].astype(F32)
    inverse = lax.rsqrt(jnp.mean(values * values, axis=-1, keepdims=True) + EPS)
    unit = values * inverse
    scaled = grad * gains[0:1, :]
    out[...] = (
        mid[...] + inverse * (scaled - unit * jnp.mean(scaled * unit, axis=-1, keepdims=True))
    ).astype(BF)


def swap_z(v, k):
    return lax.ppermute(v, "dp", [(i, i ^ (2 * k)) for i in range(8)])


def swap_x(v):
    return lax.ppermute(v, "dp", [(i, i ^ 1) for i in range(8)])


def swap_b(v, k):
    return lax.ppermute(v, "blk", [(i, i ^ k) for i in range(4)])


def swap_core(v):
    return swap_b(v, 1)


def swap_y(v):
    return swap_b(v, 2)


def after(value, *tokens):
    return lax.optimization_barrier((value, tokens))[0]


def stack_z(v):
    return jnp.stack([v] + [swap_z(v, k) for k in (1, 2, 3)])


def by_index(four, bits):
    one, two = bits % 2 == 1, bits // 2 == 1
    a, b, c, d = four
    a, b, c, d = jnp.where(one, b, a), jnp.where(one, a, b), jnp.where(one, d, c), jnp.where(one, c, d)
    return [jnp.where(two, c, a), jnp.where(two, d, b), jnp.where(two, a, c), jnp.where(two, b, d)]


def sum_z(v):
    terms = [v[0]] + [swap_z(v[k], k) for k in (1, 2, 3)]
    return sum(term.astype(F32) for term in terms)


def halve_z(v, far):
    first = [added(v[k], far[k]) for k in range(2)]
    return first[0].astype(F32) + swap_z(first[1], 1).astype(F32)


def added(kept, arrived):
    return (kept.astype(F32) + arrived.astype(F32)).astype(BF)


def fast_shards(tokens, segments, positions, cotangent, attn_gain, w_query, w_key, w_value, w_out,
                mlp_gain, w_gate, w_up, w_down):
    z, x, y, c, b = ids()
    first = c == 0
    x0 = tokens[0]
    ct0 = cotangent[0]

    *parts, x0 = prepare(x0, positions, w_query, w_key, w_value, attn_gain[None], mlp_gain[None], w_gate, w_up)
    do_own = jnp.concatenate([w_down, w_out], axis=0)
    do_z = [do_own] + [swap_z(do_own, k) for k in (1, 2, 3)]
    from_blk = [parts[0]] + [swap_b(parts[k], k) for k in (1, 2, 3)]

    from_blk, do_z, x0 = lax.optimization_barrier((from_blk, do_z, x0))
    qkv_own = columns(from_blk)
    qkv_z = [qkv_own] + [swap_z(qkv_own, k) for k in (1, 2, 3)]
    do_near = jnp.stack(do_z)
    do_far = swap_x(do_near)
    x2 = swap_y(x0)

    qkv_z, x0, do_far = lax.optimization_barrier((qkv_z, x0, do_far))
    qkv_a = jnp.stack(qkv_z)
    qkv_b = swap_x(qkv_a)
    x1, x3 = swap_core(x0), swap_core(x2)
    xs = (x0, x1, x2, x3)
    tabs = tables(xs)
    out_zx = jnp.stack([do_near[:, 64:], do_far[:, 64:]])
    out_y = swap_y(out_zx)
    g_own, u_own = units(xs)
    g_near = stack_z(g_own)
    u_near1 = swap_z(u_own, 1)

    qkv_b, out_y, tabs, ct0, g_near, u_own, u_near1 = lax.optimization_barrier(
        (qkv_b, out_y, tabs, ct0, g_near, u_own, u_near1))
    ct2 = swap_y(ct0)
    g_far = swap_x(g_near)
    u_near = jnp.stack([u_own, u_near1, swap_z(u_own, 2), swap_z(u_own, 3)])
    *saved, gains, a0, a1, a2, a3 = attend(xs, qkv_a, qkv_b, tabs)

    a1, a2, a3, u_near, ct2, g_far, out_zx, out_y, ct0 = lax.optimization_barrier(
        (a1, a2, a3, u_near, ct2, g_far, out_zx, out_y, ct0))
    a1, a2, a3 = swap_b(a1, 1), swap_b(a2, 2), swap_b(a3, 3)
    out_own = jnp.stack([out_zx[0], out_y[0], out_zx[1], out_y[1]])
    out_other = swap_core(out_own)
    u_far = swap_x(after(u_near, a1))

    ct1, ct3 = swap_core(after(ct0, a1)), swap_core(after(ct2, a1))
    a1, a2, a3, out_other, ct0, ct2, u_far, ct1, ct3 = lax.optimization_barrier(
        (a1, a2, a3, out_other, ct0, ct2, u_far, ct1, ct3))
    resid, n02, wo, heads = project((a0, a1, a2, a3), x0, x2, gains, out_own, out_other)
    n13 = swap_core(n02)

    n_all, ct_all, hid, dg, du, wgu, wd = hidden_and_back(
        (n02, n13), (ct0, ct1, ct2, ct3), (g_near, g_far, u_near, u_far, do_near, do_far))
    gn_own, gn_far, gn_send = normed_back(dg, du, wgu)
    gn_in = swap_core(gn_send)
    gu_keep, gu_send, d_keep, d_send = ff_grads(n_all, ct_all, hid, dg, du)
    gn_in, gu_send, d_send, hid = lax.optimization_barrier((gn_in, gu_send, d_send, hid))
    gn_there = swap_y((gn_far + gn_in[1].astype(F32)).astype(BF))
    gn_here = gn_own + gn_in[0].astype(F32)
    out_own, out_far, out_send = down(hid, wd, resid)
    out_in = swap_core(out_send)
    gu_in = swap_x(gu_send)
    gn_there, out_in, d_send = lax.optimization_barrier((gn_there, out_in, d_send))
    out_here, out_2, mid, br0, ga0, ga1, ga2, ga3 = mid_back(
        gn_here, gn_there, resid, ct0, gains, wo, (out_own, out_far, out_in))
    ga1, ga2, ga3 = swap_b(ga1, 1), swap_b(ga2, 2), swap_b(ga3, 3)
    d_in = swap_x(d_send)
    o_keep, o_send = out_grads(heads, br0)
    o_in = swap_core(o_send)
    o_2 = added(o_keep[1], o_in[1])
    gu_in = after(gu_in, ga1)
    gu_2 = added(gu_keep[2:], gu_in[2:])
    ga1, ga2, ga3, gu_2, o_2, out_2 = lax.optimization_barrier((ga1, ga2, ga3, gu_2, o_2, out_2))
    gu_far = swap_z(gu_2, 2)
    o_2in = swap_x(o_2)
    out_there = swap_y(out_2)
    qkv_keep, qkv_send, gn_keep, gn_keep2, gn_send = attend_back(saved, tabs, xs, (ga0, ga1, ga2, ga3))
    qkv_send, gn_send, d_in, o_2in = lax.optimization_barrier((qkv_send, gn_send, d_in, o_2in))
    qkv_in = swap_x(qkv_send)
    gn_in2 = swap_core(gn_send)
    d_2 = added(d_keep, d_in)
    d_far = swap_z(d_2[2:], 2)
    o_3 = [added(o_keep[0, j].astype(F32) + o_in[0, j].astype(F32), o_2in[j]) for j in range(2)]
    o_3in = swap_y(o_3[1])
    gn_here2 = added(gn_keep, gn_in2[0])
    there_in = swap_y(added(gn_keep2, gn_in2[1]))
    output = (out_here + out_there.astype(F32)).astype(BF)
    qkv_in, o_3in, gu_in, d_2 = lax.optimization_barrier((qkv_in, o_3in, gu_in, d_2))
    tail = list(tail_blocks(qkv_keep, qkv_in, o_3[0], o_3in))
    tail = [tail[0]] + [swap_z(tail[k], k) for k in (1, 2, 3)]
    gu_rows = halve_z(added(gu_keep[:2], gu_in[:2]), gu_far).astype(BF).reshape(4, 24, 1024)
    gu_order = by_index([gu_rows[j] for j in range(4)], b)
    grad_down = halve_z(d_2, d_far)
    tail, there_in, gu_order, grad_down = lax.optimization_barrier((tail, there_in, gu_order, grad_down))
    rows = sum(term.astype(F32) for term in tail)
    rows96 = rows[:96].astype(BF).reshape(4, 24, 640)
    order = by_index([rows96[j] for j in range(4)], b)
    from_heads = [order[0]] + [swap_b(order[j], j) for j in (1, 2, 3)]
    from_units = [gu_order[0]] + [swap_b(gu_order[j], j) for j in (1, 2, 3)]
    grad_out = jnp.concatenate(
        [rows[96:120], jnp.concatenate([rows[120:128, 128 * t : 128 * t + 128] for t in range(3)], axis=0)], axis=1)
    (grad_input,) = call(last_kernel, [((256, 768), BF)], [gn_here2, there_in, mid, x0, gains],
                         flops=10_000_000, nbytes=3_000_000)

    grad_query, grad_key, grad_value, grad_gate, grad_up, grad_gain1, grad_gain2 = finish(from_heads, from_units)
    return (output[None], grad_input[None], grad_gain1[0], grad_query, grad_key, grad_value, grad_out,
            grad_gain2[0], grad_gate, grad_up, grad_down)


def solution(mesh):
    fits = dict(mesh.shape) == {"dp": 8, "blk": 4}
    return jax.shard_map(
        fast_shards if fits else shards,
        mesh=mesh,
        in_specs=(
            P("dp", "blk", None),
            P("dp", "blk"),
            P("dp", "blk"),
            P("dp", "blk", None),
            P(("dp", "blk")),
            P(("dp", "blk"), None),
            P(("dp", "blk"), None),
            P(("dp", "blk"), None),
            P(("dp", "blk"), None),
            P(("dp", "blk")),
            P(("dp", "blk"), None),
            P(("dp", "blk"), None),
            P(("dp", "blk"), None),
        ),
        out_specs=(
            P("dp", "blk", None),
            P("dp", "blk", None),
            P(("dp", "blk")),
            P(("dp", "blk"), None),
            P(("dp", "blk"), None),
            P(("dp", "blk"), None),
            P(("dp", "blk"), None),
            P(("dp", "blk")),
            P(("dp", "blk"), None),
            P(("dp", "blk"), None),
            P(("dp", "blk"), None),
        ),
        check_vma=False,
    )
```
